32 devices in a mesh: groups: 2 (over y), row: 4 (over z), col: 2 (over x), sub: 2 (over core).
Axes of the slice: x: 2, y: 2, z: 4, core: 2. Of those that a mesh axis runs over, the one named last changes fastest.
Arguments:
- density: bfloat16 [4096, 2048], P(('groups', 'row'), ('col', 'sub')), parts along dimension 0, as said below
- margin: bfloat16 [4096, 2048], P(('groups', 'row'), ('col', 'sub')), parts along dimension 0, as said below
- pattern_d: int32 [32, 16], P(('groups', 'row'), ('col', 'sub')), parts along dimension 0, may hold values from 0 to 1, as said below
- pattern_s: int32 [32, 16], P(('groups', 'row'), ('col', 'sub')), parts along dimension 0, may hold values from 0 to 1, as said below
- dipole: bfloat16 [3, 4096], P(None, ('groups', 'col', 'sub')), parts along dimension 1, may hold values from -0.125 to 0.125
- owner: int32 [3, 32768], P(None, ('groups', 'row', 'col', 'sub')), parts along dimension 1, may hold values from 0 to 2047
- centres: float32 [3, 32768], P(None, ('groups', 'row', 'col', 'sub')), parts along dimension 1, may hold values from 0 to 3
- angles: float32 [3, 32768], P(None, ('groups', 'row', 'col', 'sub')), parts along dimension 1, may hold values from -3.140625 to 3.140625
- velocity: float32 [3, 32768], P(None, ('groups', 'row', 'col', 'sub')), parts along dimension 1, may hold values from -6 to 6
- angmom: float32 [3, 32768], P(None, ('groups', 'row', 'col', 'sub')), parts along dimension 1, may hold values from -6 to 6
- halo_list: int32 [2, 8192], P(None, ('groups', 'row', 'col', 'sub')), parts along dimension 1, may hold values from 0 to 1023
- neighbours: int32 [32, 32768], P(None, ('groups', 'row', 'col', 'sub')), parts along dimension 1, may hold values from 0 to 1535
Outputs:
- qm_out: bfloat16 [4096, 2048], P(('groups', 'row'), ('col', 'sub')), parts along dimension 0
- centres_new: float32 [3, 32768], P(None, ('groups', 'row', 'col', 'sub')), parts along dimension 1
- velocity_new: float32 [3, 32768], P(None, ('groups', 'row', 'col', 'sub')), parts along dimension 1
- angmom_new: float32 [3, 32768], P(None, ('groups', 'row', 'col', 'sub')), parts along dimension 1
- orient_new: float32 [4, 32768], P(None, ('groups', 'row', 'col', 'sub')), parts along dimension 1
The draws below stay inside these ranges and needn't reach their ends.
There are 2 independent parts, one for each index of `groups`. The reference program is written for one: setup_inputs(seed, part) draws one part's arguments, and reference() takes and returns one part's arrays. A program takes and returns all parts, laid end to end along the dimension named above; each array names one. Nothing has to cross between parts.
Inputs may be any that keep to these rules, and one draw needn't show every extreme that they name: density is symmetric. margin is symmetric. `pattern_d`: symmetric, ones on the diagonal. `pattern_s`: every block row holds exactly 1 ones in each aligned run of 4 block columns.
All inputs are finite; a program needn't handle non-finite values.
Results may differ from the reference program's by a relative error of at most 0.0075.
Values may be sent and summed in bfloat16 or wider, within the bound.
No kernel may reach another device: no remote copies, remote signals or barrier semaphores. Data moves between devices by JAX's collectives and lax.ppermute only.
A program may use at most 128 MiB of HBM per device.

```python
import math
import jax
import jax.numpy as jnp
import numpy as np
from jax import lax

BLOCK = 128
ROW_CAP = 1
NB = 16
CW = 4
ORDER = 2048
WATERS = 1024
NEIGH = 32
HALO_DEV = 256
NWAT = 16384
HALO = 4096
N_ROW = 4
N_COL = 2
N_SUB = 2


def symmetric_normal(key, spread):
    base_draw = jnp.clip(jax.random.normal(key, (ORDER, ORDER), jnp.float32), -4.0, 4.0)
    return (base_draw + base_draw.T) * (0.5 * spread)


def block_distance(count):
    row_ids = jnp.arange(count, dtype=jnp.int32)
    return jnp.abs(row_ids[:, None] - row_ids[None, :])


def draw_density(key, part):
    return symmetric_normal(jax.random.fold_in(key, 101), 1.0).astype(jnp.bfloat16)


def draw_margin(key, part):
    return symmetric_normal(jax.random.fold_in(key, 202), 0.0125).astype(jnp.bfloat16)


def draw_pattern_d(key, part):
    coin_flips = (jax.random.randint(jax.random.fold_in(key, 303), (NB, NB), 0, 8) == 0).astype(jnp.int32)
    scattered = jnp.maximum(coin_flips, coin_flips.T)
    banded = (block_distance(NB) <= 1).astype(jnp.int32)
    return jnp.maximum(scattered, banded).astype(jnp.int32)


def draw_pattern_s(key, part):
    column_ids = jnp.arange(NB, dtype=jnp.int32)
    scores = jax.random.randint(jax.random.fold_in(key, 404), (NB, NB), 0, 65536) * NB + column_ids[None, :]
    distance = block_distance(NB)
    scores = scores + jnp.where(distance == 0, 1 << 28, 0) + jnp.where(distance == 1, 1 << 27, 0)
    runs = scores.reshape(NB, NB // CW, CW)
    higher = jnp.sum((runs[:, :, None, :] > runs[:, :, :, None]).astype(jnp.int32), axis=3)
    chosen = (higher < ROW_CAP).astype(jnp.int32)
    return chosen.reshape(NB, NB).astype(jnp.int32)


def touch_ends(result, key, low, top_value):
    longest = result.shape.index(max(result.shape))
    spots = []
    for shift in (0, 1):
        where = [jax.random.randint(jax.random.fold_in(key, axis), (), 0, length) for axis, length in enumerate(result.shape)]
        where[longest] = (where[longest] + shift) % result.shape[longest]
        spots.append(tuple(where))
    return result.at[spots[0]].set(low).at[spots[1]].set(top_value)


def levels(own_key, dims, cuts, smallest, largest):
    level = 1.0
    for axis_at, shards_of in cuts:
        steps = jax.random.uniform(jax.random.fold_in(jax.random.fold_in(own_key, 6), axis_at), (shards_of,), jnp.float32, smallest / len(cuts), largest / len(cuts))
        level = level * jnp.repeat(jnp.exp(steps), dims[axis_at] // shards_of).reshape((-1,) + (1,) * (len(dims) - 1 - axis_at))
    return level


def cumulative_ranks(count, slope):
    weights = [(1 << 20) // math.isqrt(standing ** slope) + 1 for standing in range(1, count + 1)]
    scale = 1 + sum(weights) // (1 << 30)
    return np.cumsum(np.array([max(1, weight // scale) for weight in weights]))


def ranked(stream_key, dims, count, slope):
    listing = cumulative_ranks(count, slope)
    lot = jax.random.randint(jax.random.fold_in(stream_key, 1), dims, 0, int(listing[count - 1]))
    standing = jnp.searchsorted(jnp.asarray(listing, jnp.int32), lot, side="right")
    return jax.random.permutation(jax.random.fold_in(stream_key, 2), count)[standing].astype(jnp.int32)


def bell_draw(stream_key, dims, scale, most, cuts=(), held_as=jnp.bfloat16):
    drawn = jax.random.normal(stream_key, dims, jnp.float32) * scale
    if len(cuts) > 0:
        drawn = levels(stream_key, dims, cuts, -0.22, 0.18) * drawn
    return jnp.clip(drawn, min=-most, max=most).astype(held_as)


def setup_inputs(seed: int = 0, part: int = 0) -> dict:
    streams_of = jax.random.split(jax.random.key(seed), 13)
    part_keys = jax.random.split(jax.random.fold_in(streams_of[12], part), 13)
    return {
        "density": draw_density(jax.random.fold_in(jax.random.fold_in(streams_of[12], part), 71), part),
        "margin": draw_margin(jax.random.fold_in(jax.random.fold_in(streams_of[12], part), 71), part),
        "pattern_d": draw_pattern_d(jax.random.fold_in(jax.random.fold_in(streams_of[12], part), 71), part),
        "pattern_s": draw_pattern_s(jax.random.fold_in(jax.random.fold_in(streams_of[12], part), 71), part),
        "dipole": bell_draw(part_keys[4], (3, ORDER), ORDER ** -0.5, 0.125, ((1, 4),)),
        "owner": touch_ends(ranked(part_keys[5], (3, NWAT), ORDER, 2), jax.random.fold_in(part_keys[5], 3), 0, ORDER - 1).astype(jnp.int32),
        "centres": jnp.clip(3.0 * jax.random.uniform(part_keys[6], (3, NWAT), jnp.float32) ** levels(part_keys[6], (3, NWAT), ((1, 16),), -0.2, 0.2), 0.0, 3.0),
        "angles": jnp.clip(jax.random.uniform(part_keys[7], (3, NWAT), jnp.float32, -3.140625, 3.140625), -3.140625, 3.140625),
        "velocity": bell_draw(part_keys[8], (3, NWAT), 1.0, 6.0, ((1, 16),), jnp.float32),
        "angmom": bell_draw(part_keys[9], (3, NWAT), 1.0, 6.0, ((1, 16),), jnp.float32),
        "halo_list": touch_ends(jax.random.randint(part_keys[10], (2, HALO), 0, WATERS), jax.random.fold_in(part_keys[10], 1), 0, WATERS - 1).astype(jnp.int32),
        "neighbours": touch_ends(jax.random.randint(part_keys[11], (NEIGH, NWAT), 0, WATERS + 2 * HALO_DEV), jax.random.fold_in(part_keys[11], 1), 0, (WATERS + 2 * HALO_DEV) - 1).astype(jnp.int32),
    }


CHARGE = (-0.834, 0.417, 0.417)
OFFSET = ((0.0, 0.0, -0.12), (0.76, 0.0, 0.47), (-0.76, 0.0, 0.47))
COUPLE = 0.1
STEP_DT = 0.5
WATER_MASS = 1.0
INERTIA = 0.5
SOFTEN = 1.0

def expand(pattern, width):
    return jnp.repeat(jnp.repeat(pattern, width, axis=0), width, axis=1)

def quaternion(angles):
    half_angle = 0.5 * angles
    cos_r, cos_p, cos_y = (jnp.cos(half_angle[0]), jnp.cos(half_angle[1]), jnp.cos(half_angle[2]))
    sin_r, sin_p, sin_y = (jnp.sin(half_angle[0]), jnp.sin(half_angle[1]), jnp.sin(half_angle[2]))
    comp_w = cos_r * cos_p * cos_y + sin_r * sin_p * sin_y
    comp_x = sin_r * cos_p * cos_y - cos_r * sin_p * sin_y
    comp_y = cos_r * sin_p * cos_y + sin_r * cos_p * sin_y
    comp_z = cos_r * cos_p * sin_y - sin_r * sin_p * cos_y
    return jnp.stack([comp_w, comp_x, comp_y, comp_z])

def rotation(quat):
    comp_w, comp_x, comp_y, comp_z = (quat[0], quat[1], quat[2], quat[3])
    return ((1.0 - 2.0 * (comp_y * comp_y + comp_z * comp_z), 2.0 * (comp_x * comp_y - comp_w * comp_z), 2.0 * (comp_x * comp_z + comp_w * comp_y)), (2.0 * (comp_x * comp_y + comp_w * comp_z), 1.0 - 2.0 * (comp_x * comp_x + comp_z * comp_z), 2.0 * (comp_y * comp_z - comp_w * comp_x)), (2.0 * (comp_x * comp_z - comp_w * comp_y), 2.0 * (comp_y * comp_z + comp_w * comp_x), 1.0 - 2.0 * (comp_x * comp_x + comp_y * comp_y)))

def site_positions(centres, quat):
    matrix = rotation(quat)
    layers = []
    for source in range(3):
        for compo in range(3):
            layers.append(centres[compo] + matrix[compo][0] * OFFSET[source][0] + matrix[compo][1] * OFFSET[source][1] + matrix[compo][2] * OFFSET[source][2])
    return jnp.stack(layers)

def pair_forces(own_sites, partner_sites):
    pieces = []
    for source in range(3):
        own_part = own_sites[3 * source:3 * source + 3][:, None]
        total = jnp.zeros(own_sites.shape[1:], jnp.float32)[None] * jnp.zeros((3,) + (1,) * (own_sites.ndim - 1), jnp.float32)
        for target in range(3):
            offset_vec = own_part - partner_sites[3 * target:3 * target + 3]
            dist_sq = lax.optimization_barrier(jnp.sum(offset_vec * offset_vec, axis=0)) + SOFTEN
            weight = CHARGE[source] * CHARGE[target] * dist_sq ** (-1.5)
            total = total + lax.optimization_barrier(jnp.sum(offset_vec * weight[None], axis=1))
        pieces.append(total)
    return jnp.concatenate(pieces, axis=0)

def advance(centres, quat, velocity, angmom, sites, forces):
    total = forces[0:3] + forces[3:6] + forces[6:9]
    torque = jnp.zeros_like(centres)
    for source in range(3):
        lever = sites[3 * source:3 * source + 3] - centres
        torque = torque + jnp.cross(lever, forces[3 * source:3 * source + 3], axis=0)
    velocity_new = velocity + STEP_DT * total / WATER_MASS
    centres_new = centres + STEP_DT * velocity_new
    angmom_new = angmom + STEP_DT * torque
    omega = angmom_new / INERTIA
    vector = quat[1:4]
    delta_w = -lax.optimization_barrier(jnp.sum(omega * vector, axis=0))
    delta_vec = quat[0][None] * omega + jnp.cross(omega, vector, axis=0)
    moved = quat + 0.5 * STEP_DT * jnp.concatenate([delta_w[None], delta_vec], axis=0)
    length = jnp.sqrt(lax.optimization_barrier(jnp.sum(moved * moved, axis=0)))
    return (centres_new, velocity_new, angmom_new, moved / length[None])

def reference(density, margin, pattern_d, pattern_s, dipole, owner, centres, angles, velocity, angmom, halo_list, neighbours):
    dens_mask = density * expand(pattern_d, BLOCK).astype(jnp.bfloat16)
    over_mask = margin * expand(pattern_s, BLOCK).astype(jnp.bfloat16)
    product = jnp.dot(dens_mask, over_mask, preferred_element_type=jnp.float32)
    site_charge = jnp.broadcast_to(jnp.array(CHARGE, jnp.float32)[:, None], owner.shape)
    potential = jax.ops.segment_sum(site_charge.reshape(-1), owner.reshape(-1), num_segments=ORDER)
    qm_out = (product + COUPLE * (potential[:, None] + potential[None, :]) * dens_mask.astype(jnp.float32)).astype(jnp.bfloat16)
    qm_field = jnp.dot(dipole, qm_out.T, preferred_element_type=jnp.float32)
    quat = quaternion(angles)
    sites = site_positions(centres, quat)
    groups_cs = N_COL * N_SUB
    grid = sites.reshape(9, N_ROW, groups_cs, WATERS)
    halo_grid = halo_list.reshape(2, N_ROW, groups_cs, HALO_DEV)
    send_up = jnp.take_along_axis(grid, jnp.broadcast_to(halo_grid[0][None], (9, N_ROW, groups_cs, HALO_DEV)), axis=3)
    send_down = jnp.take_along_axis(grid, jnp.broadcast_to(halo_grid[1][None], (9, N_ROW, groups_cs, HALO_DEV)), axis=3)
    table = jnp.concatenate([grid, jnp.roll(send_up, 1, axis=1), jnp.roll(send_down, -1, axis=1)], axis=3)
    width = WATERS + 2 * HALO_DEV
    slots = neighbours.reshape(NEIGH, N_ROW, groups_cs, WATERS)
    partner = jnp.take_along_axis(jnp.broadcast_to(table[:, None], (9, NEIGH, N_ROW, groups_cs, width)), jnp.broadcast_to(slots[None], (9, NEIGH, N_ROW, groups_cs, WATERS)), axis=4)
    partner = partner.reshape(9, NEIGH, NWAT)
    forces = pair_forces(sites, partner)
    field_parts = []
    for source in range(3):
        field_parts.append(forces[3 * source:3 * source + 3] + CHARGE[source] * jnp.take(qm_field, owner[source], axis=1))
    forces = jnp.concatenate(field_parts, axis=0)
    centres_new, velocity_new, angmom_new, orient_new = advance(centres, quat, velocity, angmom, sites, forces)
    return (qm_out, centres_new, velocity_new, angmom_new, orient_new)
```

```python
import functools

import jax
import jax.numpy as jnp
from jax import lax
from jax.experimental import pallas as pl
from jax.experimental.pallas import tpu as pltpu
from jax.sharding import PartitionSpec as P

BLOCK = 128
LANES = 128

CHARGE = (-0.834, 0.417, 0.417)
UNIT = 0.417
MULTIPLE = (-2.0, 1.0, 1.0)
OFFSET = ((0.0, 0.0, -0.12), (0.76, 0.0, 0.47), (-0.76, 0.0, 0.47))
COUPLE = 0.1
STEP_DT = 0.5
WATER_MASS = 1.0
INERTIA = 0.5
SOFTEN = 1.0

F32 = jnp.float32
BF16 = jnp.bfloat16

SIN_TERMS = (-1 / 6, 1 / 120, -1 / 5040, 1 / 362880, -1 / 39916800, 1 / 6227020800)
COS_TERMS = (-1 / 2, 1 / 24, -1 / 720, 1 / 40320, -1 / 3628800, 1 / 479001600, -1 / 87178291200)


def at(tile):
    return slice(tile * LANES, (tile + 1) * LANES)


def pick(table, index):
    return jnp.take_along_axis(table, index, axis=1, mode="promise_in_bounds")


def contract(left, right, dims):
    return lax.dot_general(left, right, (dims, ((), ())), preferred_element_type=F32)


def series(square, terms):
    total = jnp.full_like(square, terms[-1])
    for term in terms[-2::-1]:
        total = total * square + term
    return total * square + 1.0


def open_kernel(pat_d, pat_s, marg, dip, owner, small, message, expanded):
    rows_b, cols_b = pat_d.shape
    hist_rows = message.shape[0] - 8 * max(rows_b, cols_b) - rows_b * cols_b
    message[...] = jnp.zeros(message.shape, F32)
    pattern_at = hist_rows + 8 * max(rows_b, cols_b)
    for row in range(rows_b):
        chosen = jnp.int32(0)
        for col in range(cols_b):
            chosen = chosen + col * pat_s[row, col]
            line = row * cols_b + col
            expanded[line : line + 1, :] = jnp.full((1, LANES), pat_s[row, col].astype(F32))
            message[pattern_at + line : pattern_at + line + 1, :] = jnp.full((1, LANES), pat_d[row, col].astype(F32))
        span = pl.ds(pl.multiple_of(chosen * BLOCK, BLOCK), BLOCK)
        block = marg[row * BLOCK : (row + 1) * BLOCK, span]
        small[row * BLOCK : (row + 1) * BLOCK, :] = block
        start = hist_rows + 8 * row
        message[start : start + 3, :] = contract(dip[:, span], block, ((1,), (1,)))
    for col in range(cols_b):
        start = hist_rows + 8 * col + 3
        message[start : start + 3, :] = dip[:, at(col)].astype(F32)
    waters = owner.shape[1]
    count = jnp.zeros((hist_rows, LANES), F32)
    for source in range(3):
        line = owner[source : source + 1, :]
        high = lax.broadcasted_iota(jnp.int32, (hist_rows, waters), 0) == (line >> 7)
        low = lax.broadcasted_iota(jnp.int32, (LANES, waters), 0) == (line & 127)
        count = count + contract(
            jnp.where(high, MULTIPLE[source], 0.0).astype(BF16),
            jnp.where(low, 1.0, 0.0).astype(BF16),
            ((1,), (1,)),
        )
    message[0:hist_rows, :] = count


def gathered_kernel(ways, hist_rows, *refs):
    messages, expanded, out = refs[:ways], refs[ways], refs[ways + 1]
    total = messages[0][0:hist_rows, :]
    for other in messages[1:]:
        total = total + other[0:hist_rows, :]
    out[0:hist_rows, :] = total
    out[hist_rows:, :] = expanded[...]


def project_kernel(ways, rows_n, hist_rows, where, pat_d, dens, *refs):
    firsts, seconds = refs[:ways], refs[ways : ways + rows_n]
    pot, out, dips, lines, masked = refs[ways + rows_n :]
    rows_b, cols_b = pat_d.shape
    here_row, here_col = where[0], where[1]
    total = seconds[0][0:hist_rows, :]
    for other in seconds[1:]:
        total = total + other[0:hist_rows, :]
    pot[...] = UNIT * total
    depth = 8 * max(rows_b, cols_b)
    for step in range(ways):
        dips[here_col ^ step] = firsts[step][hist_rows : hist_rows + depth, :]
    for row in range(rows_b):
        place = here_row * rows_b + row
        device = place // cols_b
        tile = dips[device, pl.ds(pl.multiple_of(8 * (place % cols_b), 8), 8), :]
        summed = firsts[0][hist_rows + 8 * row : hist_rows + 8 * row + 3, :]
        for other in firsts[1:]:
            summed = summed + other[hist_rows + 8 * row : hist_rows + 8 * row + 3, :]
        dip = tile[3:6, :]
        lines[0:3, at(row)] = summed + COUPLE * pot[pl.ds(place, 1), :] * dip
        lines[3:6, at(row)] = dip
        lines[6:8, at(row)] = jnp.zeros((2, LANES), F32)
        for col in range(cols_b):
            block = dens[row * BLOCK : (row + 1) * BLOCK, at(col)]
            masked[row * BLOCK : (row + 1) * BLOCK, at(col)] = jnp.where(
                pat_d[row, col] != 0, block, jnp.zeros_like(block)
            )
    whole = lines[...]
    first = whole.astype(BF16)
    second = (whole - first.astype(F32)).astype(BF16)
    out[...] = contract(first, masked[...], ((1,), (0,))) + contract(second, masked[...], ((1,), (0,)))


def field_kernel(rows_n, where, pot, *refs):
    parts, out = refs[:rows_n], refs[rows_n]
    cols_b = out.shape[1] // BLOCK
    total = parts[0][...]
    for other in parts[1:]:
        total = total + other[...]
    out[...] = jnp.zeros(out.shape, F32)
    for col in range(cols_b):
        line = pot[pl.ds(where[1] * cols_b + col, 1), :]
        out[0:3, at(col)] = total[0:3, at(col)] + COUPLE * line * total[3:6, at(col)]


def sites_kernel(centres, angles, halo, sites, quat, up, down):
    half_angle = 0.5 * angles[...]
    square = half_angle * half_angle
    sine = half_angle * series(square, SIN_TERMS)
    cosine = series(square, COS_TERMS)
    sin_r, sin_p, sin_y = sine[0:1], sine[1:2], sine[2:3]
    cos_r, cos_p, cos_y = cosine[0:1], cosine[1:2], cosine[2:3]
    comp_w = cos_r * cos_p * cos_y + sin_r * sin_p * sin_y
    comp_x = sin_r * cos_p * cos_y - cos_r * sin_p * sin_y
    comp_y = cos_r * sin_p * cos_y + sin_r * cos_p * sin_y
    comp_z = cos_r * cos_p * sin_y - sin_r * sin_p * cos_y
    for place, comp in enumerate((comp_w, comp_x, comp_y, comp_z)):
        quat[place : place + 1, :] = comp
    first = (
        1.0 - 2.0 * (comp_y * comp_y + comp_z * comp_z),
        2.0 * (comp_x * comp_y + comp_w * comp_z),
        2.0 * (comp_x * comp_z - comp_w * comp_y),
    )
    third = (
        2.0 * (comp_x * comp_z + comp_w * comp_y),
        2.0 * (comp_y * comp_z - comp_w * comp_x),
        1.0 - 2.0 * (comp_x * comp_x + comp_y * comp_y),
    )
    sites[...] = jnp.zeros(sites.shape, F32)
    for source in range(3):
        for compo in range(3):
            place = 3 * source + compo
            position = centres[compo : compo + 1, :] + third[compo] * OFFSET[source][2]
            if OFFSET[source][0] != 0.0:
                position = position + first[compo] * OFFSET[source][0]
            sites[place : place + 1, :] = position
    waters, listed = centres.shape[1], halo.shape[1]
    for which, out in enumerate((up, down)):
        for tile in range(listed // LANES):
            index = jnp.broadcast_to(halo[which : which + 1, at(tile)], (8, LANES))
            low, high = index & 127, index >> 7
            for part in range(2):
                found = jnp.zeros((8, LANES), F32)
                for source in range(waters // LANES):
                    value = pick(sites[8 * part : 8 * part + 8, at(source)], low)
                    found = jnp.where(high == source, value, found)
                out[8 * part : 8 * part + 8, at(tile)] = found


def pair_kernel(sites, below, above, neighbours, force, table):
    waters, listed, slots = sites.shape[1], below.shape[1], neighbours.shape[0]
    own_tiles, halo_tiles = waters // LANES, listed // LANES
    tiles = own_tiles + 2 * halo_tiles
    for word in range(9):
        for tile in range(tiles):
            if tile < own_tiles:
                line = sites[word : word + 1, at(tile)]
            elif tile < own_tiles + halo_tiles:
                line = below[word : word + 1, at(tile - own_tiles)]
            else:
                line = above[word : word + 1, at(tile - own_tiles - halo_tiles)]
            table[word, tile] = jnp.broadcast_to(line, (8, LANES))

    def one_tile(tile, carry):
        span = pl.ds(pl.multiple_of(tile * LANES, LANES), LANES)
        near = [jnp.zeros((8, LANES), F32) for _ in range(9)]
        far = [jnp.zeros((8, LANES), F32) for _ in range(9)]
        for pair in range(slots // 16):
            index = [neighbours[16 * pair + 8 * part : 16 * pair + 8 * part + 8, span] for part in range(2)]
            low = [value & 127 for value in index]
            high = [value >> 7 for value in index]
            found = [[None, None] for _ in range(9)]
            for source in range(tiles):
                here = [value == source for value in high]
                for word in range(9):
                    line = table[word, source]
                    for part in range(2):
                        value = pick(line, low[part])
                        found[word][part] = (
                            value if source == 0 else jnp.where(here[part], value, found[word][part])
                        )
            for part in range(2):
                for source in range(3):
                    own = [table[3 * source + compo, tile] for compo in range(3)]
                    for target in range(3):
                        gap = [own[compo] - found[3 * target + compo][part] for compo in range(3)]
                        root = lax.rsqrt(gap[0] * gap[0] + gap[1] * gap[1] + gap[2] * gap[2] + SOFTEN)
                        weight = root * root * root
                        sums = near if target == 0 else far
                        for compo in range(3):
                            sums[3 * source + compo] = sums[3 * source + compo] + gap[compo] * weight
        for place in range(9):
            factor = CHARGE[place // 3] * UNIT
            total = factor * (far[place] - 2.0 * near[place])
            force[place : place + 1, span] = jnp.sum(total, axis=0, keepdims=True)
        return carry

    lax.fori_loop(0, own_tiles, one_tile, 0)


def advance_kernel(ways, where, owner, sites, quat, pair, centres, velocity, angmom, *refs):
    fields = refs[:ways]
    centres_new, velocity_new, angmom_new, orient_new, force = refs[ways:]
    waters = owner.shape[1]
    cols_b = fields[0].shape[1] // BLOCK
    for tile in range(waters // LANES):
        for source in range(3):
            index = jnp.broadcast_to(owner[source : source + 1, at(tile)], (8, LANES))
            low, high = index & 127, index >> 7
            found = jnp.zeros((8, LANES), F32)
            for step in range(ways):
                base = (where[1] ^ step) * cols_b
                for col in range(cols_b):
                    value = pick(fields[step][:, at(col)], low)
                    found = jnp.where(high == base + col, value, found)
            lines = slice(3 * source, 3 * source + 3)
            force[lines, at(tile)] = pair[lines, at(tile)] + CHARGE[source] * found[0:3]

    def cross(left, right):
        return [
            left[1] * right[2] - left[2] * right[1],
            left[2] * right[0] - left[0] * right[2],
            left[0] * right[1] - left[1] * right[0],
        ]

    def split(array):
        return [array[compo : compo + 1, :] for compo in range(3)]

    total = force[0:3, :] + force[3:6, :] + force[6:9, :]
    torque = None
    centre = split(centres)
    for source in range(3):
        lever = [sites[3 * source + compo : 3 * source + compo + 1, :] - centre[compo] for compo in range(3)]
        push = [force[3 * source + compo : 3 * source + compo + 1, :] for compo in range(3)]
        turn = cross(lever, push)
        torque = turn if torque is None else [old + new for old, new in zip(torque, turn)]
    moving = velocity[...] + STEP_DT * total / WATER_MASS
    velocity_new[...] = moving
    centres_new[...] = centres[...] + STEP_DT * moving
    spin = [angmom[compo : compo + 1, :] + STEP_DT * torque[compo] for compo in range(3)]
    for compo in range(3):
        angmom_new[compo : compo + 1, :] = spin[compo]
    omega = [value * (1.0 / INERTIA) for value in spin]
    scalar = quat[0:1, :]
    vector = [quat[compo + 1 : compo + 2, :] for compo in range(3)]
    delta = [-(omega[0] * vector[0] + omega[1] * vector[1] + omega[2] * vector[2])]
    turned = cross(omega, vector)
    delta = delta + [scalar * omega[compo] + turned[compo] for compo in range(3)]
    moved = [old + 0.5 * STEP_DT * new for old, new in zip([scalar] + vector, delta)]
    length = jnp.sqrt(moved[0] * moved[0] + moved[1] * moved[1] + moved[2] * moved[2] + moved[3] * moved[3])
    for place in range(4):
        orient_new[place : place + 1, :] = moved[place] / length


def product_kernel(ways, rows_n, hist_rows, where, pot, *refs):
    firsts, seconds = refs[:ways], refs[ways : ways + rows_n]
    refs = refs[ways + rows_n :]
    dens, small = refs[:ways], refs[ways : ways + rows_n]
    out, panel, masked, total = refs[ways + rows_n :]
    rows, cols = out.shape
    rows_b, cols_b = rows // BLOCK, cols // BLOCK
    here_row, here_col = where[0], where[1]
    for step in range(rows_n):
        base = (here_row ^ step) * rows
        for row in range(rows_b):
            block = small[step][row * BLOCK : (row + 1) * BLOCK, :]
            for col in range(cols_b):
                line = hist_rows + row * cols_b + col
                keep = seconds[step][line : line + 1, :].astype(BF16)
                start = pl.multiple_of(base + row * BLOCK, BLOCK)
                panel[pl.ds(start, BLOCK), at(col)] = block * keep
    pattern_at = hist_rows + 8 * max(rows_b, cols_b)
    lane = lax.broadcasted_iota(jnp.int32, (1, LANES), 1)
    ones = jnp.ones((1, LANES), F32)

    def three(value):
        first = value.astype(BF16).astype(F32)
        second = (value - first).astype(BF16).astype(F32)
        return [first, second, value - first - second]

    row_lines = [three(pot[pl.ds(here_row * rows_b + row, 1), :]) for row in range(rows_b)]
    col_lines = [three(pot[pl.ds(here_col * cols_b + col, 1), :]) for col in range(cols_b)]
    del lane
    pad = jnp.zeros((2, LANES), F32)
    left = [jnp.concatenate(value + [ones, ones, ones, pad], axis=0).astype(BF16) for value in row_lines]
    right = [jnp.concatenate([ones, ones, ones] + value + [pad], axis=0).astype(BF16) for value in col_lines]
    for step in range(ways):
        for row in range(rows_b):
            for col in range(cols_b):
                line = pattern_at + row * cols_b + col
                keep = firsts[step][line : line + 1, :].astype(BF16)
                spot = (slice(row * BLOCK, (row + 1) * BLOCK), at(col))
                block = dens[step][spot] * keep
                masked[spot] = block
                if step == 0:
                    sums = contract(left[row], right[col], ((0,), (0,)))
                    total[spot] = COUPLE * sums * block.astype(F32)
        start = pl.multiple_of((here_col ^ step) * cols, BLOCK)
        total[...] += contract(masked[...], panel[pl.ds(start, cols), :], ((1,), (0,)))
    out[...] = total[...].astype(BF16)


VMEM = pl.BlockSpec(memory_space=pltpu.VMEM)
SMEM = pl.BlockSpec(memory_space=pltpu.SMEM)


def call(kernel, name, outs, operands, scalars=0, scratch=(), cost=(0, 0)):
    return pl.pallas_call(
        kernel,
        out_shape=[jax.ShapeDtypeStruct(shape, dtype) for shape, dtype in outs],
        in_specs=[SMEM] * scalars + [VMEM] * (len(operands) - scalars),
        out_specs=[VMEM] * len(outs),
        scratch_shapes=list(scratch),
        compiler_params=pltpu.CompilerParams(vmem_limit_bytes=48 << 20),
        cost_estimate=pl.CostEstimate(flops=cost[0], bytes_accessed=cost[1], transcendentals=0),
        name=name,
    )(*operands)


def shards(
    density,
    margin,
    pattern_d,
    pattern_s,
    dipole,
    owner,
    centres,
    angles,
    velocity,
    angmom,
    halo_list,
    neighbours,
):
    rows, cols = density.shape
    rows_b, cols_b = pattern_d.shape
    rows_n = lax.axis_size("row")
    sub_n = lax.axis_size("sub")
    across = ("col", "sub")
    ways = lax.axis_size("col") * sub_n
    hist_rows = rows * rows_n // LANES
    waters, listed = centres.shape[1], halo_list.shape[1]
    where = jnp.stack([lax.axis_index("row"), lax.axis_index(across)]).astype(jnp.int32)

    def swap(value, axis, count, step):
        return lax.ppermute(value, axis, [(i, i ^ step) for i in range(count)])

    def ring(value, by):
        return lax.ppermute(value, "row", [(i, (i + by) % rows_n) for i in range(rows_n)])

    dens_all = [density]
    for step in range(1, ways):
        if step % 2 == 1 and step > 1:
            dens_all.append(swap(dens_all[step - 1], "sub", sub_n, 1))
        else:
            dens_all.append(swap(density, across, ways, step))

    depth = 8 * max(rows_b, cols_b)
    small, first, expanded = call(
        open_kernel,
        "margin_blocks_and_counts",
        [
            ((rows, BLOCK), BF16),
            ((hist_rows + depth + rows_b * cols_b, LANES), F32),
            ((rows_b * cols_b, LANES), F32),
        ],
        [pattern_d, pattern_s, margin, dipole, owner],
        scalars=2,
        cost=(10**8, 10**6),
    )
    firsts = [first] + [swap(first, across, ways, step) for step in range(1, ways)]
    small_all = [small] + [swap(small, "row", rows_n, step) for step in range(1, rows_n)]

    sites, quat, up, down = call(
        sites_kernel,
        "sites",
        [((16, waters), F32), ((4, waters), F32), ((16, listed), F32), ((16, listed), F32)],
        [centres, angles, halo_list],
        cost=(10**7, 10**6),
    )
    below, above = ring(up, 1), ring(down, -1)

    (second,) = call(
        functools.partial(gathered_kernel, ways, hist_rows),
        "row_counts",
        [((hist_rows + rows_b * cols_b, LANES), F32)],
        firsts + [expanded],
    )
    seconds = [second] + [swap(second, "row", rows_n, step) for step in range(1, rows_n)]
    pot, part = call(
        functools.partial(project_kernel, ways, rows_n, hist_rows),
        "field_parts",
        [((hist_rows, LANES), F32), ((8, cols), F32)],
        [where, pattern_d, density] + firsts + seconds,
        scalars=2,
        scratch=[pltpu.VMEM((ways, depth, LANES), F32), pltpu.VMEM((8, rows), F32), pltpu.VMEM((rows, cols), BF16)],
        cost=(10**7, 10**6),
    )
    parts = [part] + [swap(part, "row", rows_n, step) for step in range(1, rows_n)]
    (field,) = call(
        functools.partial(field_kernel, rows_n), "field", [((8, cols), F32)], [where, pot] + parts, scalars=1
    )
    fields = [field] + [swap(field, across, ways, step) for step in range(1, ways)]

    tiles = (waters + 2 * listed) // LANES
    (pair,) = call(
        pair_kernel,
        "pair_forces",
        [((9, waters), F32)],
        [sites, below, above, neighbours],
        scratch=[pltpu.VMEM((9, tiles, 8, LANES), F32)],
        cost=(10**9, 10**7),
    )
    (qm_out,) = call(
        functools.partial(product_kernel, ways, rows_n, hist_rows),
        "product",
        [((rows, cols), BF16)],
        [where, pot] + firsts + seconds + dens_all + small_all,
        scalars=1,
        scratch=[
            pltpu.VMEM((rows * rows_n, cols), BF16),
            pltpu.VMEM((rows, cols), BF16),
            pltpu.VMEM((rows, cols), F32),
        ],
        cost=(10**9, 10**7),
    )
    centres_new, velocity_new, angmom_new, orient_new = call(
        functools.partial(advance_kernel, ways),
        "advance",
        [((3, waters), F32), ((3, waters), F32), ((3, waters), F32), ((4, waters), F32)],
        [where, owner, sites, quat, pair, centres, velocity, angmom] + fields,
        scalars=1,
        scratch=[pltpu.VMEM((16, waters), F32)],
        cost=(10**7, 10**6),
    )
    return (qm_out, centres_new, velocity_new, angmom_new, orient_new)


def solution(mesh):
    square = P(("groups", "row"), ("col", "sub"))
    spread = P(None, ("groups", "row", "col", "sub"))
    return jax.shard_map(
        shards,
        mesh=mesh,
        in_specs=(square,) * 4 + (P(None, ("groups", "col", "sub")),) + (spread,) * 7,
        out_specs=(square,) + (spread,) * 4,
        check_vma=False,
    )
```

```python
import functools

import jax
import jax.numpy as jnp
from jax import lax
from jax.experimental import pallas as pl
from jax.experimental.pallas import tpu as pltpu
from jax.sharding import PartitionSpec as P

BLOCK = 128
LANES = 128

CHARGE = (-0.834, 0.417, 0.417)
UNIT = 0.417
MULTIPLE = (-2.0, 1.0, 1.0)
OFFSET = ((0.0, 0.0, -0.12), (0.76, 0.0, 0.47), (-0.76, 0.0, 0.47))
COUPLE = 0.1
STEP_DT = 0.5
WATER_MASS = 1.0
INERTIA = 0.5
SOFTEN = 1.0

F32 = jnp.float32
BF16 = jnp.bfloat16

SIN_TERMS = (-1 / 6, 1 / 120, -1 / 5040, 1 / 362880, -1 / 39916800, 1 / 6227020800)
COS_TERMS = (-1 / 2, 1 / 24, -1 / 720, 1 / 40320, -1 / 3628800, 1 / 479001600, -1 / 87178291200)


def at(tile):
    return slice(tile * LANES, (tile + 1) * LANES)


def pick(table, index):
    return jnp.take_along_axis(table, index, axis=1, mode="promise_in_bounds")


def contract(left, right, dims):
    return lax.dot_general(left, right, (dims, ((), ())), preferred_element_type=F32)


def series(square, terms):
    total = jnp.full_like(square, terms[-1])
    for term in terms[-2::-1]:
        total = total * square + term
    return total * square + 1.0


def slot_rows(rows_b, cols_b):
    pattern_at = rows_b + cols_b
    product_at = pattern_at + 1
    return pattern_at, product_at, -(-(product_at + 3 * rows_b) // 8) * 8


def open_kernel(
    ways, rows_n, where, pat_d, pat_s, marg, dip, owner, centres, angles, halo, message, small, sites, quat, shared, count
):
    rows_b, cols_b = pat_d.shape
    pattern_at, product_at, depth = slot_rows(rows_b, cols_b)
    rows = marg.shape[0]
    lane = lax.broadcasted_iota(jnp.int32, (1, LANES), 1)
    patterns = jnp.zeros((1, LANES), F32)
    products = []
    for row in range(rows_b):
        chosen = jnp.int32(0)
        for col in range(cols_b):
            chosen = chosen + col * pat_s[row, col]
            line = row * cols_b + col
            patterns = jnp.where(lane == line, pat_d[row, col].astype(F32), patterns)
            patterns = jnp.where(lane == rows_b * cols_b + line, pat_s[row, col].astype(F32), patterns)
        span = pl.ds(pl.multiple_of(chosen * BLOCK, BLOCK), BLOCK)
        block = marg[row * BLOCK : (row + 1) * BLOCK, span]
        for copy in range(rows_n):
            small[copy * rows + row * BLOCK : copy * rows + (row + 1) * BLOCK, :] = block
        products.append(contract(dip[:, span], block, ((1,), (1,))))
    waters = owner.shape[1]
    hist_rows = count.shape[0]
    total = jnp.zeros(count.shape, F32)
    for source in range(3):
        line = owner[source : source + 1, :]
        high = lax.broadcasted_iota(jnp.int32, (hist_rows, waters), 0) == (line >> 7)
        low = lax.broadcasted_iota(jnp.int32, (LANES, waters), 0) == (line & 127)
        total = total + contract(
            jnp.where(high, MULTIPLE[source], 0.0).astype(BF16),
            jnp.where(low, 1.0, 0.0).astype(BF16),
            ((1,), (1,)),
        )
    count[...] = total
    message[...] = jnp.zeros(message.shape, F32)
    for device in range(rows_n * ways):
        base = device * depth
        row, col = device // ways, device % ways
        message[base : base + rows_b, :] = count[row * rows_b : (row + 1) * rows_b, :]
        message[base + rows_b : base + pattern_at, :] = count[col * cols_b : (col + 1) * cols_b, :]
        message[base + pattern_at : base + product_at, :] = patterns
        for block in range(rows_b):
            start = base + product_at + 3 * block
            message[start : start + 3, :] = products[block]
    water_sites(rows_n, where[0], centres, angles, halo, sites, quat, shared)


def project_kernel(ways, rows_n, where, pat_d, dens, dip, received, out, pot, lines, masked):
    rows_b, cols_b = pat_d.shape
    pattern_at, product_at, depth = slot_rows(rows_b, cols_b)
    here_col = where[1]
    total = jnp.zeros((pattern_at, LANES), F32)
    for device in range(rows_n * ways):
        total = total + received[device * depth : device * depth + pattern_at, :]
    pot[0:pattern_at, :] = UNIT * total
    lines[...] = jnp.zeros(lines.shape, F32)
    for part in range(cols_b // rows_b):
        summed = jnp.zeros((depth, LANES), F32)
        for other in range(ways):
            source = ((here_col * (cols_b // rows_b) + part) * ways + other) * depth
            summed = summed + received[pl.ds(pl.multiple_of(source, 8), depth), :]
        for block in range(rows_b):
            col = part * rows_b + block
            moment = dip[:, at(col)].astype(F32)
            start = product_at + 3 * block
            lines[0:3, at(col)] = summed[start : start + 3] + COUPLE * pot[rows_b + col : rows_b + col + 1, :] * moment
            lines[3:6, at(col)] = moment
    for row in range(rows_b):
        for col in range(cols_b):
            block = dens[row * BLOCK : (row + 1) * BLOCK, at(col)]
            masked[row * BLOCK : (row + 1) * BLOCK, at(col)] = jnp.where(
                pat_d[row, col] != 0, block, jnp.zeros_like(block)
            )
    whole = lines[...]
    first = whole.astype(BF16)
    second = (whole - first.astype(F32)).astype(BF16)
    result = contract(first, masked[...], ((1,), (1,))) + contract(second, masked[...], ((1,), (1,)))
    out_depth = out.shape[0] // (rows_n * ways)
    for row in range(rows_b):
        field = result[0:3, at(row)] + COUPLE * pot[row : row + 1, :] * result[3:6, at(row)]
        for device in range(rows_n * ways):
            start = device * out_depth + 3 * row
            out[start : start + 3, :] = field


def water_sites(rows_n, here_row, centres, angles, halo, sites, quat, shared):
    half_angle = 0.5 * angles[...]
    square = half_angle * half_angle
    sine = half_angle * series(square, SIN_TERMS)
    cosine = series(square, COS_TERMS)
    sin_r, sin_p, sin_y = sine[0:1], sine[1:2], sine[2:3]
    cos_r, cos_p, cos_y = cosine[0:1], cosine[1:2], cosine[2:3]
    comp_w = cos_r * cos_p * cos_y + sin_r * sin_p * sin_y
    comp_x = sin_r * cos_p * cos_y - cos_r * sin_p * sin_y
    comp_y = cos_r * sin_p * cos_y + sin_r * cos_p * sin_y
    comp_z = cos_r * cos_p * sin_y - sin_r * sin_p * cos_y
    for place, comp in enumerate((comp_w, comp_x, comp_y, comp_z)):
        quat[place : place + 1, :] = comp
    first = (
        1.0 - 2.0 * (comp_y * comp_y + comp_z * comp_z),
        2.0 * (comp_x * comp_y + comp_w * comp_z),
        2.0 * (comp_x * comp_z - comp_w * comp_y),
    )
    third = (
        2.0 * (comp_x * comp_z + comp_w * comp_y),
        2.0 * (comp_y * comp_z - comp_w * comp_x),
        1.0 - 2.0 * (comp_x * comp_x + comp_y * comp_y),
    )
    sites[...] = jnp.zeros(sites.shape, F32)
    for source in range(3):
        for compo in range(3):
            place = 3 * source + compo
            position = centres[compo : compo + 1, :] + third[compo] * OFFSET[source][2]
            if OFFSET[source][0] != 0.0:
                position = position + first[compo] * OFFSET[source][0]
            sites[place : place + 1, :] = position
    waters, listed = centres.shape[1], halo.shape[1]
    shared[...] = jnp.zeros(shared.shape, F32)
    for which in range(2):
        other = lax.rem(here_row + (1, rows_n - 1)[which], rows_n)
        for tile in range(listed // LANES):
            index = jnp.broadcast_to(halo[which : which + 1, at(tile)], (8, LANES))
            low, high = index & 127, index >> 7
            for part in range(2):
                found = jnp.zeros((8, LANES), F32)
                for source in range(waters // LANES):
                    value = pick(sites[8 * part : 8 * part + 8, at(source)], low)
                    found = jnp.where(high == source, value, found)
                shared[pl.ds(pl.multiple_of(16 * other + 8 * part, 8), 8), at(tile)] = found


def pair_kernel(rows_n, where, sites, received, neighbours, force, table):
    waters, listed, slots = sites.shape[1], received.shape[1], neighbours.shape[0]
    below = pl.multiple_of(16 * lax.rem(where[0] + rows_n - 1, rows_n), 16)
    above = pl.multiple_of(16 * lax.rem(where[0] + 1, rows_n), 16)
    own_tiles, halo_tiles = waters // LANES, listed // LANES
    tiles = own_tiles + 2 * halo_tiles
    for tile in range(tiles):
        if tile < own_tiles:
            lines = sites[:, at(tile)]
        elif tile < own_tiles + halo_tiles:
            lines = received[pl.ds(below, 16), at(tile - own_tiles)]
        else:
            lines = received[pl.ds(above, 16), at(tile - own_tiles - halo_tiles)]
        for word in range(9):
            table[word, tile] = jnp.broadcast_to(lines[word : word + 1], (8, LANES))

    def one_tile(tile, carry):
        span = pl.ds(pl.multiple_of(tile * LANES, LANES), LANES)
        near = [jnp.zeros((8, LANES), F32) for _ in range(9)]
        far = [jnp.zeros((8, LANES), F32) for _ in range(9)]
        for pair in range(slots // 16):
            index = [neighbours[16 * pair + 8 * part : 16 * pair + 8 * part + 8, span] for part in range(2)]
            low = [value & 127 for value in index]
            high = [value >> 7 for value in index]
            found = [[None, None] for _ in range(9)]
            for source in range(tiles):
                here = [value == source for value in high]
                for word in range(9):
                    line = table[word, source]
                    for part in range(2):
                        value = pick(line, low[part])
                        found[word][part] = (
                            value if source == 0 else jnp.where(here[part], value, found[word][part])
                        )
            for part in range(2):
                for source in range(3):
                    own = [table[3 * source + compo, tile] for compo in range(3)]
                    for target in range(3):
                        gap = [own[compo] - found[3 * target + compo][part] for compo in range(3)]
                        root = lax.rsqrt(gap[0] * gap[0] + gap[1] * gap[1] + gap[2] * gap[2] + SOFTEN)
                        weight = root * root * root
                        sums = near if target == 0 else far
                        for compo in range(3):
                            sums[3 * source + compo] = sums[3 * source + compo] + gap[compo] * weight
        for place in range(9):
            factor = CHARGE[place // 3] * UNIT
            total = factor * (far[place] - 2.0 * near[place])
            force[place : place + 1, span] = jnp.sum(total, axis=0, keepdims=True)
        return carry

    lax.fori_loop(0, own_tiles, one_tile, 0)


def advance_kernel(
    ways,
    rows_n,
    rows_b,
    received,
    owner,
    sites,
    quat,
    pair,
    centres,
    velocity,
    angmom,
    centres_new,
    velocity_new,
    angmom_new,
    orient_new,
    force,
    table,
):
    waters = owner.shape[1]
    depth = received.shape[0] // (rows_n * ways)
    for row in range(rows_n):
        summed = received[row * ways * depth : (row * ways + 1) * depth, :]
        for other in range(1, ways):
            start = (row * ways + other) * depth
            summed = summed + received[start : start + depth, :]
        for block in range(rows_b):
            start = 8 * (row * rows_b + block)
            table[start : start + 3, :] = summed[3 * block : 3 * block + 3]
            table[start + 3 : start + 8, :] = jnp.zeros((5, LANES), F32)
    for tile in range(waters // LANES):
        for source in range(3):
            index = jnp.broadcast_to(owner[source : source + 1, at(tile)], (8, LANES))
            low, high = index & 127, index >> 7
            found = jnp.zeros((8, LANES), F32)
            for block in range(rows_n * rows_b):
                value = pick(table[8 * block : 8 * block + 8, :], low)
                found = jnp.where(high == block, value, found)
            lines = slice(3 * source, 3 * source + 3)
            force[lines, at(tile)] = pair[lines, at(tile)] + CHARGE[source] * found[0:3]

    def cross(left, right):
        return [
            left[1] * right[2] - left[2] * right[1],
            left[2] * right[0] - left[0] * right[2],
            left[0] * right[1] - left[1] * right[0],
        ]

    def split(array):
        return [array[compo : compo + 1, :] for compo in range(3)]

    total = force[0:3, :] + force[3:6, :] + force[6:9, :]
    torque = None
    centre = split(centres)
    for source in range(3):
        lever = [sites[3 * source + compo : 3 * source + compo + 1, :] - centre[compo] for compo in range(3)]
        push = [force[3 * source + compo : 3 * source + compo + 1, :] for compo in range(3)]
        turn = cross(lever, push)
        torque = turn if torque is None else [old + new for old, new in zip(torque, turn)]
    moving = velocity[...] + STEP_DT * total / WATER_MASS
    velocity_new[...] = moving
    centres_new[...] = centres[...] + STEP_DT * moving
    spin = [angmom[compo : compo + 1, :] + STEP_DT * torque[compo] for compo in range(3)]
    for compo in range(3):
        angmom_new[compo : compo + 1, :] = spin[compo]
    omega = [value * (1.0 / INERTIA) for value in spin]
    scalar = quat[0:1, :]
    vector = [quat[compo + 1 : compo + 2, :] for compo in range(3)]
    delta = [-(omega[0] * vector[0] + omega[1] * vector[1] + omega[2] * vector[2])]
    turned = cross(omega, vector)
    delta = delta + [scalar * omega[compo] + turned[compo] for compo in range(3)]
    moved = [old + 0.5 * STEP_DT * new for old, new in zip([scalar] + vector, delta)]
    length = jnp.sqrt(moved[0] * moved[0] + moved[1] * moved[1] + moved[2] * moved[2] + moved[3] * moved[3])
    for place in range(4):
        orient_new[place : place + 1, :] = moved[place] / length


def product_kernel(ways, rows_n, where, pot, received, small, *refs):
    dens = refs[:ways]
    out, panel, masked, total = refs[ways:]
    rows, cols = out.shape
    rows_b, cols_b = rows // BLOCK, cols // BLOCK
    pattern_at, _, depth = slot_rows(rows_b, cols_b)
    here_row, here_col = where[0], where[1]

    def patterns(row, col):
        start = pl.multiple_of((row * ways + col) * depth, 8)
        line = received[pl.ds(start, depth), :][pattern_at : pattern_at + 1]
        return jnp.broadcast_to(line, (8, LANES))

    def flag(lines, place):
        wide = pick(lines, jnp.full((8, LANES), place, jnp.int32))
        return wide[0:1].astype(BF16)

    for other in range(rows_n):
        lines = patterns(other, here_col)
        for row in range(rows_b):
            span = slice(other * rows + row * BLOCK, other * rows + (row + 1) * BLOCK)
            block = small[span, :]
            for col in range(cols_b):
                panel[span, at(col)] = block * flag(lines, rows_b * cols_b + row * cols_b + col)
    ones = jnp.ones((1, LANES), F32)

    def three(value):
        first = value.astype(BF16).astype(F32)
        second = (value - first).astype(BF16).astype(F32)
        return [first, second, value - first - second]

    row_lines = [three(pot[row : row + 1, :]) for row in range(rows_b)]
    col_lines = [three(pot[rows_b + col : rows_b + col + 1, :]) for col in range(cols_b)]
    pad = jnp.zeros((2, LANES), F32)
    left = [jnp.concatenate(value + [ones, ones, ones, pad], axis=0).astype(BF16) for value in row_lines]
    right = [jnp.concatenate([ones, ones, ones] + value + [pad], axis=0).astype(BF16) for value in col_lines]
    for step in range(ways):
        lines = patterns(here_row, here_col ^ step)
        for row in range(rows_b):
            for col in range(cols_b):
                spot = (slice(row * BLOCK, (row + 1) * BLOCK), at(col))
                block = dens[step][spot] * flag(lines, row * cols_b + col)
                masked[spot] = block
                if step == 0:
                    sums = contract(left[row], right[col], ((0,), (0,)))
                    total[spot] = COUPLE * sums * block.astype(F32)
        start = pl.multiple_of((here_col ^ step) * cols, BLOCK)
        total[...] += contract(masked[...], panel[pl.ds(start, cols), :], ((1,), (0,)))
    out[...] = total[...].astype(BF16)


def tie_kernel(first, second, out):
    pass


VMEM = pl.BlockSpec(memory_space=pltpu.VMEM)
SMEM = pl.BlockSpec(memory_space=pltpu.SMEM)


def fetching(kernel, places, *refs):
    refs, semaphore = list(refs[:-1]), refs[-1]
    held = refs[len(refs) - len(places) :]
    copies = [pltpu.make_async_copy(refs[at_], held[n], semaphore.at[n]) for n, at_ in enumerate(places)]
    for copy in copies:
        copy.start()
    for copy in copies:
        copy.wait()
    for n, at_ in enumerate(places):
        refs[at_] = held[n]
    kernel(*refs[: len(refs) - len(places)])


def call(
    kernel, name, outs, operands, scalars=0, scratch=(), cost=(0, 0), whole=VMEM, fetch=(), limit=48 << 20, **more
):
    in_specs = [SMEM] * scalars + [whole] * (len(operands) - scalars)
    scratch = list(scratch)
    if fetch:
        for place in fetch:
            memory = pltpu.SMEM if place < scalars else pltpu.VMEM
            scratch.append(memory(operands[place].shape, operands[place].dtype))
            in_specs[place] = pl.BlockSpec(memory_space=pltpu.HBM)
        scratch.append(pltpu.SemaphoreType.DMA((len(fetch),)))
        kernel = functools.partial(fetching, kernel, tuple(fetch))
    return pl.pallas_call(
        kernel,
        out_shape=[jax.ShapeDtypeStruct(shape, dtype) for shape, dtype in outs],
        in_specs=in_specs,
        out_specs=[whole] * len(outs),
        scratch_shapes=scratch,
        compiler_params=pltpu.CompilerParams(vmem_limit_bytes=limit),
        cost_estimate=pl.CostEstimate(flops=cost[0], bytes_accessed=cost[1], transcendentals=0),
        name=name,
        **more,
    )(*operands)


def shards(
    density,
    margin,
    pattern_d,
    pattern_s,
    dipole,
    owner,
    centres,
    angles,
    velocity,
    angmom,
    halo_list,
    neighbours,
):
    rows, cols = density.shape
    rows_b, cols_b = pattern_d.shape
    rows_n = lax.axis_size("row")
    sub_n = lax.axis_size("sub")
    across = ("col", "sub")
    everyone = ("row", "col", "sub")
    ways = lax.axis_size("col") * sub_n
    devices = rows_n * ways
    hist_rows = rows * rows_n // LANES
    waters, listed = centres.shape[1], halo_list.shape[1]
    where = jnp.stack([lax.axis_index("row"), lax.axis_index(across)]).astype(jnp.int32)
    depth = slot_rows(rows_b, cols_b)[2]
    field_depth = -(-3 * rows_b // 8) * 8

    def swap(value, axis, count, step):
        return lax.ppermute(value, axis, [(i, i ^ step) for i in range(count)])

    def exchange(value, axis):
        return lax.all_to_all(value, axis, 0, 0, tiled=True)

    dens_all = [density] + [None] * (ways - 1)
    for step in [1] + list(range(2, ways, 2)):
        dens_all[step] = swap(density, across, ways, step)

    message, small, sites, quat, shared = call(
        functools.partial(open_kernel, ways, rows_n),
        "open",
        [
            ((devices * depth, LANES), F32),
            ((rows_n * rows, BLOCK), BF16),
            ((16, waters), F32),
            ((4, waters), F32),
            ((rows_n * 16, listed), F32),
        ],
        [where, pattern_d, pattern_s, margin, dipole, owner, centres, angles, halo_list],
        scalars=3,
        scratch=[pltpu.VMEM((hist_rows, LANES), F32)],
        cost=(10**8, 10**6),
        fetch=range(1, 9),
        limit=60 << 20,
    )
    listed_sites = exchange(shared, "row")
    received = exchange(message, everyone)
    small_all = exchange(small, "row")

    tiles = (waters + 2 * listed) // LANES
    (pair,) = call(
        functools.partial(pair_kernel, rows_n),
        "pair_forces",
        [((9, waters), F32)],
        [where, sites, listed_sites, neighbours],
        scalars=1,
        scratch=[pltpu.VMEM((9, tiles, 8, LANES), F32)],
        cost=(10**9, 10**7),
    )
    part, pot = call(
        functools.partial(project_kernel, ways, rows_n),
        "field_part",
        [((devices * field_depth, LANES), F32), ((rows_b + cols_b, LANES), F32)],
        [where, pattern_d, density, dipole, received],
        scalars=2,
        scratch=[pltpu.VMEM((8, cols), F32), pltpu.VMEM((rows, cols), BF16)],
        cost=(10**7, 10**6),
    )
    fields = exchange(part, everyone)

    for step in range(2, ways, 2):
        (dens_all[step],) = call(
            tie_kernel,
            "tie",
            [((rows, cols), BF16)],
            [dens_all[step], pair],
            whole=pl.BlockSpec(memory_space=pl.ANY),
            input_output_aliases={0: 0},
        )
        dens_all[step + 1] = swap(dens_all[step], "sub", sub_n, 1)

    (qm_out,) = call(
        functools.partial(product_kernel, ways, rows_n),
        "product",
        [((rows, cols), BF16)],
        [where, pot, received, small_all] + dens_all,
        scalars=1,
        scratch=[
            pltpu.VMEM((rows * rows_n, cols), BF16),
            pltpu.VMEM((rows, cols), BF16),
            pltpu.VMEM((rows, cols), F32),
        ],
        cost=(10**9, 10**7),
    )
    centres_new, velocity_new, angmom_new, orient_new = call(
        functools.partial(advance_kernel, ways, rows_n, rows_b),
        "advance",
        [((3, waters), F32), ((3, waters), F32), ((3, waters), F32), ((4, waters), F32)],
        [fields, owner, sites, quat, pair, centres, velocity, angmom],
        scratch=[pltpu.VMEM((16, waters), F32), pltpu.VMEM((8 * hist_rows, LANES), F32)],
        cost=(10**7, 10**6),
    )
    return (qm_out, centres_new, velocity_new, angmom_new, orient_new)


def solution(mesh):
    square = P(("groups", "row"), ("col", "sub"))
    spread = P(None, ("groups", "row", "col", "sub"))
    return jax.shard_map(
        shards,
        mesh=mesh,
        in_specs=(square,) * 4 + (P(None, ("groups", "col", "sub")),) + (spread,) * 7,
        out_specs=(square,) + (spread,) * 4,
        check_vma=False,
    )
```

```python
import functools

import jax
import jax.numpy as jnp
from jax import lax
from jax.experimental import pallas as pl
from jax.experimental.pallas import tpu as pltpu
from jax.sharding import PartitionSpec as P

BLOCK = 128
LANES = 128

CHARGE = (-0.834, 0.417, 0.417)
UNIT = 0.417
MULTIPLE = (-2.0, 1.0, 1.0)
OFFSET = ((0.0, 0.0, -0.12), (0.76, 0.0, 0.47), (-0.76, 0.0, 0.47))
COUPLE = 0.1
STEP_DT = 0.5
WATER_MASS = 1.0
INERTIA = 0.5
SOFTEN = 1.0

SHIFT = 1.0
SCALE = 65535.0 / 5.0

F32 = jnp.float32
BF16 = jnp.bfloat16

SIN_TERMS = (-1 / 6, 1 / 120, -1 / 5040, 1 / 362880, -1 / 39916800, 1 / 6227020800)
COS_TERMS = (-1 / 2, 1 / 24, -1 / 720, 1 / 40320, -1 / 3628800, 1 / 479001600, -1 / 87178291200)


def at(tile):
    return slice(tile * LANES, (tile + 1) * LANES)


def pick(table, index):
    return jnp.take_along_axis(table, index, axis=1, mode="promise_in_bounds")


def contract(left, right, dims):
    return lax.dot_general(left, right, (dims, ((), ())), preferred_element_type=F32)


def series(square, terms):
    total = jnp.full_like(square, terms[-1])
    for term in terms[-2::-1]:
        total = total * square + term
    return total * square + 1.0


def line_of(row, comp):
    return 3 * row + comp


def open_kernel(
    ways,
    hist_rows,
    where,
    pat_d,
    pat_s,
    dens,
    marg,
    dip,
    owner,
    centres,
    angles,
    halo,
    message,
    masked,
    small,
    sites,
    quat,
    listed,
):
    rows_b, cols_b = pat_d.shape
    rows, waters = dens.shape[0], owner.shape[1]
    message[...] = jnp.zeros(message.shape, F32)
    masked[rows:, :] = jnp.zeros((masked.shape[0] - rows, masked.shape[1]), BF16)
    masked[rows : rows + 3, :] = dip[...]
    lane = lax.broadcasted_iota(jnp.int32, (1, LANES), 1)
    patterns = jnp.zeros((1, LANES), F32)
    for row in range(rows_b):
        chosen = jnp.int32(0)
        lines = slice(row * BLOCK, (row + 1) * BLOCK)
        for col in range(cols_b):
            chosen = chosen + col * pat_s[row, col]
            patterns = jnp.where(lane == row * cols_b + col, pat_s[row, col].astype(F32), patterns)
            block = dens[lines, at(col)]
            masked[lines, at(col)] = jnp.where(pat_d[row, col] != 0, block, jnp.zeros_like(block))
        span = pl.ds(pl.multiple_of(chosen * BLOCK, BLOCK), BLOCK)
        block = marg[lines, span]
        small[lines, :] = block
        product = contract(dip[:, span], block, ((1,), (1,)))
        for comp in range(3):
            place = hist_rows + line_of(where[0] * rows_b + row, comp)
            message[pl.ds(place, 1), :] = product[comp : comp + 1]
    message[pl.ds(4 * hist_rows + where[0] * ways + where[1], 1), :] = patterns
    total = jnp.zeros((hist_rows, LANES), F32)
    for source in range(3):
        line = owner[source : source + 1, :]
        high = lax.broadcasted_iota(jnp.int32, (hist_rows, waters), 0) == (line >> 7)
        low = lax.broadcasted_iota(jnp.int32, (LANES, waters), 0) == (line & 127)
        total = total + contract(
            jnp.where(high, MULTIPLE[source], 0.0).astype(BF16),
            jnp.where(low, 1.0, 0.0).astype(BF16),
            ((1,), (1,)),
        )
    message[0:hist_rows, :] = total
    water_sites(centres, angles, halo, sites, quat, listed)


def water_sites(centres, angles, halo, sites, quat, listed):
    half_angle = 0.5 * angles[...]
    square = half_angle * half_angle
    sine = half_angle * series(square, SIN_TERMS)
    cosine = series(square, COS_TERMS)
    sin_r, sin_p, sin_y = sine[0:1], sine[1:2], sine[2:3]
    cos_r, cos_p, cos_y = cosine[0:1], cosine[1:2], cosine[2:3]
    comp_w = cos_r * cos_p * cos_y + sin_r * sin_p * sin_y
    comp_x = sin_r * cos_p * cos_y - cos_r * sin_p * sin_y
    comp_y = cos_r * sin_p * cos_y + sin_r * cos_p * sin_y
    comp_z = cos_r * cos_p * sin_y - sin_r * sin_p * cos_y
    for place, comp in enumerate((comp_w, comp_x, comp_y, comp_z)):
        quat[place : place + 1, :] = comp
    first = (
        1.0 - 2.0 * (comp_y * comp_y + comp_z * comp_z),
        2.0 * (comp_x * comp_y + comp_w * comp_z),
        2.0 * (comp_x * comp_z - comp_w * comp_y),
    )
    third = (
        2.0 * (comp_x * comp_z + comp_w * comp_y),
        2.0 * (comp_y * comp_z - comp_w * comp_x),
        1.0 - 2.0 * (comp_x * comp_x + comp_y * comp_y),
    )
    sites[...] = jnp.zeros(sites.shape, F32)
    for source in range(3):
        for compo in range(3):
            place = 3 * source + compo
            position = centres[compo : compo + 1, :] + third[compo] * OFFSET[source][2]
            if OFFSET[source][0] != 0.0:
                position = position + first[compo] * OFFSET[source][0]
            sites[place : place + 1, :] = position
    waters, tiles = centres.shape[1], halo.shape[1] // LANES
    used = 18 * tiles
    if used < listed.shape[0]:
        listed[used:, :] = jnp.zeros((listed.shape[0] - used, LANES), F32)
    for which in range(2):
        for tile in range(tiles):
            index = jnp.broadcast_to(halo[which : which + 1, at(tile)], (8, LANES))
            low, high = index & 127, index >> 7
            for part in range(2):
                found = jnp.zeros((8, LANES), F32)
                for source in range(waters // LANES):
                    value = pick(sites[8 * part : 8 * part + 8, at(source)], low)
                    found = jnp.where(high == source, value, found)
                for comp in range(8 * part, min(8 * part + 8, 9)):
                    place = (which * 9 + comp) * tiles + tile
                    listed[place : place + 1, :] = found[comp - 8 * part : comp - 8 * part + 1]


def merge_kernel(summed, first, second, *refs):
    more, out = refs[:-1], refs[-1]
    if summed > 0:
        out[0:summed, :] = first[0:summed, :] + second[0:summed, :]
    place = summed
    for number, ref in enumerate((first, second) + more):
        start = summed if number < 2 else 0
        count = ref.shape[0] - start
        if count > 0:
            out[place : place + count, :] = ref[start:, :]
            place = place + count


def pair_kernel(rows_n, summed, where, sites, message, neighbours, force, table):
    waters, slots = sites.shape[1], neighbours.shape[0]
    depth = (message.shape[0] - summed) // rows_n
    own_tiles = waters // LANES
    tiles = table.shape[1]
    halo_tiles = (tiles - own_tiles) // 2

    def store(tile, lines):
        fixed = [(line * SCALE + (SHIFT * SCALE + 0.5)).astype(jnp.int32) for line in lines]
        for word in range(5):
            value = fixed[2 * word]
            if word < 4:
                value = value | ((fixed[2 * word + 1] - 32768) << 16)
            table[word, tile] = jnp.broadcast_to(value, (8, LANES))

    for tile in range(own_tiles):
        store(tile, [sites[word : word + 1, at(tile)] for word in range(9)])
    for which in range(2):
        other = lax.rem(where[0] + (rows_n - 1, 1)[which], rows_n)
        start = pl.multiple_of(summed + (where[0] ^ other) * depth, 8)
        lines = message[pl.ds(start, depth), :]
        for tile in range(halo_tiles):
            places = [(which * 9 + word) * halo_tiles + tile for word in range(9)]
            store(own_tiles + which * halo_tiles + tile, [lines[place : place + 1] for place in places])

    def one_tile(tile, carry):
        span = pl.ds(pl.multiple_of(tile * LANES, LANES), LANES)
        lines = sites[:, span]
        own = []
        for word in range(9):
            line = jnp.broadcast_to(lines[word : word + 1] * SCALE + SHIFT * SCALE, (8, LANES))
            own.append((line, line - 32768.0))
        near = [jnp.zeros((8, LANES), F32) for _ in range(9)]
        far = [jnp.zeros((8, LANES), F32) for _ in range(9)]
        for pair in range(slots // 16):
            index = [neighbours[16 * pair + 8 * part : 16 * pair + 8 * part + 8, span] for part in range(2)]
            low = [value & 127 for value in index]
            high = [value >> 7 for value in index]
            found = [[None, None] for _ in range(5)]
            for source in range(tiles):
                here = [value == source for value in high]
                for word in range(5):
                    line = table[word, source]
                    for part in range(2):
                        value = pick(line, low[part])
                        found[word][part] = (
                            value if source == 0 else jnp.where(here[part], value, found[word][part])
                        )
            for part in range(2):
                places = []
                for word in range(9):
                    value = found[word // 2][part]
                    if word == 8:
                        places.append(value.astype(F32))
                    elif word % 2 == 0:
                        places.append((value & 65535).astype(F32))
                    else:
                        places.append((value >> 16).astype(F32))
                for source in range(3):
                    for target in range(3):
                        gap = []
                        for compo in range(3):
                            mine, other = 3 * source + compo, 3 * target + compo
                            gap.append(own[mine][other % 2] - places[other])
                        root = lax.rsqrt(
                            gap[0] * gap[0] + gap[1] * gap[1] + gap[2] * gap[2] + SOFTEN * SCALE * SCALE
                        )
                        weight = root * root * root
                        sums = near if target == 0 else far
                        for compo in range(3):
                            sums[3 * source + compo] = sums[3 * source + compo] + gap[compo] * weight
        for place in range(9):
            factor = CHARGE[place // 3] * UNIT * SCALE * SCALE
            total = factor * (far[place] - 2.0 * near[place])
            force[place : place + 1, span] = jnp.sum(total, axis=0, keepdims=True)
        return carry

    lax.fori_loop(0, own_tiles, one_tile, 0)


def field_kernel(ways, hist_rows, where, message, *refs):
    dens, out, lines = refs[:ways], refs[ways], refs[ways + 1]
    rows, cols = dens[0].shape[0] - 16, dens[0].shape[1]
    rows_b, cols_b = rows // BLOCK, cols // BLOCK
    result = jnp.zeros((16, rows), F32)
    lines[...] = jnp.zeros(lines.shape, F32)
    for step in range(ways):
        moments = dens[step][rows:, :].astype(F32)
        for col in range(cols_b):
            block = (where[1] ^ step) * cols_b + col
            moment = moments[0:3, at(col)]
            pot = UNIT * COUPLE * message[pl.ds(block, 1), :]
            for comp in range(3):
                product = message[pl.ds(hist_rows + line_of(block, comp), 1), :]
                lines[comp : comp + 1, at(col)] = product + pot * moment[comp : comp + 1]
            lines[3:6, at(col)] = moment
        whole = lines[...]
        first = whole.astype(BF16).astype(F32)
        both = jnp.concatenate([first, whole - first], axis=0).astype(BF16)
        result = result + contract(both, dens[step][0:rows, :], ((1,), (1,)))
    total = result[0:8] + result[8:16]
    out[...] = jnp.zeros(out.shape, F32)
    for row in range(rows_b):
        pot = UNIT * COUPLE * message[pl.ds(where[0] * rows_b + row, 1), :]
        start = line_of(row, 0)
        out[start : start + 3, :] = total[0:3, at(row)] + pot * total[3:6, at(row)]


def advance_kernel(
    rows_n,
    rows_b,
    where,
    fields,
    owner,
    sites,
    quat,
    pair,
    centres,
    velocity,
    angmom,
    centres_new,
    velocity_new,
    angmom_new,
    orient_new,
    force,
    table,
):
    waters = owner.shape[1]
    depth = fields.shape[0] // rows_n
    table[...] = jnp.zeros(table.shape, F32)
    for step in range(rows_n):
        for row in range(rows_b):
            start = step * depth + line_of(row, 0)
            place = 8 * (step * rows_b + row)
            table[place : place + 3, :] = fields[start : start + 3, :]
    for tile in range(waters // LANES):
        for source in range(3):
            index = jnp.broadcast_to(owner[source : source + 1, at(tile)], (8, LANES))
            low, high = index & 127, index >> 7
            found = jnp.zeros((8, LANES), F32)
            for step in range(rows_n):
                base = (where[0] ^ step) * rows_b
                for row in range(rows_b):
                    place = 8 * (step * rows_b + row)
                    value = pick(table[place : place + 8, :], low)
                    found = jnp.where(high == base + row, value, found)
            lines = slice(3 * source, 3 * source + 3)
            force[lines, at(tile)] = pair[lines, at(tile)] + CHARGE[source] * found[0:3]

    def cross(left, right):
        return [
            left[1] * right[2] - left[2] * right[1],
            left[2] * right[0] - left[0] * right[2],
            left[0] * right[1] - left[1] * right[0],
        ]

    def split(array):
        return [array[compo : compo + 1, :] for compo in range(3)]

    total = force[0:3, :] + force[3:6, :] + force[6:9, :]
    torque = None
    centre = split(centres)
    for source in range(3):
        lever = [sites[3 * source + compo : 3 * source + compo + 1, :] - centre[compo] for compo in range(3)]
        push = [force[3 * source + compo : 3 * source + compo + 1, :] for compo in range(3)]
        turn = cross(lever, push)
        torque = turn if torque is None else [old + new for old, new in zip(torque, turn)]
    moving = velocity[...] + STEP_DT * total / WATER_MASS
    velocity_new[...] = moving
    centres_new[...] = centres[...] + STEP_DT * moving
    spin = [angmom[compo : compo + 1, :] + STEP_DT * torque[compo] for compo in range(3)]
    for compo in range(3):
        angmom_new[compo : compo + 1, :] = spin[compo]
    omega = [value * (1.0 / INERTIA) for value in spin]
    scalar = quat[0:1, :]
    vector = [quat[compo + 1 : compo + 2, :] for compo in range(3)]
    delta = [-(omega[0] * vector[0] + omega[1] * vector[1] + omega[2] * vector[2])]
    turned = cross(omega, vector)
    delta = delta + [scalar * omega[compo] + turned[compo] for compo in range(3)]
    moved = [old + 0.5 * STEP_DT * new for old, new in zip([scalar] + vector, delta)]
    length = jnp.sqrt(moved[0] * moved[0] + moved[1] * moved[1] + moved[2] * moved[2] + moved[3] * moved[3])
    for place in range(4):
        orient_new[place : place + 1, :] = moved[place] / length


def product_kernel(ways, rows_n, hist_rows, where, message, *refs):
    dens, small = refs[:ways], refs[ways : ways + rows_n]
    out, panel, total = refs[ways + rows_n :]
    rows, cols = out.shape
    rows_b, cols_b = rows // BLOCK, cols // BLOCK
    here_row, here_col = where[0], where[1]
    for step in range(rows_n):
        other = here_row ^ step
        flags = jnp.broadcast_to(message[pl.ds(4 * hist_rows + other * ways + here_col, 1), :], (8, LANES))
        for row in range(rows_b):
            block = small[step][row * BLOCK : (row + 1) * BLOCK, :]
            for col in range(cols_b):
                flag = pick(flags, jnp.full((8, LANES), row * cols_b + col, jnp.int32))
                start = pl.multiple_of(other * rows + row * BLOCK, BLOCK)
                panel[pl.ds(start, BLOCK), at(col)] = block * flag[0:1].astype(BF16)
    ones = jnp.ones((1, LANES), F32)

    def three(value):
        first = value.astype(BF16).astype(F32)
        second = (value - first).astype(BF16).astype(F32)
        return [first, second, value - first - second]

    row_lines = [three(message[pl.ds(here_row * rows_b + row, 1), :]) for row in range(rows_b)]
    col_lines = [three(message[pl.ds(here_col * cols_b + col, 1), :]) for col in range(cols_b)]
    pad = jnp.zeros((2, LANES), F32)
    left = [jnp.concatenate(value + [ones, ones, ones, pad], axis=0).astype(BF16) for value in row_lines]
    right = [jnp.concatenate([ones, ones, ones] + value + [pad], axis=0).astype(BF16) for value in col_lines]
    for row in range(rows_b):
        for col in range(cols_b):
            spot = (slice(row * BLOCK, (row + 1) * BLOCK), at(col))
            sums = contract(left[row], right[col], ((0,), (0,)))
            total[spot] = (UNIT * COUPLE) * sums * dens[0][spot].astype(F32)
    for step in range(ways):
        start = pl.multiple_of((here_col ^ step) * cols, BLOCK)
        value = total[...] + contract(dens[step][0:rows, :], panel[pl.ds(start, cols), :], ((1,), (0,)))
        if step < ways - 1:
            total[...] = value
        else:
            out[...] = value.astype(BF16)


def tie_kernel(first, second, out):
    pass


VMEM = pl.BlockSpec(memory_space=pltpu.VMEM)
SMEM = pl.BlockSpec(memory_space=pltpu.SMEM)


def fetching(kernel, places, *refs):
    refs, semaphore = list(refs[:-1]), refs[-1]
    held = refs[len(refs) - len(places) :]
    copies = [pltpu.make_async_copy(refs[at_], held[n], semaphore.at[n]) for n, at_ in enumerate(places)]
    for copy in copies:
        copy.start()
    for copy in copies:
        copy.wait()
    for n, at_ in enumerate(places):
        refs[at_] = held[n]
    kernel(*refs[: len(refs) - len(places)])


def call(
    kernel, name, outs, operands, scalars=0, scratch=(), cost=(0, 0), whole=VMEM, fetch=(), limit=48 << 20, **more
):
    in_specs = [SMEM] * scalars + [whole] * (len(operands) - scalars)
    scratch = list(scratch)
    if fetch:
        for place in fetch:
            memory = pltpu.SMEM if place < scalars else pltpu.VMEM
            scratch.append(memory(operands[place].shape, operands[place].dtype))
            in_specs[place] = pl.BlockSpec(memory_space=pltpu.HBM)
        scratch.append(pltpu.SemaphoreType.DMA((len(fetch),)))
        kernel = functools.partial(fetching, kernel, tuple(fetch))
    return pl.pallas_call(
        kernel,
        out_shape=[jax.ShapeDtypeStruct(shape, dtype) for shape, dtype in outs],
        in_specs=in_specs,
        out_specs=[whole] * len(outs),
        scratch_shapes=scratch,
        compiler_params=pltpu.CompilerParams(vmem_limit_bytes=limit),
        cost_estimate=pl.CostEstimate(flops=cost[0], bytes_accessed=cost[1], transcendentals=0),
        name=name,
        **more,
    )(*operands)


def doublings(count):
    step = 1
    while step < count:
        yield step
        step = 2 * step


def shards(
    density,
    margin,
    pattern_d,
    pattern_s,
    dipole,
    owner,
    centres,
    angles,
    velocity,
    angmom,
    halo_list,
    neighbours,
):
    rows, cols = density.shape
    rows_b, cols_b = pattern_d.shape
    rows_n = lax.axis_size("row")
    across = ("col", "sub")
    ways = lax.axis_size("col") * lax.axis_size("sub")
    hist_rows = rows * rows_n // LANES
    waters, listed = centres.shape[1], halo_list.shape[1]
    where = jnp.stack([lax.axis_index("row"), lax.axis_index(across)]).astype(jnp.int32)
    summed = -(-(4 * hist_rows + rows_n * ways) // 8) * 8
    halo_rows = -(-18 * (listed // LANES) // 8) * 8
    field_rows = -(-3 * rows_b // 8) * 8

    def swap(value, axis, count, step):
        return lax.ppermute(value, axis, [(i, i ^ step) for i in range(count)])

    def tie(value, later):
        (value,) = call(
            tie_kernel,
            "tie",
            [(value.shape, value.dtype)],
            [value, later],
            whole=pl.BlockSpec(memory_space=pl.ANY),
            input_output_aliases={0: 0},
        )
        return value

    def merge(first, second, count, *more):
        total = count + sum(ref.shape[0] - start for ref, start in [(first, count), (second, count)])
        total = total + sum(ref.shape[0] for ref in more)
        (out,) = call(
            functools.partial(merge_kernel, count), "merge", [((total, LANES), F32)], [first, second] + list(more)
        )
        return out

    def send(value, axis, count):
        held = [value] + [None] * (count - 1)
        for step in doublings(count):
            held[step] = swap(value, axis, count, step)
        return held

    def relay(held, axis, count, later):
        for step in range(1, count):
            lowest = step & -step
            if step != lowest:
                if (step - lowest) & (step - lowest - 1) == 0:
                    held[step - lowest] = tie(held[step - lowest], later)
                held[step] = swap(held[step - lowest], axis, count, lowest)
        return held

    message, masked, small, sites, quat, halo = call(
        functools.partial(open_kernel, ways, hist_rows),
        "open",
        [
            ((summed, LANES), F32),
            ((rows + 16, cols), BF16),
            ((rows, BLOCK), BF16),
            ((16, waters), F32),
            ((4, waters), F32),
            ((halo_rows, LANES), F32),
        ],
        [where, pattern_d, pattern_s, density, margin, dipole, owner, centres, angles, halo_list],
        scalars=3,
        cost=(10**8, 10**6),
        fetch=range(1, 10),
        limit=60 << 20,
    )
    dens_all = send(masked, across, ways)
    steps = list(doublings(ways))
    for step in steps[:-1]:
        message = merge(message, swap(message, across, ways, step), summed)
    message = merge(message, swap(message, across, ways, steps[-1]), summed, halo)
    small_all = send(tie(small, message), "row", rows_n)
    for step in doublings(rows_n):
        message = merge(message, swap(message, "row", rows_n, step), summed)
    dens_all = relay(dens_all, across, ways, message)
    (field,) = call(
        functools.partial(field_kernel, ways, hist_rows),
        "field",
        [((field_rows, LANES), F32)],
        [where, message] + dens_all,
        scalars=1,
        scratch=[pltpu.VMEM((8, cols), F32)],
        cost=(10**7, 10**6),
    )
    small_all = relay(small_all, "row", rows_n, field)
    tiles = (waters + 2 * listed) // LANES
    (pair,) = call(
        functools.partial(pair_kernel, rows_n, summed),
        "pair_forces",
        [((9, waters), F32)],
        [where, sites, message, neighbours],
        scalars=1,
        scratch=[pltpu.VMEM((5, tiles, 8, LANES), jnp.int32)],
        cost=(10**9, 10**7),
    )
    for step in doublings(rows_n):
        field = merge(field, swap(field, "row", rows_n, step), 0)
    (qm_out,) = call(
        functools.partial(product_kernel, ways, rows_n, hist_rows),
        "product",
        [((rows, cols), BF16)],
        [where, message] + dens_all + small_all,
        scalars=1,
        scratch=[pltpu.VMEM((rows * rows_n, cols), BF16), pltpu.VMEM((rows, cols), F32)],
        cost=(10**9, 10**7),
    )
    centres_new, velocity_new, angmom_new, orient_new = call(
        functools.partial(advance_kernel, rows_n, rows_b),
        "advance",
        [((3, waters), F32), ((3, waters), F32), ((3, waters), F32), ((4, waters), F32)],
        [where, field, owner, sites, quat, pair, centres, velocity, angmom],
        scalars=1,
        scratch=[pltpu.VMEM((16, waters), F32), pltpu.VMEM((8 * hist_rows, LANES), F32)],
        cost=(10**7, 10**6),
    )
    return (qm_out, centres_new, velocity_new, angmom_new, orient_new)


def solution(mesh):
    square = P(("groups", "row"), ("col", "sub"))
    spread = P(None, ("groups", "row", "col", "sub"))
    return jax.shard_map(
        shards,
        mesh=mesh,
        in_specs=(square,) * 4 + (P(None, ("groups", "col", "sub")),) + (spread,) * 7,
        out_specs=(square,) + (spread,) * 4,
        check_vma=False,
    )
```

```python
import functools

import jax
import jax.numpy as jnp
from jax import lax
from jax.experimental import pallas as pl
from jax.experimental.pallas import tpu as pltpu
from jax.sharding import PartitionSpec as P

BLOCK = 128
LANES = 128

CHARGE = (-0.834, 0.417, 0.417)
UNIT = 0.417
MULTIPLE = (-2.0, 1.0, 1.0)
OFFSET = ((0.0, 0.0, -0.12), (0.76, 0.0, 0.47), (-0.76, 0.0, 0.47))
COUPLE = 0.1
STEP_DT = 0.5
WATER_MASS = 1.0
INERTIA = 0.5
SOFTEN = 1.0

SHIFT = 1.0
SCALE = 65535.0 / 5.0

F32 = jnp.float32
BF16 = jnp.bfloat16

SIN_TERMS = (-1 / 6, 1 / 120, -1 / 5040, 1 / 362880, -1 / 39916800, 1 / 6227020800)
COS_TERMS = (-1 / 2, 1 / 24, -1 / 720, 1 / 40320, -1 / 3628800, 1 / 479001600, -1 / 87178291200)


def at(tile):
    return slice(tile * LANES, (tile + 1) * LANES)


def pick(table, index):
    return jnp.take_along_axis(table, index, axis=1, mode="promise_in_bounds")


def contract(left, right, dims):
    return lax.dot_general(left, right, (dims, ((), ())), preferred_element_type=F32)


def series(square, terms):
    total = jnp.full_like(square, terms[-1])
    for term in terms[-2::-1]:
        total = total * square + term
    return total * square + 1.0


def line_of(row, comp):
    return 3 * row + comp


def open_kernel(
    ways,
    hist_rows,
    where,
    pat_d,
    pat_s,
    marg,
    dip,
    owner,
    centres,
    angles,
    halo,
    message,
    small,
    sites,
    quat,
    moments,
):
    rows_b, cols_b = pat_d.shape
    waters = owner.shape[1]
    message[...] = jnp.zeros(message.shape, F32)
    moments[...] = jnp.zeros(moments.shape, F32)
    for col in range(cols_b):
        moments[3 * col : 3 * col + 3, :] = dip[:, at(col)].astype(F32)
    lane = lax.broadcasted_iota(jnp.int32, (1, LANES), 1)
    patterns = jnp.zeros((1, LANES), F32)
    for row in range(rows_b):
        chosen = jnp.int32(0)
        lines = slice(row * BLOCK, (row + 1) * BLOCK)
        for col in range(cols_b):
            chosen = chosen + col * pat_s[row, col]
            line = row * cols_b + col
            patterns = jnp.where(lane == line, pat_s[row, col].astype(F32), patterns)
            patterns = jnp.where(lane == rows_b * cols_b + line, pat_d[row, col].astype(F32), patterns)
        span = pl.ds(pl.multiple_of(chosen * BLOCK, BLOCK), BLOCK)
        block = marg[lines, span]
        small[lines, :] = block
        product = contract(dip[:, span], block, ((1,), (1,)))
        for comp in range(3):
            place = hist_rows + line_of(where[0] * rows_b + row, comp)
            message[pl.ds(place, 1), :] = product[comp : comp + 1]
    message[pl.ds(4 * hist_rows + where[0] * ways + where[1], 1), :] = patterns
    total = jnp.zeros((hist_rows, LANES), F32)
    for source in range(3):
        line = owner[source : source + 1, :]
        high = lax.broadcasted_iota(jnp.int32, (hist_rows, waters), 0) == (line >> 7)
        low = lax.broadcasted_iota(jnp.int32, (LANES, waters), 0) == (line & 127)
        total = total + contract(
            jnp.where(high, MULTIPLE[source], 0.0).astype(BF16),
            jnp.where(low, 1.0, 0.0).astype(BF16),
            ((1,), (1,)),
        )
    message[0:hist_rows, :] = total
    summed = message.shape[0] - (-(-18 * (halo.shape[1] // LANES) // 8) * 8)
    water_sites(centres, angles, halo, sites, quat, message.at[summed:, :])


def water_sites(centres, angles, halo, sites, quat, listed):
    half_angle = 0.5 * angles[...]
    square = half_angle * half_angle
    sine = half_angle * series(square, SIN_TERMS)
    cosine = series(square, COS_TERMS)
    sin_r, sin_p, sin_y = sine[0:1], sine[1:2], sine[2:3]
    cos_r, cos_p, cos_y = cosine[0:1], cosine[1:2], cosine[2:3]
    comp_w = cos_r * cos_p * cos_y + sin_r * sin_p * sin_y
    comp_x = sin_r * cos_p * cos_y - cos_r * sin_p * sin_y
    comp_y = cos_r * sin_p * cos_y + sin_r * cos_p * sin_y
    comp_z = cos_r * cos_p * sin_y - sin_r * sin_p * cos_y
    for place, comp in enumerate((comp_w, comp_x, comp_y, comp_z)):
        quat[place : place + 1, :] = comp
    first = (
        1.0 - 2.0 * (comp_y * comp_y + comp_z * comp_z),
        2.0 * (comp_x * comp_y + comp_w * comp_z),
        2.0 * (comp_x * comp_z - comp_w * comp_y),
    )
    third = (
        2.0 * (comp_x * comp_z + comp_w * comp_y),
        2.0 * (comp_y * comp_z - comp_w * comp_x),
        1.0 - 2.0 * (comp_x * comp_x + comp_y * comp_y),
    )
    sites[...] = jnp.zeros(sites.shape, F32)
    for source in range(3):
        for compo in range(3):
            place = 3 * source + compo
            position = centres[compo : compo + 1, :] + third[compo] * OFFSET[source][2]
            if OFFSET[source][0] != 0.0:
                position = position + first[compo] * OFFSET[source][0]
            sites[place : place + 1, :] = position
    waters, tiles = centres.shape[1], halo.shape[1] // LANES
    for which in range(2):
        for tile in range(tiles):
            index = jnp.broadcast_to(halo[which : which + 1, at(tile)], (8, LANES))
            low, high = index & 127, index >> 7
            for part in range(2):
                found = jnp.zeros((8, LANES), F32)
                for source in range(waters // LANES):
                    value = pick(sites[8 * part : 8 * part + 8, at(source)], low)
                    found = jnp.where(high == source, value, found)
                for comp in range(8 * part, min(8 * part + 8, 9)):
                    place = (which * 9 + comp) * tiles + tile
                    listed[place : place + 1, :] = found[comp - 8 * part : comp - 8 * part + 1]


def merge_kernel(summed, first, second, out):
    if summed > 0:
        out[0:summed, :] = first[0:summed, :] + second[0:summed, :]
    count = first.shape[0] - summed
    if count > 0:
        out[summed : summed + count, :] = first[summed:, :]
        out[summed + count :, :] = second[summed:, :]


def turn_kernel(summed, first, second, moments, out, halos):
    out[0:summed, :] = first[0:summed, :] + second[0:summed, :]
    out[summed:, :] = moments[...]
    count = first.shape[0] - summed
    halos[0:count, :] = first[summed:, :]
    halos[count:, :] = second[summed:, :]


def pair_kernel(rows_n, where, sites, halos, neighbours, force, table):
    waters, slots = sites.shape[1], neighbours.shape[0]
    depth = halos.shape[0] // rows_n
    own_tiles = waters // LANES
    tiles = table.shape[1]
    halo_tiles = (tiles - own_tiles) // 2

    def store(tile, lines):
        fixed = [(line * SCALE + (SHIFT * SCALE + 0.5)).astype(jnp.int32) for line in lines]
        for word in range(5):
            value = fixed[2 * word]
            if word < 4:
                value = value | ((fixed[2 * word + 1] - 32768) << 16)
            table[word, tile] = jnp.broadcast_to(value, (8, LANES))

    for tile in range(own_tiles):
        store(tile, [sites[word : word + 1, at(tile)] for word in range(9)])
    for which in range(2):
        other = lax.rem(where[0] + (rows_n - 1, 1)[which], rows_n)
        start = pl.multiple_of((where[0] ^ other) * depth, 8)
        lines = halos[pl.ds(start, depth), :]
        for tile in range(halo_tiles):
            places = [(which * 9 + word) * halo_tiles + tile for word in range(9)]
            store(own_tiles + which * halo_tiles + tile, [lines[place : place + 1] for place in places])

    def one_tile(tile, carry):
        span = pl.ds(pl.multiple_of(tile * LANES, LANES), LANES)
        lines = sites[:, span]
        own = []
        for word in range(9):
            line = jnp.broadcast_to(lines[word : word + 1] * SCALE + SHIFT * SCALE, (8, LANES))
            own.append((line, line - 32768.0))
        near = [jnp.zeros((8, LANES), F32) for _ in range(9)]
        far = [jnp.zeros((8, LANES), F32) for _ in range(9)]
        for pair in range(slots // 16):
            index = [neighbours[16 * pair + 8 * part : 16 * pair + 8 * part + 8, span] for part in range(2)]
            low = [value & 127 for value in index]
            high = [value >> 7 for value in index]
            found = [[None, None] for _ in range(5)]
            for source in range(tiles):
                here = [value == source for value in high]
                for word in range(5):
                    line = table[word, source]
                    for part in range(2):
                        value = pick(line, low[part])
                        found[word][part] = (
                            value if source == 0 else jnp.where(here[part], value, found[word][part])
                        )
            for part in range(2):
                places = []
                for word in range(9):
                    value = found[word // 2][part]
                    if word == 8:
                        places.append(value.astype(F32))
                    elif word % 2 == 0:
                        places.append((value & 65535).astype(F32))
                    else:
                        places.append((value >> 16).astype(F32))
                for source in range(3):
                    for target in range(3):
                        gap = []
                        for compo in range(3):
                            mine, other = 3 * source + compo, 3 * target + compo
                            gap.append(own[mine][other % 2] - places[other])
                        root = lax.rsqrt(
                            gap[0] * gap[0] + gap[1] * gap[1] + gap[2] * gap[2] + SOFTEN * SCALE * SCALE
                        )
                        weight = root * root * root
                        sums = near if target == 0 else far
                        for compo in range(3):
                            sums[3 * source + compo] = sums[3 * source + compo] + gap[compo] * weight
        for place in range(9):
            factor = CHARGE[place // 3] * UNIT * SCALE * SCALE
            total = factor * (far[place] - 2.0 * near[place])
            force[place : place + 1, span] = jnp.sum(total, axis=0, keepdims=True)
        return carry

    lax.fori_loop(0, own_tiles, one_tile, 0)


def pattern_flags(message, hist_rows, device):
    line = jnp.broadcast_to(message[pl.ds(4 * hist_rows + device, 1), :], (8, LANES))
    return lambda place: pick(line, jnp.full((8, LANES), place, jnp.int32))[0:1].astype(BF16)


def field_kernel(ways, hist_rows, summed, where, message, *refs):
    dens, out, masked, lines = refs[:ways], refs[ways], refs[ways + 1], refs[ways + 2]
    rows, cols = dens[0].shape
    rows_b, cols_b = rows // BLOCK, cols // BLOCK
    depth = (message.shape[0] - summed) // ways
    result = jnp.zeros((16, rows), F32)
    lines[...] = jnp.zeros(lines.shape, F32)
    for step in range(ways):
        device = where[1] ^ step
        flag = pattern_flags(message, hist_rows, where[0] * ways + device)
        for col in range(cols_b):
            block = device * cols_b + col
            start = summed + step * depth + 3 * col
            moment = message[start : start + 3, :]
            pot = UNIT * COUPLE * message[pl.ds(block, 1), :]
            for comp in range(3):
                product = message[pl.ds(hist_rows + line_of(block, comp), 1), :]
                lines[comp : comp + 1, at(col)] = product + pot * moment[comp : comp + 1]
            lines[3:6, at(col)] = moment
            for row in range(rows_b):
                spot = slice(row * BLOCK, (row + 1) * BLOCK)
                masked[step, spot, at(col)] = dens[step][spot, at(col)] * flag(
                    rows_b * cols_b + row * cols_b + col
                )
        whole = lines[...]
        first = whole.astype(BF16).astype(F32)
        both = jnp.concatenate([first, whole - first], axis=0).astype(BF16)
        result = result + contract(both, masked[step], ((1,), (1,)))
    total = result[0:8] + result[8:16]
    out[...] = jnp.zeros(out.shape, F32)
    for row in range(rows_b):
        pot = UNIT * COUPLE * message[pl.ds(where[0] * rows_b + row, 1), :]
        start = line_of(row, 0)
        out[start : start + 3, :] = total[0:3, at(row)] + pot * total[3:6, at(row)]


def advance_kernel(
    rows_n,
    rows_b,
    where,
    fields,
    owner,
    sites,
    quat,
    pair,
    centres,
    velocity,
    angmom,
    centres_new,
    velocity_new,
    angmom_new,
    orient_new,
    force,
    table,
):
    waters = owner.shape[1]
    depth = fields.shape[0] // rows_n
    table[...] = jnp.zeros(table.shape, F32)
    for step in range(rows_n):
        for row in range(rows_b):
            start = step * depth + line_of(row, 0)
            place = 8 * (step * rows_b + row)
            table[place : place + 3, :] = fields[start : start + 3, :]
    for tile in range(waters // LANES):
        for source in range(3):
            index = jnp.broadcast_to(owner[source : source + 1, at(tile)], (8, LANES))
            low, high = index & 127, index >> 7
            found = jnp.zeros((8, LANES), F32)
            for step in range(rows_n):
                base = (where[0] ^ step) * rows_b
                for row in range(rows_b):
                    place = 8 * (step * rows_b + row)
                    value = pick(table[place : place + 8, :], low)
                    found = jnp.where(high == base + row, value, found)
            lines = slice(3 * source, 3 * source + 3)
            force[lines, at(tile)] = pair[lines, at(tile)] + CHARGE[source] * found[0:3]

    def cross(left, right):
        return [
            left[1] * right[2] - left[2] * right[1],
            left[2] * right[0] - left[0] * right[2],
            left[0] * right[1] - left[1] * right[0],
        ]

    def split(array):
        return [array[compo : compo + 1, :] for compo in range(3)]

    total = force[0:3, :] + force[3:6, :] + force[6:9, :]
    torque = None
    centre = split(centres)
    for source in range(3):
        lever = [sites[3 * source + compo : 3 * source + compo + 1, :] - centre[compo] for compo in range(3)]
        push = [force[3 * source + compo : 3 * source + compo + 1, :] for compo in range(3)]
        turn = cross(lever, push)
        torque = turn if torque is None else [old + new for old, new in zip(torque, turn)]
    moving = velocity[...] + STEP_DT * total / WATER_MASS
    velocity_new[...] = moving
    centres_new[...] = centres[...] + STEP_DT * moving
    spin = [angmom[compo : compo + 1, :] + STEP_DT * torque[compo] for compo in range(3)]
    for compo in range(3):
        angmom_new[compo : compo + 1, :] = spin[compo]
    omega = [value * (1.0 / INERTIA) for value in spin]
    scalar = quat[0:1, :]
    vector = [quat[compo + 1 : compo + 2, :] for compo in range(3)]
    delta = [-(omega[0] * vector[0] + omega[1] * vector[1] + omega[2] * vector[2])]
    turned = cross(omega, vector)
    delta = delta + [scalar * omega[compo] + turned[compo] for compo in range(3)]
    moved = [old + 0.5 * STEP_DT * new for old, new in zip([scalar] + vector, delta)]
    length = jnp.sqrt(moved[0] * moved[0] + moved[1] * moved[1] + moved[2] * moved[2] + moved[3] * moved[3])
    for place in range(4):
        orient_new[place : place + 1, :] = moved[place] / length


def product_kernel(ways, rows_n, hist_rows, where, message, *refs):
    dens, small = refs[0], refs[1 : 1 + rows_n]
    out, panel, total = refs[1 + rows_n :]
    rows, cols = out.shape
    rows_b, cols_b = rows // BLOCK, cols // BLOCK
    here_row, here_col = where[0], where[1]
    for step in range(rows_n):
        other = here_row ^ step
        flag = pattern_flags(message, hist_rows, other * ways + here_col)
        for row in range(rows_b):
            block = small[step][row * BLOCK : (row + 1) * BLOCK, :]
            for col in range(cols_b):
                start = pl.multiple_of(other * rows + row * BLOCK, BLOCK)
                panel[pl.ds(start, BLOCK), at(col)] = block * flag(row * cols_b + col)
    ones = jnp.ones((1, LANES), F32)

    def three(value):
        first = value.astype(BF16).astype(F32)
        second = (value - first).astype(BF16).astype(F32)
        return [first, second, value - first - second]

    row_lines = [three(message[pl.ds(here_row * rows_b + row, 1), :]) for row in range(rows_b)]
    col_lines = [three(message[pl.ds(here_col * cols_b + col, 1), :]) for col in range(cols_b)]
    pad = jnp.zeros((2, LANES), F32)
    left = [jnp.concatenate(value + [ones, ones, ones, pad], axis=0).astype(BF16) for value in row_lines]
    right = [jnp.concatenate([ones, ones, ones] + value + [pad], axis=0).astype(BF16) for value in col_lines]
    for row in range(rows_b):
        for col in range(cols_b):
            spot = (slice(row * BLOCK, (row + 1) * BLOCK), at(col))
            sums = contract(left[row], right[col], ((0,), (0,)))
            total[spot] = (UNIT * COUPLE) * sums * dens[0, spot[0], spot[1]].astype(F32)
    for step in range(ways):
        start = pl.multiple_of((here_col ^ step) * cols, BLOCK)
        value = total[...] + contract(dens[step], panel[pl.ds(start, cols), :], ((1,), (0,)))
        if step < ways - 1:
            total[...] = value
        else:
            out[...] = value.astype(BF16)


def tie_kernel(first, second, out):
    pass


VMEM = pl.BlockSpec(memory_space=pltpu.VMEM)
SMEM = pl.BlockSpec(memory_space=pltpu.SMEM)


def fetching(kernel, places, *refs):
    refs, semaphore = list(refs[:-1]), refs[-1]
    held = refs[len(refs) - len(places) :]
    copies = [pltpu.make_async_copy(refs[at_], held[n], semaphore.at[n]) for n, at_ in enumerate(places)]
    for copy in copies:
        copy.start()
    for copy in copies:
        copy.wait()
    for n, at_ in enumerate(places):
        refs[at_] = held[n]
    kernel(*refs[: len(refs) - len(places)])


def call(
    kernel, name, outs, operands, scalars=0, scratch=(), cost=(0, 0), whole=VMEM, fetch=(), limit=48 << 20, **more
):
    in_specs = [SMEM] * scalars + [whole] * (len(operands) - scalars)
    scratch = list(scratch)
    if fetch:
        for place in fetch:
            memory = pltpu.SMEM if place < scalars else pltpu.VMEM
            scratch.append(memory(operands[place].shape, operands[place].dtype))
            in_specs[place] = pl.BlockSpec(memory_space=pltpu.HBM)
        scratch.append(pltpu.SemaphoreType.DMA((len(fetch),)))
        kernel = functools.partial(fetching, kernel, tuple(fetch))
    return pl.pallas_call(
        kernel,
        out_shape=[jax.ShapeDtypeStruct(shape, dtype) for shape, dtype in outs],
        in_specs=in_specs,
        out_specs=[whole] * len(outs),
        scratch_shapes=scratch,
        compiler_params=pltpu.CompilerParams(vmem_limit_bytes=limit),
        cost_estimate=pl.CostEstimate(flops=cost[0], bytes_accessed=cost[1], transcendentals=0),
        name=name,
        **more,
    )(*operands)


def doublings(count):
    step = 1
    while step < count:
        yield step
        step = 2 * step


def shards(
    density,
    margin,
    pattern_d,
    pattern_s,
    dipole,
    owner,
    centres,
    angles,
    velocity,
    angmom,
    halo_list,
    neighbours,
):
    rows, cols = density.shape
    rows_b, cols_b = pattern_d.shape
    rows_n = lax.axis_size("row")
    across = ("col", "sub")
    ways = lax.axis_size("col") * lax.axis_size("sub")
    hist_rows = rows * rows_n // LANES
    waters, listed = centres.shape[1], halo_list.shape[1]
    where = jnp.stack([lax.axis_index("row"), lax.axis_index(across)]).astype(jnp.int32)
    summed = -(-(4 * hist_rows + rows_n * ways) // 8) * 8
    halo_rows = -(-18 * (listed // LANES) // 8) * 8
    field_rows = -(-3 * rows_b // 8) * 8
    moment_rows = -(-3 * cols_b // 8) * 8

    def swap(value, axis, count, step):
        return lax.ppermute(value, axis, [(i, i ^ step) for i in range(count)])

    def tie(value, later):
        (value,) = call(
            tie_kernel,
            "tie",
            [(value.shape, value.dtype)],
            [value, later],
            whole=pl.BlockSpec(memory_space=pl.ANY),
            input_output_aliases={0: 0},
        )
        return value

    def merge(first, second, count):
        total = 2 * first.shape[0] - count
        (out,) = call(functools.partial(merge_kernel, count), "merge", [((total, LANES), F32)], [first, second])
        return out

    def send(value, axis, count):
        held = [value] + [None] * (count - 1)
        for step in doublings(count):
            held[step] = swap(value, axis, count, step)
        return held

    def relay(held, axis, count, later):
        for step in range(1, count):
            lowest = step & -step
            if step != lowest:
                if (step - lowest) & (step - lowest - 1) == 0:
                    held[step - lowest] = tie(held[step - lowest], later)
                held[step] = swap(held[step - lowest], axis, count, lowest)
        return held

    dens_all = send(density, across, ways)
    message, small, sites, quat, moments = call(
        functools.partial(open_kernel, ways, hist_rows),
        "open",
        [
            ((summed + halo_rows, LANES), F32),
            ((rows, BLOCK), BF16),
            ((16, waters), F32),
            ((4, waters), F32),
            ((moment_rows, LANES), F32),
        ],
        [where, pattern_d, pattern_s, margin, dipole, owner, centres, angles, halo_list],
        scalars=3,
        cost=(10**6, 12 * 10**6),
        fetch=range(1, 9),
        limit=60 << 20,
    )
    steps = list(doublings(rows_n))
    for step in steps[:-1]:
        message = merge(message, swap(message, "row", rows_n, step), summed)
    message, halos = call(
        functools.partial(turn_kernel, summed),
        "turn",
        [((summed + moment_rows, LANES), F32), ((rows_n * halo_rows, LANES), F32)],
        [message, swap(message, "row", rows_n, steps[-1]), moments],
    )
    dens_all = relay(dens_all, across, ways, message)
    small_all = send(tie(small, message), "row", rows_n)
    for step in doublings(ways):
        message = merge(message, swap(message, across, ways, step), summed)
    field, masked = call(
        functools.partial(field_kernel, ways, hist_rows, summed),
        "field",
        [((field_rows, LANES), F32), ((ways, rows, cols), BF16)],
        [where, message] + dens_all,
        scalars=1,
        scratch=[pltpu.VMEM((8, cols), F32)],
        cost=(10**6, 5 * 10**6),
    )
    small_all = relay(small_all, "row", rows_n, field)
    tiles = (waters + 2 * listed) // LANES
    (pair,) = call(
        functools.partial(pair_kernel, rows_n),
        "pair_forces",
        [((9, waters), F32)],
        [where, sites, halos, neighbours],
        scalars=1,
        scratch=[pltpu.VMEM((5, tiles, 8, LANES), jnp.int32)],
        cost=(10**6, 15 * 10**6),
    )
    for step in doublings(rows_n):
        field = merge(field, swap(field, "row", rows_n, step), 0)
    (qm_out,) = call(
        functools.partial(product_kernel, ways, rows_n, hist_rows),
        "product",
        [((rows, cols), BF16)],
        [where, message, masked] + small_all,
        scalars=1,
        scratch=[pltpu.VMEM((rows * rows_n, cols), BF16), pltpu.VMEM((rows, cols), F32)],
        cost=(10**6, 15 * 10**6),
    )
    centres_new, velocity_new, angmom_new, orient_new = call(
        functools.partial(advance_kernel, rows_n, rows_b),
        "advance",
        [((3, waters), F32), ((3, waters), F32), ((3, waters), F32), ((4, waters), F32)],
        [where, field, owner, sites, quat, pair, centres, velocity, angmom],
        scalars=1,
        scratch=[pltpu.VMEM((16, waters), F32), pltpu.VMEM((8 * hist_rows, LANES), F32)],
        cost=(10**6, 6 * 10**6),
    )
    return (qm_out, centres_new, velocity_new, angmom_new, orient_new)


def solution(mesh):
    square = P(("groups", "row"), ("col", "sub"))
    spread = P(None, ("groups", "row", "col", "sub"))
    return jax.shard_map(
        shards,
        mesh=mesh,
        in_specs=(square,) * 4 + (P(None, ("groups", "col", "sub")),) + (spread,) * 7,
        out_specs=(square,) + (spread,) * 4,
        check_vma=False,
    )
```

```python
import functools

import jax
import jax.numpy as jnp
from jax import lax
from jax.experimental import pallas as pl
from jax.experimental.pallas import tpu as pltpu
from jax.sharding import PartitionSpec as P

BLOCK = 128
LANES = 128

CHARGE = (-0.834, 0.417, 0.417)
UNIT = 0.417
MULTIPLE = (-2.0, 1.0, 1.0)
OFFSET = ((0.0, 0.0, -0.12), (0.76, 0.0, 0.47), (-0.76, 0.0, 0.47))
COUPLE = 0.1
STEP_DT = 0.5
WATER_MASS = 1.0
INERTIA = 0.5
SOFTEN = 1.0

SHIFT = 1.0
SCALE = 65535.0 / 5.0

F32 = jnp.float32
BF16 = jnp.bfloat16

SIN_TERMS = (-1 / 6, 1 / 120, -1 / 5040, 1 / 362880, -1 / 39916800, 1 / 6227020800)
COS_TERMS = (-1 / 2, 1 / 24, -1 / 720, 1 / 40320, -1 / 3628800, 1 / 479001600, -1 / 87178291200)


def at(tile):
    return slice(tile * LANES, (tile + 1) * LANES)


def position():
    return lax.axis_index("row"), lax.axis_index(("col", "sub"))


def pick(table, index):
    return jnp.take_along_axis(table, index, axis=1, mode="promise_in_bounds")


def contract(left, right, dims):
    return lax.dot_general(left, right, (dims, ((), ())), preferred_element_type=F32)


def series(square, terms):
    total = jnp.full_like(square, terms[-1])
    for term in terms[-2::-1]:
        total = total * square + term
    return total * square + 1.0


def line_of(row, comp):
    return 3 * row + comp


def round8(count):
    return -(-count // 8) * 8


def open_kernel(
    ways,
    hist_rows,
    pat_d,
    pat_s,
    marg,
    dip,
    owner,
    centres,
    angles,
    halo,
    message,
    small,
    again,
    sites,
    quat,
    moments,
):
    rows_b, cols_b = pat_d.shape
    waters = owner.shape[1]
    here_col = position()[1]
    message[...] = jnp.zeros(message.shape, F32)
    moments[...] = jnp.zeros(moments.shape, F32)
    for col in range(cols_b):
        moments[3 * col : 3 * col + 3, :] = dip[:, at(col)].astype(F32)
    lane = lax.broadcasted_iota(jnp.int32, (1, LANES), 1)
    patterns = jnp.zeros((1, LANES), F32)
    for row in range(rows_b):
        chosen = jnp.int32(0)
        lines = slice(row * BLOCK, (row + 1) * BLOCK)
        for col in range(cols_b):
            chosen = chosen + col * pat_s[row, col]
            line = row * cols_b + col
            patterns = jnp.where(lane == line, pat_s[row, col].astype(F32), patterns)
            patterns = jnp.where(lane == rows_b * cols_b + line, pat_d[row, col].astype(F32), patterns)
        span = pl.ds(pl.multiple_of(chosen * BLOCK, BLOCK), BLOCK)
        block = marg[lines, span]
        for copy in (small, again):
            copy[lines, :] = block
        product = contract(dip[:, span], block, ((1,), (1,)))
        place = hist_rows + line_of(row, 0)
        message[place : place + 3, :] = product
    message[pl.ds(hist_rows + 3 * rows_b + here_col, 1), :] = patterns
    total = jnp.zeros((hist_rows, LANES), F32)
    for source in range(3):
        line = owner[source : source + 1, :]
        high = lax.broadcasted_iota(jnp.int32, (hist_rows, waters), 0) == (line >> 7)
        low = lax.broadcasted_iota(jnp.int32, (LANES, waters), 0) == (line & 127)
        total = total + contract(
            jnp.where(high, MULTIPLE[source], 0.0).astype(BF16),
            jnp.where(low, 1.0, 0.0).astype(BF16),
            ((1,), (1,)),
        )
    message[0:hist_rows, :] = total
    halo_at = hist_rows + round8(3 * rows_b + ways)
    water_sites(centres, angles, halo, sites, quat, message.at[halo_at:, :])


def water_sites(centres, angles, halo, sites, quat, listed):
    half_angle = 0.5 * angles[...]
    square = half_angle * half_angle
    sine = half_angle * series(square, SIN_TERMS)
    cosine = series(square, COS_TERMS)
    sin_r, sin_p, sin_y = sine[0:1], sine[1:2], sine[2:3]
    cos_r, cos_p, cos_y = cosine[0:1], cosine[1:2], cosine[2:3]
    comp_w = cos_r * cos_p * cos_y + sin_r * sin_p * sin_y
    comp_x = sin_r * cos_p * cos_y - cos_r * sin_p * sin_y
    comp_y = cos_r * sin_p * cos_y + sin_r * cos_p * sin_y
    comp_z = cos_r * cos_p * sin_y - sin_r * sin_p * cos_y
    for place, comp in enumerate((comp_w, comp_x, comp_y, comp_z)):
        quat[place : place + 1, :] = comp
    first = (
        1.0 - 2.0 * (comp_y * comp_y + comp_z * comp_z),
        2.0 * (comp_x * comp_y + comp_w * comp_z),
        2.0 * (comp_x * comp_z - comp_w * comp_y),
    )
    third = (
        2.0 * (comp_x * comp_z + comp_w * comp_y),
        2.0 * (comp_y * comp_z - comp_w * comp_x),
        1.0 - 2.0 * (comp_x * comp_x + comp_y * comp_y),
    )
    sites[...] = jnp.zeros(sites.shape, F32)
    for source in range(3):
        for compo in range(3):
            place = 3 * source + compo
            position = centres[compo : compo + 1, :] + third[compo] * OFFSET[source][2]
            if OFFSET[source][0] != 0.0:
                position = position + first[compo] * OFFSET[source][0]
            sites[place : place + 1, :] = position
    waters, tiles = centres.shape[1], halo.shape[1] // LANES
    for which in range(2):
        for tile in range(tiles):
            index = jnp.broadcast_to(halo[which : which + 1, at(tile)], (8, LANES))
            low, high = index & 127, index >> 7
            for part in range(2):
                found = jnp.zeros((8, LANES), F32)
                for source in range(waters // LANES):
                    value = pick(sites[8 * part : 8 * part + 8, at(source)], low)
                    found = jnp.where(high == source, value, found)
                for comp in range(8 * part, min(8 * part + 8, 9)):
                    place = (which * 9 + comp) * tiles + tile
                    listed[place : place + 1, :] = found[comp - 8 * part : comp - 8 * part + 1]


def merge_kernel(summed, first, second, out):
    if summed > 0:
        out[0:summed, :] = first[0:summed, :] + second[0:summed, :]
    count = first.shape[0] - summed
    if count > 0:
        out[summed : summed + count, :] = first[summed:, :]
        out[summed + count :, :] = second[summed:, :]


def turn_kernel(summed, block_rows, halo_rows, first, second, moments, out, halos):
    out[0:summed, :] = first[0:summed, :] + second[0:summed, :]
    count = (first.shape[0] - summed) // (block_rows + halo_rows)
    for number, ref in enumerate((first, second)):
        for block in range(count):
            start = summed + block * (block_rows + halo_rows)
            place = number * count + block
            out[summed + place * block_rows : summed + (place + 1) * block_rows, :] = ref[
                start : start + block_rows, :
            ]
            halos[place * halo_rows : (place + 1) * halo_rows, :] = ref[
                start + block_rows : start + block_rows + halo_rows, :
            ]
    out[summed + 2 * count * block_rows :, :] = moments[...]


def pair_kernel(rows_n, sites, halos, neighbours, force, table):
    waters, slots = sites.shape[1], neighbours.shape[0]
    depth = halos.shape[0] // rows_n
    own_tiles = waters // LANES
    tiles = table.shape[1]
    halo_tiles = (tiles - own_tiles) // 2

    def store(tile, lines):
        fixed = [(line * SCALE + (SHIFT * SCALE + 0.5)).astype(jnp.int32) for line in lines]
        for word in range(5):
            value = fixed[2 * word]
            if word < 4:
                value = value | ((fixed[2 * word + 1] - 32768) << 16)
            table[word, tile] = jnp.broadcast_to(value, (8, LANES))

    for tile in range(own_tiles):
        store(tile, [sites[word : word + 1, at(tile)] for word in range(9)])
    for which in range(2):
        here_row = position()[0]
        other = lax.rem(here_row + (rows_n - 1, 1)[which], rows_n)
        start = pl.multiple_of((here_row ^ other) * depth, 8)
        lines = halos[pl.ds(start, depth), :]
        for tile in range(halo_tiles):
            places = [(which * 9 + word) * halo_tiles + tile for word in range(9)]
            store(own_tiles + which * halo_tiles + tile, [lines[place : place + 1] for place in places])

    def one_tile(tile, carry):
        span = pl.ds(pl.multiple_of(tile * LANES, LANES), LANES)
        lines = sites[:, span]
        own = []
        for word in range(9):
            line = jnp.broadcast_to(lines[word : word + 1] * SCALE + SHIFT * SCALE, (8, LANES))
            own.append((line, line - 32768.0))
        near = [jnp.zeros((8, LANES), F32) for _ in range(9)]
        far = [jnp.zeros((8, LANES), F32) for _ in range(9)]
        for pair in range(slots // 16):
            index = [neighbours[16 * pair + 8 * part : 16 * pair + 8 * part + 8, span] for part in range(2)]
            low = [value & 127 for value in index]
            high = [value >> 7 for value in index]
            found = [[None, None] for _ in range(5)]
            for source in range(tiles):
                here = [value == source for value in high]
                for word in range(5):
                    line = table[word, source]
                    for part in range(2):
                        value = pick(line, low[part])
                        found[word][part] = (
                            value if source == 0 else jnp.where(here[part], value, found[word][part])
                        )
            for part in range(2):
                places = []
                for word in range(9):
                    value = found[word // 2][part]
                    if word == 8:
                        places.append(value.astype(F32))
                    elif word % 2 == 0:
                        places.append((value & 65535).astype(F32))
                    else:
                        places.append((value >> 16).astype(F32))
                for source in range(3):
                    for target in range(3):
                        gap = []
                        for compo in range(3):
                            mine, other = 3 * source + compo, 3 * target + compo
                            gap.append(own[mine][other % 2] - places[other])
                        root = lax.rsqrt(
                            gap[0] * gap[0] + gap[1] * gap[1] + gap[2] * gap[2] + SOFTEN * SCALE * SCALE
                        )
                        weight = root * root * root
                        sums = near if target == 0 else far
                        for compo in range(3):
                            sums[3 * source + compo] = sums[3 * source + compo] + gap[compo] * weight
        for place in range(9):
            factor = CHARGE[place // 3] * UNIT * SCALE * SCALE
            total = factor * (far[place] - 2.0 * near[place])
            force[place : place + 1, span] = jnp.sum(total, axis=0, keepdims=True)
        return carry

    lax.fori_loop(0, own_tiles, one_tile, 0)


def pattern_flags(message, place):
    line = jnp.broadcast_to(message[pl.ds(place, 1), :], (8, LANES))
    return lambda block: pick(line, jnp.full((8, LANES), block, jnp.int32))[0:1].astype(BF16)


def field_kernel(ways, hist_rows, block_rows, summed, message, *refs):
    dens, out, masked, lines = refs[:ways], refs[ways], refs[ways + 1], refs[ways + 2]
    rows, cols = dens[0].shape
    rows_b, cols_b = rows // BLOCK, cols // BLOCK
    depth = (message.shape[0] - summed) // ways
    here_row, here_col = position()
    result = jnp.zeros((16, rows), F32)
    lines[...] = jnp.zeros(lines.shape, F32)
    for step in range(ways):
        device = here_col ^ step
        flag = pattern_flags(message, hist_rows + 3 * rows_b + device)
        for col in range(cols_b):
            other = device * (cols_b // rows_b) + col // rows_b
            place = hist_rows + (here_row ^ other) * block_rows + line_of(col % rows_b, 0)
            start = summed + step * depth + 3 * col
            moment = message[start : start + 3, :]
            pot = UNIT * COUPLE * message[pl.ds(device * cols_b + col, 1), :]
            for comp in range(3):
                product = message[pl.ds(place + comp, 1), :]
                lines[comp : comp + 1, at(col)] = product + pot * moment[comp : comp + 1]
            lines[3:6, at(col)] = moment
            for row in range(rows_b):
                spot = slice(row * BLOCK, (row + 1) * BLOCK)
                target = slice(step * cols + col * BLOCK, step * cols + (col + 1) * BLOCK)
                masked[spot, target] = dens[step][spot, at(col)] * flag(rows_b * cols_b + row * cols_b + col)
        whole = lines[...]
        first = whole.astype(BF16).astype(F32)
        both = jnp.concatenate([first, whole - first], axis=0).astype(BF16)
        result = result + contract(both, masked[:, step * cols : (step + 1) * cols], ((1,), (1,)))
    total = result[0:8] + result[8:16]
    out[...] = jnp.zeros(out.shape, F32)
    for row in range(rows_b):
        pot = UNIT * COUPLE * message[pl.ds(here_row * rows_b + row, 1), :]
        start = line_of(row, 0)
        out[start : start + 3, :] = total[0:3, at(row)] + pot * total[3:6, at(row)]


def advance_kernel(
    rows_n,
    rows_b,
    fields,
    owner,
    sites,
    quat,
    pair,
    centres,
    velocity,
    angmom,
    centres_new,
    velocity_new,
    angmom_new,
    orient_new,
    force,
    table,
):
    waters = owner.shape[1]
    depth = fields.shape[0] // rows_n
    here_row = position()[0]
    table[...] = jnp.zeros(table.shape, F32)
    for step in range(rows_n):
        for row in range(rows_b):
            start = step * depth + line_of(row, 0)
            place = 8 * (step * rows_b + row)
            table[place : place + 3, :] = fields[start : start + 3, :]
    for tile in range(waters // LANES):
        for source in range(3):
            index = jnp.broadcast_to(owner[source : source + 1, at(tile)], (8, LANES))
            low, high = index & 127, index >> 7
            found = jnp.zeros((8, LANES), F32)
            for step in range(rows_n):
                base = (here_row ^ step) * rows_b
                for row in range(rows_b):
                    place = 8 * (step * rows_b + row)
                    value = pick(table[place : place + 8, :], low)
                    found = jnp.where(high == base + row, value, found)
            lines = slice(3 * source, 3 * source + 3)
            force[lines, at(tile)] = pair[lines, at(tile)] + CHARGE[source] * found[0:3]

    def cross(left, right):
        return [
            left[1] * right[2] - left[2] * right[1],
            left[2] * right[0] - left[0] * right[2],
            left[0] * right[1] - left[1] * right[0],
        ]

    def split(array):
        return [array[compo : compo + 1, :] for compo in range(3)]

    total = force[0:3, :] + force[3:6, :] + force[6:9, :]
    torque = None
    centre = split(centres)
    for source in range(3):
        lever = [sites[3 * source + compo : 3 * source + compo + 1, :] - centre[compo] for compo in range(3)]
        push = [force[3 * source + compo : 3 * source + compo + 1, :] for compo in range(3)]
        turn = cross(lever, push)
        torque = turn if torque is None else [old + new for old, new in zip(torque, turn)]
    moving = velocity[...] + STEP_DT * total / WATER_MASS
    velocity_new[...] = moving
    centres_new[...] = centres[...] + STEP_DT * moving
    spin = [angmom[compo : compo + 1, :] + STEP_DT * torque[compo] for compo in range(3)]
    for compo in range(3):
        angmom_new[compo : compo + 1, :] = spin[compo]
    omega = [value * (1.0 / INERTIA) for value in spin]
    scalar = quat[0:1, :]
    vector = [quat[compo + 1 : compo + 2, :] for compo in range(3)]
    delta = [-(omega[0] * vector[0] + omega[1] * vector[1] + omega[2] * vector[2])]
    turned = cross(omega, vector)
    delta = delta + [scalar * omega[compo] + turned[compo] for compo in range(3)]
    moved = [old + 0.5 * STEP_DT * new for old, new in zip([scalar] + vector, delta)]
    length = jnp.sqrt(moved[0] * moved[0] + moved[1] * moved[1] + moved[2] * moved[2] + moved[3] * moved[3])
    for place in range(4):
        orient_new[place : place + 1, :] = moved[place] / length


def product_kernel(rows_n, hist_rows, block_rows, message, *refs):
    dens, small = refs[0], refs[1 : 1 + rows_n]
    out, panel = refs[1 + rows_n :]
    rows, cols = out.shape
    rows_b, cols_b = rows // BLOCK, cols // BLOCK
    here_row, here_col = position()
    for step in range(rows_n):
        other = here_row ^ step
        base = (here_col ^ (other * rows // cols)) * cols + lax.rem(other * rows, cols)
        flag = pattern_flags(message, hist_rows + step * block_rows + 3 * rows_b + here_col)
        for row in range(rows_b):
            block = small[step][row * BLOCK : (row + 1) * BLOCK, :]
            start = pl.multiple_of(base + row * BLOCK, BLOCK)
            for col in range(cols_b):
                panel[pl.ds(start, BLOCK), at(col)] = block * flag(row * cols_b + col)
    for row in range(rows_b):
        lines = slice(row * BLOCK, (row + 1) * BLOCK)
        own = UNIT * COUPLE * message[pl.ds(here_row * rows_b + row, 1), :]
        across = jnp.transpose(jnp.broadcast_to(own, (BLOCK, BLOCK)))
        value = contract(dens[lines, :], panel[...], ((1,), (0,)))
        for col in range(cols_b):
            pot = UNIT * COUPLE * message[pl.ds(here_col * cols_b + col, 1), :]
            sums = (across + pot) * dens[lines, at(col)].astype(F32)
            out[lines, at(col)] = (value[:, at(col)] + sums).astype(BF16)


def tie_kernel(first, second, out):
    pass


VMEM = pl.BlockSpec(memory_space=pltpu.VMEM)
SMEM = pl.BlockSpec(memory_space=pltpu.SMEM)


def fetching(kernel, places, *refs):
    refs, semaphore = list(refs[:-1]), refs[-1]
    held = refs[len(refs) - len(places) :]
    copies = [pltpu.make_async_copy(refs[at_], held[n], semaphore.at[n]) for n, at_ in enumerate(places)]
    for copy in copies:
        copy.start()
    for copy in copies:
        copy.wait()
    for n, at_ in enumerate(places):
        refs[at_] = held[n]
    kernel(*refs[: len(refs) - len(places)])


def call(
    kernel, name, outs, operands, scalars=0, scratch=(), cost=(0, 0), whole=VMEM, fetch=(), limit=48 << 20, **more
):
    in_specs = [SMEM] * scalars + [whole] * (len(operands) - scalars)
    scratch = list(scratch)
    if fetch:
        for place in fetch:
            memory = pltpu.SMEM if place < scalars else pltpu.VMEM
            scratch.append(memory(operands[place].shape, operands[place].dtype))
            in_specs[place] = pl.BlockSpec(memory_space=pltpu.HBM)
        scratch.append(pltpu.SemaphoreType.DMA((len(fetch),)))
        kernel = functools.partial(fetching, kernel, tuple(fetch))
    return pl.pallas_call(
        kernel,
        out_shape=[jax.ShapeDtypeStruct(shape, dtype) for shape, dtype in outs],
        in_specs=in_specs,
        out_specs=[whole] * len(outs),
        scratch_shapes=scratch,
        compiler_params=pltpu.CompilerParams(vmem_limit_bytes=limit),
        cost_estimate=pl.CostEstimate(flops=cost[0], bytes_accessed=cost[1], transcendentals=0),
        name=name,
        **more,
    )(*operands)


def doublings(count):
    step = 1
    while step < count:
        yield step
        step = 2 * step


def shards(
    density,
    margin,
    pattern_d,
    pattern_s,
    dipole,
    owner,
    centres,
    angles,
    velocity,
    angmom,
    halo_list,
    neighbours,
):
    rows, cols = density.shape
    rows_b, cols_b = pattern_d.shape
    rows_n = lax.axis_size("row")
    across = ("col", "sub")
    ways = lax.axis_size("col") * lax.axis_size("sub")
    hist_rows = rows * rows_n // LANES
    waters, listed = centres.shape[1], halo_list.shape[1]
    block_rows = round8(3 * rows_b + ways)
    halo_rows = round8(18 * (listed // LANES))
    summed = hist_rows + rows_n * block_rows
    field_rows = round8(3 * rows_b)
    moment_rows = round8(3 * cols_b)

    def swap(value, axis, count, step):
        return lax.ppermute(value, axis, [(i, i ^ step) for i in range(count)])

    def tie(value, later):
        (value,) = call(
            tie_kernel,
            "tie",
            [(value.shape, value.dtype)],
            [value, later],
            whole=pl.BlockSpec(memory_space=pl.ANY),
            input_output_aliases={0: 0},
        )
        return value

    def merge(first, second, count):
        total = 2 * first.shape[0] - count
        (out,) = call(functools.partial(merge_kernel, count), "merge", [((total, LANES), F32)], [first, second])
        return out

    def send(value, axis, count):
        held = [value] + [None] * (count - 1)
        for step in doublings(count):
            held[step] = swap(value, axis, count, step)
        return held

    def relay(held, axis, count, later):
        for step in range(1, count):
            lowest = step & -step
            if step != lowest:
                if (step - lowest) & (step - lowest - 1) == 0:
                    held[step - lowest] = tie(held[step - lowest], later)
                held[step] = swap(held[step - lowest], axis, count, lowest)
        return held

    dens_all = send(density, across, ways)
    message, small, again, sites, quat, moments = call(
        functools.partial(open_kernel, ways, hist_rows),
        "open",
        [
            ((hist_rows + block_rows + halo_rows, LANES), F32),
            ((rows, BLOCK), BF16),
            ((rows, BLOCK), BF16),
            ((16, waters), F32),
            ((4, waters), F32),
            ((moment_rows, LANES), F32),
        ],
        [pattern_d, pattern_s, margin, dipole, owner, centres, angles, halo_list],
        scalars=2,
        cost=(10**6, 12 * 10**6),
        fetch=range(8),
        limit=60 << 20,
    )
    small_all = [small] + [None] * (rows_n - 1)
    small_all[1] = swap(small, "row", rows_n, 1)
    steps = list(doublings(rows_n))
    for step in steps[:-1]:
        message = merge(message, swap(message, "row", rows_n, step), hist_rows)
    message, halos = call(
        functools.partial(turn_kernel, hist_rows, block_rows, halo_rows),
        "turn",
        [((summed + moment_rows, LANES), F32), ((rows_n * halo_rows, LANES), F32)],
        [message, swap(message, "row", rows_n, steps[-1]), moments],
    )
    dens_all = relay(dens_all, across, ways, message)
    for step in doublings(ways):
        message = merge(message, swap(message, across, ways, step), summed)
        if step == 1:
            later = tie(again, message)
            for further in steps[1:]:
                small_all[further] = swap(later, "row", rows_n, further)
    field, masked = call(
        functools.partial(field_kernel, ways, hist_rows, block_rows, summed),
        "field",
        [((field_rows, LANES), F32), ((rows, ways * cols), BF16)],
        [message] + dens_all,
        scratch=[pltpu.VMEM((8, cols), F32)],
        cost=(10**6, 5 * 10**6),
    )
    tiles = (waters + 2 * listed) // LANES
    (pair,) = call(
        functools.partial(pair_kernel, rows_n),
        "pair_forces",
        [((9, waters), F32)],
        [sites, halos, neighbours],
        scratch=[pltpu.VMEM((5, tiles, 8, LANES), jnp.int32)],
        cost=(10**6, 15 * 10**6),
    )
    for step in doublings(rows_n):
        field = merge(field, swap(field, "row", rows_n, step), 0)
        if step == 1:
            small_all = relay(small_all, "row", rows_n, field)
    (qm_out,) = call(
        functools.partial(product_kernel, rows_n, hist_rows, block_rows),
        "product",
        [((rows, cols), BF16)],
        [message, masked] + small_all,
        scratch=[pltpu.VMEM((rows * rows_n, cols), BF16)],
        cost=(10**6, 15 * 10**6),
    )
    centres_new, velocity_new, angmom_new, orient_new = call(
        functools.partial(advance_kernel, rows_n, rows_b),
        "advance",
        [((3, waters), F32), ((3, waters), F32), ((3, waters), F32), ((4, waters), F32)],
        [field, owner, sites, quat, pair, centres, velocity, angmom],
        scratch=[pltpu.VMEM((16, waters), F32), pltpu.VMEM((8 * hist_rows, LANES), F32)],
        cost=(10**6, 6 * 10**6),
    )
    return (qm_out, centres_new, velocity_new, angmom_new, orient_new)


def solution(mesh):
    square = P(("groups", "row"), ("col", "sub"))
    spread = P(None, ("groups", "row", "col", "sub"))
    return jax.shard_map(
        shards,
        mesh=mesh,
        in_specs=(square,) * 4 + (P(None, ("groups", "col", "sub")),) + (spread,) * 7,
        out_specs=(square,) + (spread,) * 4,
        check_vma=False,
    )
```

```python
import functools

import jax
import jax.numpy as jnp
from jax import lax
from jax.experimental import pallas as pl
from jax.experimental.pallas import tpu as pltpu
from jax.sharding import PartitionSpec as P

BLOCK = 128
LANES = 128

CHARGE = (-0.834, 0.417, 0.417)
UNIT = 0.417
MULTIPLE = (-2.0, 1.0, 1.0)
OFFSET = ((0.0, 0.0, -0.12), (0.76, 0.0, 0.47), (-0.76, 0.0, 0.47))
COUPLE = 0.1
STEP_DT = 0.5
WATER_MASS = 1.0
INERTIA = 0.5
SOFTEN = 1.0

SHIFT = 1.0
SCALE = 65535.0 / 5.0

F32 = jnp.float32
BF16 = jnp.bfloat16

SIN_TERMS = (-1 / 6, 1 / 120, -1 / 5040, 1 / 362880, -1 / 39916800, 1 / 6227020800)
COS_TERMS = (-1 / 2, 1 / 24, -1 / 720, 1 / 40320, -1 / 3628800, 1 / 479001600, -1 / 87178291200)


def at(tile):
    return slice(tile * LANES, (tile + 1) * LANES)


def position():
    return lax.axis_index("row"), lax.axis_index(("col", "sub"))


def pick(table, index):
    return jnp.take_along_axis(table, index, axis=1, mode="promise_in_bounds")


def contract(left, right, dims):
    return lax.dot_general(left, right, (dims, ((), ())), preferred_element_type=F32)


def series(square, terms):
    total = jnp.full_like(square, terms[-1])
    for term in terms[-2::-1]:
        total = total * square + term
    return total * square + 1.0


def line_of(row, comp):
    return 3 * row + comp


def round8(count):
    return -(-count // 8) * 8


def open_kernel(
    ways,
    hist_rows,
    pat_d,
    pat_s,
    marg,
    dip,
    owner,
    centres,
    angles,
    halo,
    message,
    small,
    again,
    sites,
    quat,
):
    rows_b, cols_b = pat_d.shape
    waters = owner.shape[1]
    here_col = position()[1]
    message[...] = jnp.zeros(message.shape, F32)
    lane = lax.broadcasted_iota(jnp.int32, (1, LANES), 1)
    patterns = jnp.zeros((1, LANES), F32)
    for row in range(rows_b):
        chosen = jnp.int32(0)
        lines = slice(row * BLOCK, (row + 1) * BLOCK)
        for col in range(cols_b):
            chosen = chosen + col * pat_s[row, col]
            line = row * cols_b + col
            patterns = jnp.where(lane == line, pat_s[row, col].astype(F32), patterns)
            patterns = jnp.where(lane == rows_b * cols_b + line, pat_d[row, col].astype(F32), patterns)
        span = pl.ds(pl.multiple_of(chosen * BLOCK, BLOCK), BLOCK)
        block = marg[lines, span]
        for copy in (small, again):
            copy[lines, :] = block
        product = contract(dip[:, span], block, ((1,), (1,)))
        place = hist_rows + line_of(row, 0)
        message[place : place + 3, :] = product
    message[pl.ds(hist_rows + 3 * rows_b + here_col, 1), :] = patterns
    total = jnp.zeros((hist_rows, LANES), F32)
    for source in range(3):
        line = owner[source : source + 1, :]
        high = lax.broadcasted_iota(jnp.int32, (hist_rows, waters), 0) == (line >> 7)
        low = lax.broadcasted_iota(jnp.int32, (LANES, waters), 0) == (line & 127)
        total = total + contract(
            jnp.where(high, MULTIPLE[source], 0.0).astype(BF16),
            jnp.where(low, 1.0, 0.0).astype(BF16),
            ((1,), (1,)),
        )
    message[0:hist_rows, :] = total
    halo_at = hist_rows + round8(3 * rows_b + ways)
    water_sites(centres, angles, halo, sites, quat, message.at[halo_at:, :])


def water_sites(centres, angles, halo, sites, quat, listed):
    half_angle = 0.5 * angles[...]
    square = half_angle * half_angle
    sine = half_angle * series(square, SIN_TERMS)
    cosine = series(square, COS_TERMS)
    sin_r, sin_p, sin_y = sine[0:1], sine[1:2], sine[2:3]
    cos_r, cos_p, cos_y = cosine[0:1], cosine[1:2], cosine[2:3]
    comp_w = cos_r * cos_p * cos_y + sin_r * sin_p * sin_y
    comp_x = sin_r * cos_p * cos_y - cos_r * sin_p * sin_y
    comp_y = cos_r * sin_p * cos_y + sin_r * cos_p * sin_y
    comp_z = cos_r * cos_p * sin_y - sin_r * sin_p * cos_y
    for place, comp in enumerate((comp_w, comp_x, comp_y, comp_z)):
        quat[place : place + 1, :] = comp
    first = (
        1.0 - 2.0 * (comp_y * comp_y + comp_z * comp_z),
        2.0 * (comp_x * comp_y + comp_w * comp_z),
        2.0 * (comp_x * comp_z - comp_w * comp_y),
    )
    third = (
        2.0 * (comp_x * comp_z + comp_w * comp_y),
        2.0 * (comp_y * comp_z - comp_w * comp_x),
        1.0 - 2.0 * (comp_x * comp_x + comp_y * comp_y),
    )
    sites[...] = jnp.zeros(sites.shape, F32)
    for source in range(3):
        for compo in range(3):
            place = 3 * source + compo
            position = centres[compo : compo + 1, :] + third[compo] * OFFSET[source][2]
            if OFFSET[source][0] != 0.0:
                position = position + first[compo] * OFFSET[source][0]
            sites[place : place + 1, :] = position
    waters, tiles = centres.shape[1], halo.shape[1] // LANES
    for which in range(2):
        for tile in range(tiles):
            index = jnp.broadcast_to(halo[which : which + 1, at(tile)], (8, LANES))
            low, high = index & 127, index >> 7
            for part in range(2):
                found = jnp.zeros((8, LANES), F32)
                for source in range(waters // LANES):
                    value = pick(sites[8 * part : 8 * part + 8, at(source)], low)
                    found = jnp.where(high == source, value, found)
                for comp in range(8 * part, min(8 * part + 8, 9)):
                    place = (which * 9 + comp) * tiles + tile
                    listed[place : place + 1, :] = found[comp - 8 * part : comp - 8 * part + 1]


def merge_kernel(summed, first, second, *refs):
    out = refs[-1]
    if summed > 0:
        out[0:summed, :] = first[0:summed, :] + second[0:summed, :]
    count = first.shape[0] - summed
    if count > 0:
        out[summed : summed + count, :] = first[summed:, :]
        out[summed + count :, :] = second[summed:, :]


def turn_kernel(summed, block_rows, halo_rows, first, second, moments, done, out, halos):
    out[0:summed, :] = first[0:summed, :] + second[0:summed, :]
    count = (first.shape[0] - summed) // (block_rows + halo_rows)
    for number, ref in enumerate((first, second)):
        for block in range(count):
            start = summed + block * (block_rows + halo_rows)
            place = number * count + block
            out[summed + place * block_rows : summed + (place + 1) * block_rows, :] = ref[
                start : start + block_rows, :
            ]
            halos[place * halo_rows : (place + 1) * halo_rows, :] = ref[
                start + block_rows : start + block_rows + halo_rows, :
            ]
    out[summed + 2 * count * block_rows :, :] = moments[...]


def store_words(table, tile, lines):
    fixed = [(line * SCALE + (SHIFT * SCALE + 0.5)).astype(jnp.int32) for line in lines]
    for word in range(5):
        value = fixed[2 * word]
        if word < 4:
            value = value | ((fixed[2 * word + 1] - 32768) << 16)
        table[word, tile] = jnp.broadcast_to(value, (8, LANES))


def gather_words(table, base, index, found):
    low = [value & 127 for value in index]
    high = [value >> 7 for value in index]
    for source in range(table.shape[1]):
        here = [value == base + source for value in high]
        for word in range(5):
            line = table[word, source]
            for part in range(len(index)):
                value = pick(line, low[part])
                old = found[word][part]
                found[word][part] = value if old is None else jnp.where(here[part], value, old)
    return found


def prepare_kernel(sites, dip, message, table, moments, held):
    held[...] = message[...]
    moments[...] = jnp.zeros(moments.shape, F32)
    for col in range(dip.shape[1] // BLOCK):
        moments[3 * col : 3 * col + 3, :] = dip[:, at(col)].astype(F32)
    for tile in range(sites.shape[1] // LANES):
        store_words(table, tile, [sites[word : word + 1, at(tile)] for word in range(9)])


def own_kernel(table, neighbours, out):
    slots, waters = neighbours.shape

    def one_tile(tile, carry):
        span = pl.ds(pl.multiple_of(tile * LANES, LANES), LANES)
        for pair in range(slots // 16):
            rows = [slice(16 * pair + 8 * part, 16 * pair + 8 * part + 8) for part in range(2)]
            found = gather_words(table, 0, [neighbours[row, span] for row in rows], [[None, None] for _ in range(5)])
            for word in range(5):
                for part in range(2):
                    start = word * slots + 16 * pair + 8 * part
                    out[start : start + 8, span] = found[word][part]
        return carry

    lax.fori_loop(0, waters // LANES, one_tile, 0)


def pair_kernel(rows_n, sites, own_words, halos, neighbours, force, table):
    waters, slots = sites.shape[1], neighbours.shape[0]
    depth = halos.shape[0] // rows_n
    own_tiles = waters // LANES
    halo_tiles = table.shape[1] // 2
    here_row = position()[0]
    for which in range(2):
        other = lax.rem(here_row + (rows_n - 1, 1)[which], rows_n)
        start = pl.multiple_of((here_row ^ other) * depth, 8)
        lines = halos[pl.ds(start, depth), :]
        for tile in range(halo_tiles):
            places = [(which * 9 + word) * halo_tiles + tile for word in range(9)]
            store_words(table, which * halo_tiles + tile, [lines[place : place + 1] for place in places])

    def one_tile(tile, carry):
        span = pl.ds(pl.multiple_of(tile * LANES, LANES), LANES)
        lines = sites[:, span]
        own = []
        for word in range(9):
            line = jnp.broadcast_to(lines[word : word + 1] * SCALE + SHIFT * SCALE, (8, LANES))
            own.append((line, line - 32768.0))
        near = [jnp.zeros((8, LANES), F32) for _ in range(9)]
        far = [jnp.zeros((8, LANES), F32) for _ in range(9)]
        for pair in range(slots // 16):
            starts = [16 * pair + 8 * part for part in range(2)]
            found = [
                [own_words[word * slots + start : word * slots + start + 8, span] for start in starts]
                for word in range(5)
            ]
            index = [neighbours[start : start + 8, span] for start in starts]
            found = gather_words(table, own_tiles, index, found)
            for part in range(2):
                places = []
                for word in range(9):
                    value = found[word // 2][part]
                    if word == 8:
                        places.append(value.astype(F32))
                    elif word % 2 == 0:
                        places.append((value & 65535).astype(F32))
                    else:
                        places.append((value >> 16).astype(F32))
                for source in range(3):
                    for target in range(3):
                        gap = []
                        for compo in range(3):
                            mine, other = 3 * source + compo, 3 * target + compo
                            gap.append(own[mine][other % 2] - places[other])
                        root = lax.rsqrt(
                            gap[0] * gap[0] + gap[1] * gap[1] + gap[2] * gap[2] + SOFTEN * SCALE * SCALE
                        )
                        weight = root * root * root
                        sums = near if target == 0 else far
                        for compo in range(3):
                            sums[3 * source + compo] = sums[3 * source + compo] + gap[compo] * weight
        for place in range(9):
            factor = CHARGE[place // 3] * UNIT * SCALE * SCALE
            total = factor * (far[place] - 2.0 * near[place])
            force[place : place + 1, span] = jnp.sum(total, axis=0, keepdims=True)
        return carry

    lax.fori_loop(0, own_tiles, one_tile, 0)


def pattern_flags(message, place):
    line = jnp.broadcast_to(message[pl.ds(place, 1), :], (8, LANES))
    return lambda block: pick(line, jnp.full((8, LANES), block, jnp.int32))[0:1].astype(BF16)


def field_kernel(ways, hist_rows, block_rows, summed, message, *refs):
    dens, out, masked, lines = refs[:ways], refs[ways], refs[ways + 1], refs[ways + 2]
    rows, cols = dens[0].shape
    rows_b, cols_b = rows // BLOCK, cols // BLOCK
    depth = (message.shape[0] - summed) // ways
    here_row, here_col = position()
    result = jnp.zeros((16, rows), F32)
    lines[...] = jnp.zeros(lines.shape, F32)
    for step in range(ways):
        device = here_col ^ step
        flag = pattern_flags(message, hist_rows + 3 * rows_b + device)
        for col in range(cols_b):
            other = device * (cols_b // rows_b) + col // rows_b
            place = hist_rows + (here_row ^ other) * block_rows + line_of(col % rows_b, 0)
            start = summed + step * depth + 3 * col
            moment = message[start : start + 3, :]
            pot = UNIT * COUPLE * message[pl.ds(device * cols_b + col, 1), :]
            for comp in range(3):
                product = message[pl.ds(place + comp, 1), :]
                lines[comp : comp + 1, at(col)] = product + pot * moment[comp : comp + 1]
            lines[3:6, at(col)] = moment
            for row in range(rows_b):
                spot = slice(row * BLOCK, (row + 1) * BLOCK)
                target = slice(step * cols + col * BLOCK, step * cols + (col + 1) * BLOCK)
                masked[spot, target] = dens[step][spot, at(col)] * flag(rows_b * cols_b + row * cols_b + col)
        whole = lines[...]
        first = whole.astype(BF16).astype(F32)
        both = jnp.concatenate([first, whole - first], axis=0).astype(BF16)
        result = result + contract(both, masked[:, step * cols : (step + 1) * cols], ((1,), (1,)))
    total = result[0:8] + result[8:16]
    out[...] = jnp.zeros(out.shape, F32)
    for row in range(rows_b):
        pot = UNIT * COUPLE * message[pl.ds(here_row * rows_b + row, 1), :]
        start = line_of(row, 0)
        out[start : start + 3, :] = total[0:3, at(row)] + pot * total[3:6, at(row)]


def advance_kernel(
    rows_n,
    rows_b,
    fields,
    owner,
    sites,
    quat,
    pair,
    centres,
    velocity,
    angmom,
    centres_new,
    velocity_new,
    angmom_new,
    orient_new,
    force,
    table,
):
    waters = owner.shape[1]
    depth = fields.shape[0] // rows_n
    here_row = position()[0]
    table[...] = jnp.zeros(table.shape, F32)
    for step in range(rows_n):
        for row in range(rows_b):
            start = step * depth + line_of(row, 0)
            place = 8 * (step * rows_b + row)
            table[place : place + 3, :] = fields[start : start + 3, :]
    for tile in range(waters // LANES):
        for source in range(3):
            index = jnp.broadcast_to(owner[source : source + 1, at(tile)], (8, LANES))
            low, high = index & 127, index >> 7
            found = jnp.zeros((8, LANES), F32)
            for step in range(rows_n):
                base = (here_row ^ step) * rows_b
                for row in range(rows_b):
                    place = 8 * (step * rows_b + row)
                    value = pick(table[place : place + 8, :], low)
                    found = jnp.where(high == base + row, value, found)
            lines = slice(3 * source, 3 * source + 3)
            force[lines, at(tile)] = pair[lines, at(tile)] + CHARGE[source] * found[0:3]

    def cross(left, right):
        return [
            left[1] * right[2] - left[2] * right[1],
            left[2] * right[0] - left[0] * right[2],
            left[0] * right[1] - left[1] * right[0],
        ]

    def split(array):
        return [array[compo : compo + 1, :] for compo in range(3)]

    total = force[0:3, :] + force[3:6, :] + force[6:9, :]
    torque = None
    centre = split(centres)
    for source in range(3):
        lever = [sites[3 * source + compo : 3 * source + compo + 1, :] - centre[compo] for compo in range(3)]
        push = [force[3 * source + compo : 3 * source + compo + 1, :] for compo in range(3)]
        turn = cross(lever, push)
        torque = turn if torque is None else [old + new for old, new in zip(torque, turn)]
    moving = velocity[...] + STEP_DT * total / WATER_MASS
    velocity_new[...] = moving
    centres_new[...] = centres[...] + STEP_DT * moving
    spin = [angmom[compo : compo + 1, :] + STEP_DT * torque[compo] for compo in range(3)]
    for compo in range(3):
        angmom_new[compo : compo + 1, :] = spin[compo]
    omega = [value * (1.0 / INERTIA) for value in spin]
    scalar = quat[0:1, :]
    vector = [quat[compo + 1 : compo + 2, :] for compo in range(3)]
    delta = [-(omega[0] * vector[0] + omega[1] * vector[1] + omega[2] * vector[2])]
    turned = cross(omega, vector)
    delta = delta + [scalar * omega[compo] + turned[compo] for compo in range(3)]
    moved = [old + 0.5 * STEP_DT * new for old, new in zip([scalar] + vector, delta)]
    length = jnp.sqrt(moved[0] * moved[0] + moved[1] * moved[1] + moved[2] * moved[2] + moved[3] * moved[3])
    for place in range(4):
        orient_new[place : place + 1, :] = moved[place] / length


def product_kernel(rows_n, hist_rows, block_rows, message, *refs):
    dens, small = refs[0], refs[1 : 1 + rows_n]
    out, panel = refs[1 + rows_n :]
    rows, cols = out.shape
    rows_b, cols_b = rows // BLOCK, cols // BLOCK
    here_row, here_col = position()
    for step in range(rows_n):
        other = here_row ^ step
        base = (here_col ^ (other * rows // cols)) * cols + lax.rem(other * rows, cols)
        flag = pattern_flags(message, hist_rows + step * block_rows + 3 * rows_b + here_col)
        for row in range(rows_b):
            block = small[step][row * BLOCK : (row + 1) * BLOCK, :]
            start = pl.multiple_of(base + row * BLOCK, BLOCK)
            for col in range(cols_b):
                panel[pl.ds(start, BLOCK), at(col)] = block * flag(row * cols_b + col)

    def one_row(row, carry):
        lines = pl.ds(pl.multiple_of(row * BLOCK, BLOCK), BLOCK)
        own = UNIT * COUPLE * message[pl.ds(here_row * rows_b + row, 1), :]
        across = jnp.transpose(jnp.broadcast_to(own, (BLOCK, BLOCK)))
        value = contract(dens[lines, :], panel[...], ((1,), (0,)))
        for col in range(cols_b):
            pot = UNIT * COUPLE * message[pl.ds(here_col * cols_b + col, 1), :]
            sums = (across + pot) * dens[lines, at(col)].astype(F32)
            out[lines, at(col)] = (value[:, at(col)] + sums).astype(BF16)
        return carry

    lax.fori_loop(0, rows_b, one_row, 0)


def tie_kernel(first, second, out):
    pass


VMEM = pl.BlockSpec(memory_space=pltpu.VMEM)
SMEM = pl.BlockSpec(memory_space=pltpu.SMEM)


def fetching(kernel, places, *refs):
    refs, semaphore = list(refs[:-1]), refs[-1]
    held = refs[len(refs) - len(places) :]
    copies = [pltpu.make_async_copy(refs[at_], held[n], semaphore.at[n]) for n, at_ in enumerate(places)]
    for copy in copies:
        copy.start()
    for copy in copies:
        copy.wait()
    for n, at_ in enumerate(places):
        refs[at_] = held[n]
    kernel(*refs[: len(refs) - len(places)])


def call(
    kernel, name, outs, operands, scalars=0, scratch=(), cost=(0, 0), whole=VMEM, fetch=(), unread=(), limit=48 << 20, **more
):
    in_specs = [SMEM] * scalars + [whole] * (len(operands) - scalars)
    scratch = list(scratch)
    for place in unread:
        in_specs[place] = pl.BlockSpec(memory_space=pl.ANY)
    if fetch:
        for place in fetch:
            memory = pltpu.SMEM if place < scalars else pltpu.VMEM
            scratch.append(memory(operands[place].shape, operands[place].dtype))
            in_specs[place] = pl.BlockSpec(memory_space=pltpu.HBM)
        scratch.append(pltpu.SemaphoreType.DMA((len(fetch),)))
        kernel = functools.partial(fetching, kernel, tuple(fetch))
    return pl.pallas_call(
        kernel,
        out_shape=[jax.ShapeDtypeStruct(shape, dtype) for shape, dtype in outs],
        in_specs=in_specs,
        out_specs=[whole] * len(outs),
        scratch_shapes=scratch,
        compiler_params=pltpu.CompilerParams(vmem_limit_bytes=limit),
        cost_estimate=pl.CostEstimate(flops=cost[0], bytes_accessed=cost[1], transcendentals=0),
        name=name,
        **more,
    )(*operands)


def doublings(count):
    step = 1
    while step < count:
        yield step
        step = 2 * step


def shards(
    density,
    margin,
    pattern_d,
    pattern_s,
    dipole,
    owner,
    centres,
    angles,
    velocity,
    angmom,
    halo_list,
    neighbours,
):
    rows, cols = density.shape
    rows_b, cols_b = pattern_d.shape
    rows_n = lax.axis_size("row")
    across = ("col", "sub")
    ways = lax.axis_size("col") * lax.axis_size("sub")
    hist_rows = rows * rows_n // LANES
    waters, listed, slots = centres.shape[1], halo_list.shape[1], neighbours.shape[0]
    block_rows = round8(3 * rows_b + ways)
    halo_rows = round8(18 * (listed // LANES))
    summed = hist_rows + rows_n * block_rows
    field_rows = round8(3 * rows_b)
    moment_rows = round8(3 * cols_b)

    def swap(value, axis, count, step):
        return lax.ppermute(value, axis, [(i, i ^ step) for i in range(count)])

    def tie(value, later):
        (value,) = call(
            tie_kernel,
            "tie",
            [(value.shape, value.dtype)],
            [value, later],
            whole=pl.BlockSpec(memory_space=pl.ANY),
            input_output_aliases={0: 0},
        )
        return value

    def merge(first, second, count, done=None):
        total = 2 * first.shape[0] - count
        operands = [first, second] + ([] if done is None else [done])
        (out,) = call(
            functools.partial(merge_kernel, count),
            "merge",
            [((total, LANES), F32)],
            operands,
            unread=range(2, len(operands)),
        )
        return out

    def send(value, axis, count):
        held = [value] + [None] * (count - 1)
        for step in doublings(count):
            held[step] = swap(value, axis, count, step)
        return held

    def relay(held, axis, count, later):
        for step in range(1, count):
            lowest = step & -step
            if step != lowest:
                if (step - lowest) & (step - lowest - 1) == 0:
                    held[step - lowest] = tie(held[step - lowest], later)
                held[step] = swap(held[step - lowest], axis, count, lowest)
        return held

    dens_all = send(density, across, ways)
    message, small, again, sites, quat = call(
        functools.partial(open_kernel, ways, hist_rows),
        "open",
        [
            ((hist_rows + block_rows + halo_rows, LANES), F32),
            ((rows, BLOCK), BF16),
            ((rows, BLOCK), BF16),
            ((16, waters), F32),
            ((4, waters), F32),
        ],
        [pattern_d, pattern_s, margin, dipole, owner, centres, angles, halo_list],
        scalars=2,
        cost=(10**6, 12 * 10**6),
        fetch=range(8),
        limit=60 << 20,
    )
    table, moments, held = call(
        prepare_kernel,
        "prepare",
        [
            ((5, waters // LANES, 8, LANES), jnp.int32),
            ((moment_rows, LANES), F32),
            (message.shape, F32),
        ],
        [sites, dipole, message],
    )
    (found,) = call(
        own_kernel,
        "own_gathers",
        [((5 * slots, waters), jnp.int32)],
        [table, neighbours],
        cost=(10**6, 6 * 10**6),
    )
    small_all = [small] + [None] * (rows_n - 1)
    small_all[1] = swap(small, "row", rows_n, 1)
    steps = list(doublings(rows_n))
    for step in steps[:-1]:
        message = merge(held, swap(message, "row", rows_n, step), hist_rows, moments)
        held = message
    later = tie(again, message)
    message, halos = call(
        functools.partial(turn_kernel, hist_rows, block_rows, halo_rows),
        "turn",
        [((summed + moment_rows, LANES), F32), ((rows_n * halo_rows, LANES), F32)],
        [message, swap(message, "row", rows_n, steps[-1]), moments, found],
        unread=(3,),
    )
    for step in steps[1:]:
        small_all[step] = swap(later, "row", rows_n, step)
    dens_all = relay(dens_all, across, ways, message)
    for step in doublings(ways):
        message = merge(message, swap(message, across, ways, step), summed)
    field, masked = call(
        functools.partial(field_kernel, ways, hist_rows, block_rows, summed),
        "field",
        [((field_rows, LANES), F32), ((rows, ways * cols), BF16)],
        [message] + dens_all,
        scratch=[pltpu.VMEM((8, cols), F32)],
        cost=(10**6, 5 * 10**6),
    )
    (pair,) = call(
        functools.partial(pair_kernel, rows_n),
        "pair_forces",
        [((9, waters), F32)],
        [sites, found, halos, neighbours],
        scratch=[pltpu.VMEM((5, 2 * listed // LANES, 8, LANES), jnp.int32)],
        cost=(10**6, 15 * 10**6),
    )
    for step in doublings(rows_n):
        field = merge(field, swap(field, "row", rows_n, step), 0)
        if step == 1:
            small_all = relay(small_all, "row", rows_n, field)
    (qm_out,) = call(
        functools.partial(product_kernel, rows_n, hist_rows, block_rows),
        "product",
        [((rows, cols), BF16)],
        [message, masked] + small_all,
        scratch=[pltpu.VMEM((rows * rows_n, cols), BF16)],
        cost=(10**6, 15 * 10**6),
    )
    centres_new, velocity_new, angmom_new, orient_new = call(
        functools.partial(advance_kernel, rows_n, rows_b),
        "advance",
        [((3, waters), F32), ((3, waters), F32), ((3, waters), F32), ((4, waters), F32)],
        [field, owner, sites, quat, pair, centres, velocity, angmom],
        scratch=[pltpu.VMEM((16, waters), F32), pltpu.VMEM((8 * hist_rows, LANES), F32)],
        cost=(10**6, 6 * 10**6),
    )
    return (qm_out, centres_new, velocity_new, angmom_new, orient_new)


def solution(mesh):
    square = P(("groups", "row"), ("col", "sub"))
    spread = P(None, ("groups", "row", "col", "sub"))
    return jax.shard_map(
        shards,
        mesh=mesh,
        in_specs=(square,) * 4 + (P(None, ("groups", "col", "sub")),) + (spread,) * 7,
        out_specs=(square,) + (spread,) * 4,
        check_vma=False,
    )
```

```python
import functools

import jax
import jax.numpy as jnp
from jax import lax
from jax.experimental import pallas as pl
from jax.experimental.pallas import tpu as pltpu
from jax.sharding import PartitionSpec as P

BLOCK = 128
LANES = 128

CHARGE = (-0.834, 0.417, 0.417)
UNIT = 0.417
MULTIPLE = (-2.0, 1.0, 1.0)
OFFSET = ((0.0, 0.0, -0.12), (0.76, 0.0, 0.47), (-0.76, 0.0, 0.47))
COUPLE = 0.1
STEP_DT = 0.5
WATER_MASS = 1.0
INERTIA = 0.5
SOFTEN = 1.0

SHIFT = 1.0
SCALE = 65535.0 / 5.0

F32 = jnp.float32
BF16 = jnp.bfloat16

SIN_TERMS = (-1 / 6, 1 / 120, -1 / 5040, 1 / 362880, -1 / 39916800, 1 / 6227020800)
COS_TERMS = (-1 / 2, 1 / 24, -1 / 720, 1 / 40320, -1 / 3628800, 1 / 479001600, -1 / 87178291200)


def at(tile):
    return slice(tile * LANES, (tile + 1) * LANES)


def position():
    return lax.axis_index("row"), lax.axis_index(("col", "sub"))


def pick(table, index):
    return jnp.take_along_axis(table, index, axis=1, mode="promise_in_bounds")


def contract(left, right, dims):
    return lax.dot_general(left, right, (dims, ((), ())), preferred_element_type=F32)


def series(square, terms):
    total = jnp.full_like(square, terms[-1])
    for term in terms[-2::-1]:
        total = total * square + term
    return total * square + 1.0


def line_of(row, comp):
    return 3 * row + comp


def round8(count):
    return -(-count // 8) * 8


def open_kernel(
    ways,
    hist_rows,
    pat_d,
    pat_s,
    marg,
    dip,
    owner,
    centres,
    angles,
    halo,
    message,
    small,
    again,
    sites,
    quat,
):
    rows_b, cols_b = pat_d.shape
    waters = owner.shape[1]
    here_col = position()[1]
    message[...] = jnp.zeros(message.shape, F32)
    lane = lax.broadcasted_iota(jnp.int32, (1, LANES), 1)
    patterns = jnp.zeros((1, LANES), F32)
    for row in range(rows_b):
        chosen = jnp.int32(0)
        lines = slice(row * BLOCK, (row + 1) * BLOCK)
        for col in range(cols_b):
            chosen = chosen + col * pat_s[row, col]
            line = row * cols_b + col
            patterns = jnp.where(lane == line, pat_s[row, col].astype(F32), patterns)
            patterns = jnp.where(lane == rows_b * cols_b + line, pat_d[row, col].astype(F32), patterns)
        span = pl.ds(pl.multiple_of(chosen * BLOCK, BLOCK), BLOCK)
        block = marg[lines, span]
        for copy in (small, again):
            copy[lines, :] = block
        product = contract(dip[:, span], block, ((1,), (1,)))
        place = hist_rows + line_of(row, 0)
        message[place : place + 3, :] = product
    message[pl.ds(hist_rows + 3 * rows_b + here_col, 1), :] = patterns
    total = jnp.zeros((hist_rows, LANES), F32)
    for source in range(3):
        line = owner[source : source + 1, :]
        high = lax.broadcasted_iota(jnp.int32, (hist_rows, waters), 0) == (line >> 7)
        low = lax.broadcasted_iota(jnp.int32, (LANES, waters), 0) == (line & 127)
        total = total + contract(
            jnp.where(high, MULTIPLE[source], 0.0).astype(BF16),
            jnp.where(low, 1.0, 0.0).astype(BF16),
            ((1,), (1,)),
        )
    message[0:hist_rows, :] = total
    halo_at = hist_rows + round8(3 * rows_b + ways)
    water_sites(centres, angles, halo, sites, quat, message.at[halo_at:, :])


def water_sites(centres, angles, halo, sites, quat, listed):
    half_angle = 0.5 * angles[...]
    square = half_angle * half_angle
    sine = half_angle * series(square, SIN_TERMS)
    cosine = series(square, COS_TERMS)
    sin_r, sin_p, sin_y = sine[0:1], sine[1:2], sine[2:3]
    cos_r, cos_p, cos_y = cosine[0:1], cosine[1:2], cosine[2:3]
    comp_w = cos_r * cos_p * cos_y + sin_r * sin_p * sin_y
    comp_x = sin_r * cos_p * cos_y - cos_r * sin_p * sin_y
    comp_y = cos_r * sin_p * cos_y + sin_r * cos_p * sin_y
    comp_z = cos_r * cos_p * sin_y - sin_r * sin_p * cos_y
    for place, comp in enumerate((comp_w, comp_x, comp_y, comp_z)):
        quat[place : place + 1, :] = comp
    first = (
        1.0 - 2.0 * (comp_y * comp_y + comp_z * comp_z),
        2.0 * (comp_x * comp_y + comp_w * comp_z),
        2.0 * (comp_x * comp_z - comp_w * comp_y),
    )
    third = (
        2.0 * (comp_x * comp_z + comp_w * comp_y),
        2.0 * (comp_y * comp_z - comp_w * comp_x),
        1.0 - 2.0 * (comp_x * comp_x + comp_y * comp_y),
    )
    sites[...] = jnp.zeros(sites.shape, F32)
    for source in range(3):
        for compo in range(3):
            place = 3 * source + compo
            position = centres[compo : compo + 1, :] + third[compo] * OFFSET[source][2]
            if OFFSET[source][0] != 0.0:
                position = position + first[compo] * OFFSET[source][0]
            sites[place : place + 1, :] = position
    waters, tiles = centres.shape[1], halo.shape[1] // LANES
    for which in range(2):
        for tile in range(tiles):
            index = jnp.broadcast_to(halo[which : which + 1, at(tile)], (8, LANES))
            low, high = index & 127, index >> 7
            for part in range(2):
                found = jnp.zeros((8, LANES), F32)
                for source in range(waters // LANES):
                    value = pick(sites[8 * part : 8 * part + 8, at(source)], low)
                    found = jnp.where(high == source, value, found)
                for comp in range(8 * part, min(8 * part + 8, 9)):
                    place = (which * 9 + comp) * tiles + tile
                    listed[place : place + 1, :] = found[comp - 8 * part : comp - 8 * part + 1]


def merge_kernel(summed, first, second, *refs):
    out = refs[-1]
    if summed > 0:
        out[0:summed, :] = first[0:summed, :] + second[0:summed, :]
    count = first.shape[0] - summed
    if count > 0:
        out[summed : summed + count, :] = first[summed:, :]
        out[summed + count :, :] = second[summed:, :]


def turn_kernel(summed, block_rows, halo_rows, first, second, moments, done, out, halos):
    out[0:summed, :] = first[0:summed, :] + second[0:summed, :]
    count = (first.shape[0] - summed) // (block_rows + halo_rows)
    for number, ref in enumerate((first, second)):
        for block in range(count):
            start = summed + block * (block_rows + halo_rows)
            place = number * count + block
            out[summed + place * block_rows : summed + (place + 1) * block_rows, :] = ref[
                start : start + block_rows, :
            ]
            halos[place * halo_rows : (place + 1) * halo_rows, :] = ref[
                start + block_rows : start + block_rows + halo_rows, :
            ]
    out[summed + 2 * count * block_rows :, :] = moments[...]


def store_words(table, tile, lines):
    fixed = [(line * SCALE + (SHIFT * SCALE + 0.5)).astype(jnp.int32) for line in lines]
    for word in range(5):
        value = fixed[2 * word]
        if word < 4:
            value = value | ((fixed[2 * word + 1] - 32768) << 16)
        table[word, tile] = jnp.broadcast_to(value, (8, LANES))


def gather_words(sources, index, found):
    low = [value & 127 for value in index]
    high = [value >> 7 for value in index]
    for number, table, place in sources:
        here = [value == number for value in high]
        for word in range(5):
            line = table[word, place]
            for part in range(len(index)):
                value = pick(line, low[part])
                old = found[word][part]
                found[word][part] = value if old is None else jnp.where(here[part], value, old)
    return found


def prepare_kernel(sites, dip, message, table, moments, held):
    held[...] = message[...]
    moments[...] = jnp.zeros(moments.shape, F32)
    for col in range(dip.shape[1] // BLOCK):
        moments[3 * col : 3 * col + 3, :] = dip[:, at(col)].astype(F32)
    for tile in range(sites.shape[1] // LANES):
        store_words(table, tile, [sites[word : word + 1, at(tile)] for word in range(9)])


def own_kernel(first, table, neighbours, out):
    slots, waters = neighbours.shape
    sources = [(tile, table, tile) for tile in range(first)]

    def one_tile(tile, carry):
        span = pl.ds(pl.multiple_of(tile * LANES, LANES), LANES)
        for pair in range(slots // 16):
            rows = [slice(16 * pair + 8 * part, 16 * pair + 8 * part + 8) for part in range(2)]
            found = gather_words(sources, [neighbours[row, span] for row in rows], [[None, None] for _ in range(5)])
            for word in range(5):
                for part in range(2):
                    start = word * slots + 16 * pair + 8 * part
                    out[start : start + 8, span] = found[word][part]
        return carry

    lax.fori_loop(0, waters // LANES, one_tile, 0)


def pair_kernel(rows_n, first, sites, own_words, own_table, halos, neighbours, force, table):
    waters, slots = sites.shape[1], neighbours.shape[0]
    depth = halos.shape[0] // rows_n
    own_tiles = waters // LANES
    halo_tiles = table.shape[1] // 2
    here_row = position()[0]
    for which in range(2):
        other = lax.rem(here_row + (rows_n - 1, 1)[which], rows_n)
        start = pl.multiple_of((here_row ^ other) * depth, 8)
        lines = halos[pl.ds(start, depth), :]
        for tile in range(halo_tiles):
            places = [(which * 9 + word) * halo_tiles + tile for word in range(9)]
            store_words(table, which * halo_tiles + tile, [lines[place : place + 1] for place in places])

    sources = [(tile, own_table, tile) for tile in range(first, own_tiles)]
    sources = sources + [(own_tiles + tile, table, tile) for tile in range(2 * halo_tiles)]

    def one_tile(tile, carry):
        span = pl.ds(pl.multiple_of(tile * LANES, LANES), LANES)
        lines = sites[:, span]
        own = []
        for word in range(9):
            line = jnp.broadcast_to(lines[word : word + 1] * SCALE + SHIFT * SCALE, (8, LANES))
            own.append((line, line - 32768.0))
        near = [jnp.zeros((8, LANES), F32) for _ in range(9)]
        far = [jnp.zeros((8, LANES), F32) for _ in range(9)]
        for pair in range(slots // 16):
            starts = [16 * pair + 8 * part for part in range(2)]
            found = [
                [own_words[word * slots + start : word * slots + start + 8, span] for start in starts]
                for word in range(5)
            ]
            index = [neighbours[start : start + 8, span] for start in starts]
            found = gather_words(sources, index, found)
            for part in range(2):
                places = []
                for word in range(9):
                    value = found[word // 2][part]
                    if word == 8:
                        places.append(value.astype(F32))
                    elif word % 2 == 0:
                        places.append((value & 65535).astype(F32))
                    else:
                        places.append((value >> 16).astype(F32))
                for source in range(3):
                    for target in range(3):
                        gap = []
                        for compo in range(3):
                            mine, other = 3 * source + compo, 3 * target + compo
                            gap.append(own[mine][other % 2] - places[other])
                        root = lax.rsqrt(
                            gap[0] * gap[0] + gap[1] * gap[1] + gap[2] * gap[2] + SOFTEN * SCALE * SCALE
                        )
                        weight = root * root * root
                        sums = near if target == 0 else far
                        for compo in range(3):
                            sums[3 * source + compo] = sums[3 * source + compo] + gap[compo] * weight
        for place in range(9):
            factor = CHARGE[place // 3] * UNIT * SCALE * SCALE
            total = factor * (far[place] - 2.0 * near[place])
            force[place : place + 1, span] = jnp.sum(total, axis=0, keepdims=True)
        return carry

    lax.fori_loop(0, own_tiles, one_tile, 0)


def pattern_flags(message, place):
    line = jnp.broadcast_to(message[pl.ds(place, 1), :], (8, LANES))
    return lambda block: pick(line, jnp.full((8, LANES), block, jnp.int32))[0:1].astype(BF16)


def field_kernel(ways, hist_rows, block_rows, summed, message, *refs):
    dens, out, masked, lines = refs[:ways], refs[ways + 1], refs[ways + 2], refs[ways + 3]
    rows, cols = dens[0].shape
    rows_b, cols_b = rows // BLOCK, cols // BLOCK
    depth = (message.shape[0] - summed) // ways
    here_row, here_col = position()
    result = jnp.zeros((16, rows), F32)
    lines[...] = jnp.zeros(lines.shape, F32)
    for step in range(ways):
        device = here_col ^ step
        flag = pattern_flags(message, hist_rows + 3 * rows_b + device)
        for col in range(cols_b):
            other = device * (cols_b // rows_b) + col // rows_b
            place = hist_rows + (here_row ^ other) * block_rows + line_of(col % rows_b, 0)
            start = summed + step * depth + 3 * col
            moment = message[start : start + 3, :]
            pot = UNIT * COUPLE * message[pl.ds(device * cols_b + col, 1), :]
            for comp in range(3):
                product = message[pl.ds(place + comp, 1), :]
                lines[comp : comp + 1, at(col)] = product + pot * moment[comp : comp + 1]
            lines[3:6, at(col)] = moment
            for row in range(rows_b):
                spot = slice(row * BLOCK, (row + 1) * BLOCK)
                target = slice(step * cols + col * BLOCK, step * cols + (col + 1) * BLOCK)
                masked[spot, target] = dens[step][spot, at(col)] * flag(rows_b * cols_b + row * cols_b + col)
        whole = lines[...]
        first = whole.astype(BF16).astype(F32)
        both = jnp.concatenate([first, whole - first], axis=0).astype(BF16)
        result = result + contract(both, masked[:, step * cols : (step + 1) * cols], ((1,), (1,)))
    total = result[0:8] + result[8:16]
    out[...] = jnp.zeros(out.shape, F32)
    for row in range(rows_b):
        pot = UNIT * COUPLE * message[pl.ds(here_row * rows_b + row, 1), :]
        start = line_of(row, 0)
        out[start : start + 3, :] = total[0:3, at(row)] + pot * total[3:6, at(row)]


def advance_kernel(
    rows_n,
    rows_b,
    fields,
    owner,
    sites,
    quat,
    pair,
    centres,
    velocity,
    angmom,
    centres_new,
    velocity_new,
    angmom_new,
    orient_new,
    force,
    table,
):
    waters = owner.shape[1]
    depth = fields.shape[0] // rows_n
    here_row = position()[0]
    table[...] = jnp.zeros(table.shape, F32)
    for step in range(rows_n):
        for row in range(rows_b):
            start = step * depth + line_of(row, 0)
            place = 8 * (step * rows_b + row)
            table[place : place + 3, :] = fields[start : start + 3, :]
    for tile in range(waters // LANES):
        for source in range(3):
            index = jnp.broadcast_to(owner[source : source + 1, at(tile)], (8, LANES))
            low, high = index & 127, index >> 7
            found = jnp.zeros((8, LANES), F32)
            for step in range(rows_n):
                base = (here_row ^ step) * rows_b
                for row in range(rows_b):
                    place = 8 * (step * rows_b + row)
                    value = pick(table[place : place + 8, :], low)
                    found = jnp.where(high == base + row, value, found)
            lines = slice(3 * source, 3 * source + 3)
            force[lines, at(tile)] = pair[lines, at(tile)] + CHARGE[source] * found[0:3]

    def cross(left, right):
        return [
            left[1] * right[2] - left[2] * right[1],
            left[2] * right[0] - left[0] * right[2],
            left[0] * right[1] - left[1] * right[0],
        ]

    def split(array):
        return [array[compo : compo + 1, :] for compo in range(3)]

    total = force[0:3, :] + force[3:6, :] + force[6:9, :]
    torque = None
    centre = split(centres)
    for source in range(3):
        lever = [sites[3 * source + compo : 3 * source + compo + 1, :] - centre[compo] for compo in range(3)]
        push = [force[3 * source + compo : 3 * source + compo + 1, :] for compo in range(3)]
        turn = cross(lever, push)
        torque = turn if torque is None else [old + new for old, new in zip(torque, turn)]
    moving = velocity[...] + STEP_DT * total / WATER_MASS
    velocity_new[...] = moving
    centres_new[...] = centres[...] + STEP_DT * moving
    spin = [angmom[compo : compo + 1, :] + STEP_DT * torque[compo] for compo in range(3)]
    for compo in range(3):
        angmom_new[compo : compo + 1, :] = spin[compo]
    omega = [value * (1.0 / INERTIA) for value in spin]
    scalar = quat[0:1, :]
    vector = [quat[compo + 1 : compo + 2, :] for compo in range(3)]
    delta = [-(omega[0] * vector[0] + omega[1] * vector[1] + omega[2] * vector[2])]
    turned = cross(omega, vector)
    delta = delta + [scalar * omega[compo] + turned[compo] for compo in range(3)]
    moved = [old + 0.5 * STEP_DT * new for old, new in zip([scalar] + vector, delta)]
    length = jnp.sqrt(moved[0] * moved[0] + moved[1] * moved[1] + moved[2] * moved[2] + moved[3] * moved[3])
    for place in range(4):
        orient_new[place : place + 1, :] = moved[place] / length


def product_kernel(steps, hist_rows, block_rows, message, dens, *refs):
    count = len(steps)
    small, before = refs[:count], refs[count:-2]
    out, panel = refs[-2:]
    rows, cols = out.shape
    rows_b, cols_b = rows // BLOCK, cols // BLOCK
    here_row, here_col = position()
    spans = []
    for place, step in enumerate(steps):
        other = here_row ^ step
        base = (here_col ^ (other * rows // cols)) * cols + lax.rem(other * rows, cols)
        spans.append(pl.ds(pl.multiple_of(base, BLOCK), rows))
        flag = pattern_flags(message, hist_rows + step * block_rows + 3 * rows_b + here_col)
        for row in range(rows_b):
            block = small[place][row * BLOCK : (row + 1) * BLOCK, :]
            for col in range(cols_b):
                panel[place, row * BLOCK : (row + 1) * BLOCK, at(col)] = block * flag(row * cols_b + col)

    def one_row(row, carry):
        lines = pl.ds(pl.multiple_of(row * BLOCK, BLOCK), BLOCK)
        value = contract(dens[lines, spans[0]], panel[0], ((1,), (0,)))
        for place in range(1, count):
            value = value + contract(dens[lines, spans[place]], panel[place], ((1,), (0,)))
        if before:
            out[lines, :] = (value + before[0][lines, :]).astype(out.dtype)
        else:
            own = UNIT * COUPLE * message[pl.ds(here_row * rows_b + row, 1), :]
            across = jnp.transpose(jnp.broadcast_to(own, (BLOCK, BLOCK)))
            for col in range(cols_b):
                pot = UNIT * COUPLE * message[pl.ds(here_col * cols_b + col, 1), :]
                sums = (across + pot) * dens[lines, at(col)].astype(F32)
                out[lines, at(col)] = (value[:, at(col)] + sums).astype(out.dtype)
        return carry

    lax.fori_loop(0, rows_b, one_row, 0)


def tie_kernel(first, second, out):
    pass


VMEM = pl.BlockSpec(memory_space=pltpu.VMEM)
SMEM = pl.BlockSpec(memory_space=pltpu.SMEM)


def fetching(kernel, places, *refs):
    refs, semaphore = list(refs[:-1]), refs[-1]
    held = refs[len(refs) - len(places) :]
    copies = [pltpu.make_async_copy(refs[at_], held[n], semaphore.at[n]) for n, at_ in enumerate(places)]
    for copy in copies:
        copy.start()
    for copy in copies:
        copy.wait()
    for n, at_ in enumerate(places):
        refs[at_] = held[n]
    kernel(*refs[: len(refs) - len(places)])


def call(
    kernel, name, outs, operands, scalars=0, scratch=(), cost=(0, 0), whole=VMEM, fetch=(), unread=(), limit=48 << 20, **more
):
    in_specs = [SMEM] * scalars + [whole] * (len(operands) - scalars)
    scratch = list(scratch)
    for place in unread:
        in_specs[place] = pl.BlockSpec(memory_space=pl.ANY)
    if fetch:
        for place in fetch:
            memory = pltpu.SMEM if place < scalars else pltpu.VMEM
            scratch.append(memory(operands[place].shape, operands[place].dtype))
            in_specs[place] = pl.BlockSpec(memory_space=pltpu.HBM)
        scratch.append(pltpu.SemaphoreType.DMA((len(fetch),)))
        kernel = functools.partial(fetching, kernel, tuple(fetch))
    return pl.pallas_call(
        kernel,
        out_shape=[jax.ShapeDtypeStruct(shape, dtype) for shape, dtype in outs],
        in_specs=in_specs,
        out_specs=[whole] * len(outs),
        scratch_shapes=scratch,
        compiler_params=pltpu.CompilerParams(vmem_limit_bytes=limit),
        cost_estimate=pl.CostEstimate(flops=cost[0], bytes_accessed=cost[1], transcendentals=0),
        name=name,
        **more,
    )(*operands)


def doublings(count):
    step = 1
    while step < count:
        yield step
        step = 2 * step


def shards(
    density,
    margin,
    pattern_d,
    pattern_s,
    dipole,
    owner,
    centres,
    angles,
    velocity,
    angmom,
    halo_list,
    neighbours,
):
    rows, cols = density.shape
    rows_b, cols_b = pattern_d.shape
    rows_n = lax.axis_size("row")
    across = ("col", "sub")
    ways = lax.axis_size("col") * lax.axis_size("sub")
    hist_rows = rows * rows_n // LANES
    waters, listed, slots = centres.shape[1], halo_list.shape[1], neighbours.shape[0]
    block_rows = round8(3 * rows_b + ways)
    halo_rows = round8(18 * (listed // LANES))
    summed = hist_rows + rows_n * block_rows
    field_rows = round8(3 * rows_b)
    moment_rows = round8(3 * cols_b)

    def swap(value, axis, count, step):
        return lax.ppermute(value, axis, [(i, i ^ step) for i in range(count)])

    def tie(value, later):
        (value,) = call(
            tie_kernel,
            "tie",
            [(value.shape, value.dtype)],
            [value, later],
            whole=pl.BlockSpec(memory_space=pl.ANY),
            input_output_aliases={0: 0},
        )
        return value

    def merge(first, second, count, done=None):
        total = 2 * first.shape[0] - count
        operands = [first, second] + ([] if done is None else [done])
        (out,) = call(
            functools.partial(merge_kernel, count),
            "merge",
            [((total, LANES), F32)],
            operands,
            unread=range(2, len(operands)),
        )
        return out

    def send(value, axis, count):
        held = [value] + [None] * (count - 1)
        for step in doublings(count):
            held[step] = swap(value, axis, count, step)
        return held

    def relay(held, axis, count, later):
        for step in range(1, count):
            lowest = step & -step
            if step != lowest:
                if (step - lowest) & (step - lowest - 1) == 0:
                    held[step - lowest] = tie(held[step - lowest], later)
                held[step] = swap(held[step - lowest], axis, count, lowest)
        return held

    dens_all = send(density, across, ways)
    message, small, again, sites, quat = call(
        functools.partial(open_kernel, ways, hist_rows),
        "open",
        [
            ((hist_rows + block_rows + halo_rows, LANES), F32),
            ((rows, BLOCK), BF16),
            ((rows, BLOCK), BF16),
            ((16, waters), F32),
            ((4, waters), F32),
        ],
        [pattern_d, pattern_s, margin, dipole, owner, centres, angles, halo_list],
        scalars=2,
        cost=(10**6, 12 * 10**6),
        fetch=range(8),
        limit=60 << 20,
    )
    table, moments, held = call(
        prepare_kernel,
        "prepare",
        [
            ((5, waters // LANES, 8, LANES), jnp.int32),
            ((moment_rows, LANES), F32),
            (message.shape, F32),
        ],
        [sites, dipole, message],
    )
    first = -(-5 * (waters // LANES) // 8)
    (found,) = call(
        functools.partial(own_kernel, first),
        "own_gathers",
        [((5 * slots, waters), jnp.int32)],
        [table, neighbours],
        cost=(10**6, 6 * 10**6),
    )
    small_all = [small] + [None] * (rows_n - 1)
    small_all[1] = swap(small, "row", rows_n, 1)
    steps = list(doublings(rows_n))
    for step in steps[:-1]:
        message = merge(held, swap(message, "row", rows_n, step), hist_rows, moments)
        held = message
    later = tie(again, message)
    message, halos = call(
        functools.partial(turn_kernel, hist_rows, block_rows, halo_rows),
        "turn",
        [((summed + moment_rows, LANES), F32), ((rows_n * halo_rows, LANES), F32)],
        [message, swap(message, "row", rows_n, steps[-1]), moments, found],
        unread=(3,),
    )
    for step in steps[1:]:
        small_all[step] = swap(later, "row", rows_n, step)
    dens_all = relay(dens_all, across, ways, message)
    for step in doublings(ways):
        message = merge(message, swap(message, across, ways, step), summed)
    (pair,) = call(
        functools.partial(pair_kernel, rows_n, first),
        "pair_forces",
        [((9, waters), F32)],
        [sites, found, table, halos, neighbours],
        scratch=[pltpu.VMEM((5, 2 * listed // LANES, 8, LANES), jnp.int32)],
        cost=(10**6, 15 * 10**6),
    )
    field, masked = call(
        functools.partial(field_kernel, ways, hist_rows, block_rows, summed),
        "field",
        [((field_rows, LANES), F32), ((rows, ways * cols), BF16)],
        [message] + dens_all + [pair],
        unread=(1 + ways,),
        scratch=[pltpu.VMEM((8, cols), F32)],
        cost=(10**6, 5 * 10**6),
    )
    for step in doublings(rows_n):
        field = merge(field, swap(field, "row", rows_n, step), 0)
        if step == 1:
            small_all = relay(small_all, "row", rows_n, field)
    early = [0] + list(steps)
    late = [step for step in range(rows_n) if step not in early]
    partial, kinds = [], [(early, F32 if late else BF16)] + ([(late, BF16)] if late else [])
    for these, kind in kinds:
        partial = call(
            functools.partial(product_kernel, these, hist_rows, block_rows),
            "product",
            [((rows, cols), kind)],
            [message, masked] + [small_all[step] for step in these] + list(partial),
            scratch=[pltpu.VMEM((len(these), rows, cols), BF16)],
            cost=(10**6, 10 * 10**6),
        )
    (qm_out,) = partial
    centres_new, velocity_new, angmom_new, orient_new = call(
        functools.partial(advance_kernel, rows_n, rows_b),
        "advance",
        [((3, waters), F32), ((3, waters), F32), ((3, waters), F32), ((4, waters), F32)],
        [field, owner, sites, quat, pair, centres, velocity, angmom],
        scratch=[pltpu.VMEM((16, waters), F32), pltpu.VMEM((8 * hist_rows, LANES), F32)],
        cost=(10**6, 6 * 10**6),
    )
    return (qm_out, centres_new, velocity_new, angmom_new, orient_new)


def solution(mesh):
    square = P(("groups", "row"), ("col", "sub"))
    spread = P(None, ("groups", "row", "col", "sub"))
    return jax.shard_map(
        shards,
        mesh=mesh,
        in_specs=(square,) * 4 + (P(None, ("groups", "col", "sub")),) + (spread,) * 7,
        out_specs=(square,) + (spread,) * 4,
        check_vma=False,
    )
```

```python
import functools

import jax
import jax.numpy as jnp
from jax import lax
from jax.experimental import pallas as pl
from jax.experimental.pallas import tpu as pltpu
from jax.sharding import PartitionSpec as P

BLOCK = 128
LANES = 128

CHARGE = (-0.834, 0.417, 0.417)
UNIT = 0.417
MULTIPLE = (-2.0, 1.0, 1.0)
OFFSET = ((0.0, 0.0, -0.12), (0.76, 0.0, 0.47), (-0.76, 0.0, 0.47))
COUPLE = 0.1
STEP_DT = 0.5
WATER_MASS = 1.0
INERTIA = 0.5
SOFTEN = 1.0

SHIFT = 1.0
SCALE = 65535.0 / 5.0

F32 = jnp.float32
BF16 = jnp.bfloat16

SIN_TERMS = (-1 / 6, 1 / 120, -1 / 5040, 1 / 362880, -1 / 39916800, 1 / 6227020800)
COS_TERMS = (-1 / 2, 1 / 24, -1 / 720, 1 / 40320, -1 / 3628800, 1 / 479001600, -1 / 87178291200)


def at(tile):
    return slice(tile * LANES, (tile + 1) * LANES)


def position():
    return lax.axis_index("row"), lax.axis_index(("col", "sub"))


def pick(table, index):
    return jnp.take_along_axis(table, index, axis=1, mode="promise_in_bounds")


def contract(left, right, dims):
    return lax.dot_general(left, right, (dims, ((), ())), preferred_element_type=F32)


def series(square, terms):
    total = jnp.full_like(square, terms[-1])
    for term in terms[-2::-1]:
        total = total * square + term
    return total * square + 1.0


def line_of(row, comp):
    return 3 * row + comp


def round8(count):
    return -(-count // 8) * 8


def open_kernel(
    ways,
    hist_rows,
    pat_d,
    pat_s,
    marg,
    dip,
    owner,
    centres,
    angles,
    halo,
    message,
    small,
    again,
    sites,
    quat,
):
    rows_b, cols_b = pat_d.shape
    waters = owner.shape[1]
    here_col = position()[1]
    message[...] = jnp.zeros(message.shape, F32)
    lane = lax.broadcasted_iota(jnp.int32, (1, LANES), 1)
    patterns = jnp.zeros((1, LANES), F32)
    for row in range(rows_b):
        chosen = jnp.int32(0)
        lines = slice(row * BLOCK, (row + 1) * BLOCK)
        for col in range(cols_b):
            chosen = chosen + col * pat_s[row, col]
            line = row * cols_b + col
            patterns = jnp.where(lane == line, pat_s[row, col].astype(F32), patterns)
            patterns = jnp.where(lane == rows_b * cols_b + line, pat_d[row, col].astype(F32), patterns)
        span = pl.ds(pl.multiple_of(chosen * BLOCK, BLOCK), BLOCK)
        block = marg[lines, span]
        for copy in (small, again):
            copy[lines, :] = block
        product = contract(dip[:, span], block, ((1,), (1,)))
        place = hist_rows + line_of(row, 0)
        message[place : place + 3, :] = product
    message[pl.ds(hist_rows + 3 * rows_b + here_col, 1), :] = patterns
    total = jnp.zeros((hist_rows, LANES), F32)
    for source in range(3):
        line = owner[source : source + 1, :]
        high = lax.broadcasted_iota(jnp.int32, (hist_rows, waters), 0) == (line >> 7)
        low = lax.broadcasted_iota(jnp.int32, (LANES, waters), 0) == (line & 127)
        total = total + contract(
            jnp.where(high, MULTIPLE[source], 0.0).astype(BF16),
            jnp.where(low, 1.0, 0.0).astype(BF16),
            ((1,), (1,)),
        )
    message[0:hist_rows, :] = total
    halo_at = hist_rows + round8(3 * rows_b + ways)
    water_sites(centres, angles, halo, sites, quat, message.at[halo_at:, :])


def water_sites(centres, angles, halo, sites, quat, listed):
    half_angle = 0.5 * angles[...]
    square = half_angle * half_angle
    sine = half_angle * series(square, SIN_TERMS)
    cosine = series(square, COS_TERMS)
    sin_r, sin_p, sin_y = sine[0:1], sine[1:2], sine[2:3]
    cos_r, cos_p, cos_y = cosine[0:1], cosine[1:2], cosine[2:3]
    comp_w = cos_r * cos_p * cos_y + sin_r * sin_p * sin_y
    comp_x = sin_r * cos_p * cos_y - cos_r * sin_p * sin_y
    comp_y = cos_r * sin_p * cos_y + sin_r * cos_p * sin_y
    comp_z = cos_r * cos_p * sin_y - sin_r * sin_p * cos_y
    for place, comp in enumerate((comp_w, comp_x, comp_y, comp_z)):
        quat[place : place + 1, :] = comp
    first = (
        1.0 - 2.0 * (comp_y * comp_y + comp_z * comp_z),
        2.0 * (comp_x * comp_y + comp_w * comp_z),
        2.0 * (comp_x * comp_z - comp_w * comp_y),
    )
    third = (
        2.0 * (comp_x * comp_z + comp_w * comp_y),
        2.0 * (comp_y * comp_z - comp_w * comp_x),
        1.0 - 2.0 * (comp_x * comp_x + comp_y * comp_y),
    )
    sites[...] = jnp.zeros(sites.shape, F32)
    for source in range(3):
        for compo in range(3):
            place = 3 * source + compo
            position = centres[compo : compo + 1, :] + third[compo] * OFFSET[source][2]
            if OFFSET[source][0] != 0.0:
                position = position + first[compo] * OFFSET[source][0]
            sites[place : place + 1, :] = position
    waters, tiles = centres.shape[1], halo.shape[1] // LANES
    for which in range(2):
        for tile in range(tiles):
            index = jnp.broadcast_to(halo[which : which + 1, at(tile)], (8, LANES))
            low, high = index & 127, index >> 7
            for part in range(2):
                found = jnp.zeros((8, LANES), F32)
                for source in range(waters // LANES):
                    value = pick(sites[8 * part : 8 * part + 8, at(source)], low)
                    found = jnp.where(high == source, value, found)
                for comp in range(8 * part, min(8 * part + 8, 9)):
                    place = (which * 9 + comp) * tiles + tile
                    listed[place : place + 1, :] = found[comp - 8 * part : comp - 8 * part + 1]


def merge_kernel(summed, first, second, *refs):
    out = refs[-1]
    if summed > 0:
        out[0:summed, :] = first[0:summed, :] + second[0:summed, :]
    count = first.shape[0] - summed
    if count > 0:
        out[summed : summed + count, :] = first[summed:, :]
        out[summed + count :, :] = second[summed:, :]


def turn_kernel(summed, block_rows, halo_rows, first, second, moments, done, out, halos):
    out[0:summed, :] = first[0:summed, :] + second[0:summed, :]
    count = (first.shape[0] - summed) // (block_rows + halo_rows)
    for number, ref in enumerate((first, second)):
        for block in range(count):
            start = summed + block * (block_rows + halo_rows)
            place = number * count + block
            out[summed + place * block_rows : summed + (place + 1) * block_rows, :] = ref[
                start : start + block_rows, :
            ]
            halos[place * halo_rows : (place + 1) * halo_rows, :] = ref[
                start + block_rows : start + block_rows + halo_rows, :
            ]
    out[summed + 2 * count * block_rows :, :] = moments[...]


def store_words(table, tile, lines):
    fixed = [(line * SCALE + (SHIFT * SCALE + 0.5)).astype(jnp.int32) for line in lines]
    for word in range(5):
        value = fixed[2 * word]
        if word < 4:
            value = value | ((fixed[2 * word + 1] - 32768) << 16)
        table[word, tile] = jnp.broadcast_to(value, (8, LANES))


def gather_words(sources, index, found):
    low = [value & 127 for value in index]
    high = [value >> 7 for value in index]
    for number, table, place in sources:
        here = [value == number for value in high]
        for word in range(5):
            line = table[word, place]
            for part in range(len(index)):
                value = pick(line, low[part])
                old = found[word][part]
                found[word][part] = value if old is None else jnp.where(here[part], value, old)
    return found


def prepare_kernel(sites, dip, message, table, moments, held):
    held[...] = message[...]
    moments[...] = jnp.zeros(moments.shape, F32)
    for col in range(dip.shape[1] // BLOCK):
        moments[3 * col : 3 * col + 3, :] = dip[:, at(col)].astype(F32)
    for tile in range(sites.shape[1] // LANES):
        store_words(table, tile, [sites[word : word + 1, at(tile)] for word in range(9)])


def own_kernel(first, table, neighbours, out):
    slots, waters = neighbours.shape
    sources = [(tile, table, tile) for tile in range(first)]

    def one_tile(tile, carry):
        span = pl.ds(pl.multiple_of(tile * LANES, LANES), LANES)
        for pair in range(slots // 16):
            rows = [slice(16 * pair + 8 * part, 16 * pair + 8 * part + 8) for part in range(2)]
            found = gather_words(sources, [neighbours[row, span] for row in rows], [[None, None] for _ in range(5)])
            for word in range(5):
                for part in range(2):
                    start = word * slots + 16 * pair + 8 * part
                    out[start : start + 8, span] = found[word][part]
        return carry

    lax.fori_loop(0, waters // LANES, one_tile, 0)


def pair_kernel(rows_n, first, sites, own_words, own_table, halos, neighbours, force, table):
    waters, slots = sites.shape[1], neighbours.shape[0]
    depth = halos.shape[0] // rows_n
    own_tiles = waters // LANES
    halo_tiles = table.shape[1] // 2
    here_row = position()[0]
    for which in range(2):
        other = lax.rem(here_row + (rows_n - 1, 1)[which], rows_n)
        start = pl.multiple_of((here_row ^ other) * depth, 8)
        lines = halos[pl.ds(start, depth), :]
        for tile in range(halo_tiles):
            places = [(which * 9 + word) * halo_tiles + tile for word in range(9)]
            store_words(table, which * halo_tiles + tile, [lines[place : place + 1] for place in places])

    sources = [(tile, own_table, tile) for tile in range(first, own_tiles)]
    sources = sources + [(own_tiles + tile, table, tile) for tile in range(2 * halo_tiles)]

    def one_tile(tile, carry):
        span = pl.ds(pl.multiple_of(tile * LANES, LANES), LANES)
        lines = sites[:, span]
        own = []
        for word in range(9):
            line = jnp.broadcast_to(lines[word : word + 1] * SCALE + SHIFT * SCALE, (8, LANES))
            own.append((line, line - 32768.0))
        near = [jnp.zeros((8, LANES), F32) for _ in range(9)]
        far = [jnp.zeros((8, LANES), F32) for _ in range(9)]
        for pair in range(slots // 16):
            starts = [16 * pair + 8 * part for part in range(2)]
            found = [
                [own_words[word * slots + start : word * slots + start + 8, span] for start in starts]
                for word in range(5)
            ]
            index = [neighbours[start : start + 8, span] for start in starts]
            found = gather_words(sources, index, found)
            for part in range(2):
                places = []
                for word in range(9):
                    value = found[word // 2][part]
                    if word == 8:
                        places.append(value.astype(F32))
                    elif word % 2 == 0:
                        places.append((value & 65535).astype(F32))
                    else:
                        places.append((value >> 16).astype(F32))
                for source in range(3):
                    for target in range(3):
                        gap = []
                        for compo in range(3):
                            mine, other = 3 * source + compo, 3 * target + compo
                            gap.append(own[mine][other % 2] - places[other])
                        root = lax.rsqrt(
                            gap[0] * gap[0] + gap[1] * gap[1] + gap[2] * gap[2] + SOFTEN * SCALE * SCALE
                        )
                        weight = root * root * root
                        sums = near if target == 0 else far
                        for compo in range(3):
                            sums[3 * source + compo] = sums[3 * source + compo] + gap[compo] * weight
        for place in range(9):
            factor = CHARGE[place // 3] * UNIT * SCALE * SCALE
            total = factor * (far[place] - 2.0 * near[place])
            force[place : place + 1, span] = jnp.sum(total, axis=0, keepdims=True)
        return carry

    lax.fori_loop(0, own_tiles, one_tile, 0)


def pattern_flags(message, place):
    line = jnp.broadcast_to(message[pl.ds(place, 1), :], (8, LANES))
    return lambda block: pick(line, jnp.full((8, LANES), block, jnp.int32))[0:1].astype(BF16)


def field_kernel(ways, hist_rows, block_rows, summed, message, *refs):
    dens, out, masked, lines = refs[:ways], refs[ways + 1], refs[ways + 2], refs[ways + 3]
    rows, cols = dens[0].shape
    rows_b, cols_b = rows // BLOCK, cols // BLOCK
    depth = (message.shape[0] - summed) // ways
    here_row, here_col = position()
    result = jnp.zeros((16, rows), F32)
    lines[...] = jnp.zeros(lines.shape, F32)
    for step in range(ways):
        device = here_col ^ step
        flag = pattern_flags(message, hist_rows + 3 * rows_b + device)
        for col in range(cols_b):
            other = device * (cols_b // rows_b) + col // rows_b
            place = hist_rows + (here_row ^ other) * block_rows + line_of(col % rows_b, 0)
            start = summed + step * depth + 3 * col
            moment = message[start : start + 3, :]
            pot = UNIT * COUPLE * message[pl.ds(device * cols_b + col, 1), :]
            for comp in range(3):
                product = message[pl.ds(place + comp, 1), :]
                lines[comp : comp + 1, at(col)] = product + pot * moment[comp : comp + 1]
            lines[3:6, at(col)] = moment
            for row in range(rows_b):
                spot = slice(row * BLOCK, (row + 1) * BLOCK)
                target = slice(step * cols + col * BLOCK, step * cols + (col + 1) * BLOCK)
                masked[spot, target] = dens[step][spot, at(col)] * flag(rows_b * cols_b + row * cols_b + col)
        whole = lines[...]
        first = whole.astype(BF16).astype(F32)
        both = jnp.concatenate([first, whole - first], axis=0).astype(BF16)
        result = result + contract(both, masked[:, step * cols : (step + 1) * cols], ((1,), (1,)))
    total = result[0:8] + result[8:16]
    out[...] = jnp.zeros(out.shape, F32)
    for row in range(rows_b):
        pot = UNIT * COUPLE * message[pl.ds(here_row * rows_b + row, 1), :]
        start = line_of(row, 0)
        out[start : start + 3, :] = total[0:3, at(row)] + pot * total[3:6, at(row)]


def advance_kernel(
    rows_n,
    rows_b,
    fields,
    owner,
    sites,
    quat,
    pair,
    centres,
    velocity,
    angmom,
    centres_new,
    velocity_new,
    angmom_new,
    orient_new,
    force,
    table,
):
    waters = owner.shape[1]
    depth = fields.shape[0] // rows_n
    here_row = position()[0]
    table[...] = jnp.zeros(table.shape, F32)
    for step in range(rows_n):
        for row in range(rows_b):
            start = step * depth + line_of(row, 0)
            place = 4 * (step * rows_b + row)
            table[place : place + 3, :] = fields[start : start + 3, :]
    for tile in range(waters // LANES):
        for source in range(3):
            index = jnp.broadcast_to(owner[source : source + 1, at(tile)], (8, LANES))
            low, high = index & 127, index >> 7
            found = jnp.zeros((8, LANES), F32)
            for step in range(rows_n):
                base = (here_row ^ step) * (rows_b // 2)
                for two in range(rows_b // 2):
                    place = 8 * (step * (rows_b // 2) + two)
                    value = pick(table[place : place + 8, :], low)
                    found = jnp.where((high >> 1) == base + two, value, found)
            odd = (high[0:3] & 1) == 1
            found = jnp.where(odd, found[4:7], found[0:3])
            lines = slice(3 * source, 3 * source + 3)
            force[lines, at(tile)] = pair[lines, at(tile)] + CHARGE[source] * found

    def cross(left, right):
        return [
            left[1] * right[2] - left[2] * right[1],
            left[2] * right[0] - left[0] * right[2],
            left[0] * right[1] - left[1] * right[0],
        ]

    def split(array):
        return [array[compo : compo + 1, :] for compo in range(3)]

    total = force[0:3, :] + force[3:6, :] + force[6:9, :]
    torque = None
    centre = split(centres)
    for source in range(3):
        lever = [sites[3 * source + compo : 3 * source + compo + 1, :] - centre[compo] for compo in range(3)]
        push = [force[3 * source + compo : 3 * source + compo + 1, :] for compo in range(3)]
        turn = cross(lever, push)
        torque = turn if torque is None else [old + new for old, new in zip(torque, turn)]
    moving = velocity[...] + STEP_DT * total / WATER_MASS
    velocity_new[...] = moving
    centres_new[...] = centres[...] + STEP_DT * moving
    spin = [angmom[compo : compo + 1, :] + STEP_DT * torque[compo] for compo in range(3)]
    for compo in range(3):
        angmom_new[compo : compo + 1, :] = spin[compo]
    omega = [value * (1.0 / INERTIA) for value in spin]
    scalar = quat[0:1, :]
    vector = [quat[compo + 1 : compo + 2, :] for compo in range(3)]
    delta = [-(omega[0] * vector[0] + omega[1] * vector[1] + omega[2] * vector[2])]
    turned = cross(omega, vector)
    delta = delta + [scalar * omega[compo] + turned[compo] for compo in range(3)]
    moved = [old + 0.5 * STEP_DT * new for old, new in zip([scalar] + vector, delta)]
    length = jnp.sqrt(moved[0] * moved[0] + moved[1] * moved[1] + moved[2] * moved[2] + moved[3] * moved[3])
    for place in range(4):
        orient_new[place : place + 1, :] = moved[place] / length


def product_kernel(steps, hist_rows, block_rows, message, dens, *refs):
    count = len(steps)
    small, before = refs[:count], refs[count:-2]
    out, panel = refs[-2:]
    rows, cols = out.shape
    rows_b, cols_b = rows // BLOCK, cols // BLOCK
    here_row, here_col = position()
    spans = []
    for place, step in enumerate(steps):
        other = here_row ^ step
        base = (here_col ^ (other * rows // cols)) * cols + lax.rem(other * rows, cols)
        spans.append(pl.ds(pl.multiple_of(base, BLOCK), rows))
        flag = pattern_flags(message, hist_rows + step * block_rows + 3 * rows_b + here_col)
        for row in range(rows_b):
            block = small[place][row * BLOCK : (row + 1) * BLOCK, :]
            for col in range(cols_b):
                panel[place, row * BLOCK : (row + 1) * BLOCK, at(col)] = block * flag(row * cols_b + col)

    def one_row(row, carry):
        lines = pl.ds(pl.multiple_of(row * BLOCK, BLOCK), BLOCK)
        value = contract(dens[lines, spans[0]], panel[0], ((1,), (0,)))
        for place in range(1, count):
            value = value + contract(dens[lines, spans[place]], panel[place], ((1,), (0,)))
        if before:
            out[lines, :] = (value + before[0][lines, :]).astype(out.dtype)
        else:
            own = UNIT * COUPLE * message[pl.ds(here_row * rows_b + row, 1), :]
            across = jnp.transpose(jnp.broadcast_to(own, (BLOCK, BLOCK)))
            for col in range(cols_b):
                pot = UNIT * COUPLE * message[pl.ds(here_col * cols_b + col, 1), :]
                sums = (across + pot) * dens[lines, at(col)].astype(F32)
                out[lines, at(col)] = (value[:, at(col)] + sums).astype(out.dtype)
        return carry

    lax.fori_loop(0, rows_b, one_row, 0)


def tie_kernel(first, second, out):
    pass


VMEM = pl.BlockSpec(memory_space=pltpu.VMEM)
SMEM = pl.BlockSpec(memory_space=pltpu.SMEM)


def fetching(kernel, places, *refs):
    refs, semaphore = list(refs[:-1]), refs[-1]
    held = refs[len(refs) - len(places) :]
    copies = [pltpu.make_async_copy(refs[at_], held[n], semaphore.at[n]) for n, at_ in enumerate(places)]
    for copy in copies:
        copy.start()
    for copy in copies:
        copy.wait()
    for n, at_ in enumerate(places):
        refs[at_] = held[n]
    kernel(*refs[: len(refs) - len(places)])


def call(
    kernel, name, outs, operands, scalars=0, scratch=(), cost=(0, 0), whole=VMEM, fetch=(), unread=(), limit=48 << 20, **more
):
    in_specs = [SMEM] * scalars + [whole] * (len(operands) - scalars)
    scratch = list(scratch)
    for place in unread:
        in_specs[place] = pl.BlockSpec(memory_space=pl.ANY)
    if fetch:
        for place in fetch:
            memory = pltpu.SMEM if place < scalars else pltpu.VMEM
            scratch.append(memory(operands[place].shape, operands[place].dtype))
            in_specs[place] = pl.BlockSpec(memory_space=pltpu.HBM)
        scratch.append(pltpu.SemaphoreType.DMA((len(fetch),)))
        kernel = functools.partial(fetching, kernel, tuple(fetch))
    return pl.pallas_call(
        kernel,
        out_shape=[jax.ShapeDtypeStruct(shape, dtype) for shape, dtype in outs],
        in_specs=in_specs,
        out_specs=[whole] * len(outs),
        scratch_shapes=scratch,
        compiler_params=pltpu.CompilerParams(vmem_limit_bytes=limit),
        cost_estimate=pl.CostEstimate(flops=cost[0], bytes_accessed=cost[1], transcendentals=0),
        name=name,
        **more,
    )(*operands)


def doublings(count):
    step = 1
    while step < count:
        yield step
        step = 2 * step


def shards(
    density,
    margin,
    pattern_d,
    pattern_s,
    dipole,
    owner,
    centres,
    angles,
    velocity,
    angmom,
    halo_list,
    neighbours,
):
    rows, cols = density.shape
    rows_b, cols_b = pattern_d.shape
    rows_n = lax.axis_size("row")
    across = ("col", "sub")
    ways = lax.axis_size("col") * lax.axis_size("sub")
    hist_rows = rows * rows_n // LANES
    waters, listed, slots = centres.shape[1], halo_list.shape[1], neighbours.shape[0]
    block_rows = round8(3 * rows_b + ways)
    halo_rows = round8(18 * (listed // LANES))
    summed = hist_rows + rows_n * block_rows
    field_rows = round8(3 * rows_b)
    moment_rows = round8(3 * cols_b)

    def swap(value, axis, count, step):
        return lax.ppermute(value, axis, [(i, i ^ step) for i in range(count)])

    def tie(value, later):
        (value,) = call(
            tie_kernel,
            "tie",
            [(value.shape, value.dtype)],
            [value, later],
            whole=pl.BlockSpec(memory_space=pl.ANY),
            input_output_aliases={0: 0},
        )
        return value

    def merge(first, second, count, done=None):
        total = 2 * first.shape[0] - count
        operands = [first, second] + ([] if done is None else [done])
        (out,) = call(
            functools.partial(merge_kernel, count),
            "merge",
            [((total, LANES), F32)],
            operands,
            unread=range(2, len(operands)),
        )
        return out

    def send(value, axis, count):
        held = [value] + [None] * (count - 1)
        for step in doublings(count):
            held[step] = swap(value, axis, count, step)
        return held

    def relay(held, axis, count, later):
        for step in range(1, count):
            lowest = step & -step
            if step != lowest:
                if (step - lowest) & (step - lowest - 1) == 0:
                    held[step - lowest] = tie(held[step - lowest], later)
                held[step] = swap(held[step - lowest], axis, count, lowest)
        return held

    dens_all = send(density, across, ways)
    message, small, again, sites, quat = call(
        functools.partial(open_kernel, ways, hist_rows),
        "open",
        [
            ((hist_rows + block_rows + halo_rows, LANES), F32),
            ((rows, BLOCK), BF16),
            ((rows, BLOCK), BF16),
            ((16, waters), F32),
            ((4, waters), F32),
        ],
        [pattern_d, pattern_s, margin, dipole, owner, centres, angles, halo_list],
        scalars=2,
        cost=(10**6, 12 * 10**6),
        fetch=range(8),
        limit=60 << 20,
    )
    table, moments, held = call(
        prepare_kernel,
        "prepare",
        [
            ((5, waters // LANES, 8, LANES), jnp.int32),
            ((moment_rows, LANES), F32),
            (message.shape, F32),
        ],
        [sites, dipole, message],
    )
    first = -(-5 * (waters // LANES) // 8)
    (found,) = call(
        functools.partial(own_kernel, first),
        "own_gathers",
        [((5 * slots, waters), jnp.int32)],
        [table, neighbours],
        cost=(10**6, 6 * 10**6),
    )
    small_all = [small] + [None] * (rows_n - 1)
    small_all[1] = swap(small, "row", rows_n, 1)
    steps = list(doublings(rows_n))
    for step in steps[:-1]:
        message = merge(held, swap(message, "row", rows_n, step), hist_rows, moments)
        held = message
    later = tie(again, message)
    message, halos = call(
        functools.partial(turn_kernel, hist_rows, block_rows, halo_rows),
        "turn",
        [((summed + moment_rows, LANES), F32), ((rows_n * halo_rows, LANES), F32)],
        [message, swap(message, "row", rows_n, steps[-1]), moments, found],
        unread=(3,),
    )
    for step in steps[1:]:
        small_all[step] = swap(later, "row", rows_n, step)
    dens_all = relay(dens_all, across, ways, message)
    for step in doublings(ways):
        message = merge(message, swap(message, across, ways, step), summed)
    (pair,) = call(
        functools.partial(pair_kernel, rows_n, first),
        "pair_forces",
        [((9, waters), F32)],
        [sites, found, table, halos, neighbours],
        scratch=[pltpu.VMEM((5, 2 * listed // LANES, 8, LANES), jnp.int32)],
        cost=(10**6, 15 * 10**6),
    )
    field, masked = call(
        functools.partial(field_kernel, ways, hist_rows, block_rows, summed),
        "field",
        [((field_rows, LANES), F32), ((rows, ways * cols), BF16)],
        [message] + dens_all + [pair],
        unread=(1 + ways,),
        scratch=[pltpu.VMEM((8, cols), F32)],
        cost=(10**6, 5 * 10**6),
    )
    for step in doublings(rows_n):
        field = merge(field, swap(field, "row", rows_n, step), 0)
        if step == 1:
            small_all = relay(small_all, "row", rows_n, field)
    early = [0] + steps[1:]
    late = [step for step in range(rows_n) if step not in early]
    partial, kinds = [], [(early, F32 if late else BF16)] + ([(late, BF16)] if late else [])
    for these, kind in kinds:
        partial = call(
            functools.partial(product_kernel, these, hist_rows, block_rows),
            "product",
            [((rows, cols), kind)],
            [message, masked] + [small_all[step] for step in these] + list(partial),
            scratch=[pltpu.VMEM((len(these), rows, cols), BF16)],
            cost=(10**6, 10 * 10**6),
        )
    (qm_out,) = partial
    centres_new, velocity_new, angmom_new, orient_new = call(
        functools.partial(advance_kernel, rows_n, rows_b),
        "advance",
        [((3, waters), F32), ((3, waters), F32), ((3, waters), F32), ((4, waters), F32)],
        [field, owner, sites, quat, pair, centres, velocity, angmom],
        scratch=[pltpu.VMEM((16, waters), F32), pltpu.VMEM((4 * hist_rows, LANES), F32)],
        cost=(10**6, 6 * 10**6),
    )
    return (qm_out, centres_new, velocity_new, angmom_new, orient_new)


def solution(mesh):
    square = P(("groups", "row"), ("col", "sub"))
    spread = P(None, ("groups", "row", "col", "sub"))
    return jax.shard_map(
        shards,
        mesh=mesh,
        in_specs=(square,) * 4 + (P(None, ("groups", "col", "sub")),) + (spread,) * 7,
        out_specs=(square,) + (spread,) * 4,
        check_vma=False,
    )
```

```python
import functools

import jax
import jax.numpy as jnp
from jax import lax
from jax.experimental import pallas as pl
from jax.experimental.pallas import tpu as pltpu
from jax.sharding import PartitionSpec as P

BLOCK = 128
LANES = 128

CHARGE = (-0.834, 0.417, 0.417)
UNIT = 0.417
MULTIPLE = (-2.0, 1.0, 1.0)
OFFSET = ((0.0, 0.0, -0.12), (0.76, 0.0, 0.47), (-0.76, 0.0, 0.47))
COUPLE = 0.1
STEP_DT = 0.5
WATER_MASS = 1.0
INERTIA = 0.5
SOFTEN = 1.0

SHIFT = 1.0
SCALE = 65535.0 / 5.0

F32 = jnp.float32
BF16 = jnp.bfloat16

SIN_TERMS = (-1 / 6, 1 / 120, -1 / 5040, 1 / 362880, -1 / 39916800, 1 / 6227020800)
COS_TERMS = (-1 / 2, 1 / 24, -1 / 720, 1 / 40320, -1 / 3628800, 1 / 479001600, -1 / 87178291200)


def at(tile):
    return slice(tile * LANES, (tile + 1) * LANES)


def position():
    return lax.axis_index("row"), lax.axis_index(("col", "sub"))


def pick(table, index):
    return jnp.take_along_axis(table, index, axis=1, mode="promise_in_bounds")


def contract(left, right, dims):
    return lax.dot_general(left, right, (dims, ((), ())), preferred_element_type=F32)


def series(square, terms):
    total = jnp.full_like(square, terms[-1])
    for term in terms[-2::-1]:
        total = total * square + term
    return total * square + 1.0


def line_of(row, comp):
    return 3 * row + comp


def round8(count):
    return -(-count // 8) * 8


def open_kernel(
    ways,
    hist_rows,
    pat_d,
    pat_s,
    marg,
    dip,
    owner,
    centres,
    angles,
    halo,
    message,
    small,
    again,
    sites,
    quat,
):
    rows_b, cols_b = pat_d.shape
    waters = owner.shape[1]
    here_col = position()[1]
    message[...] = jnp.zeros(message.shape, F32)
    lane = lax.broadcasted_iota(jnp.int32, (1, LANES), 1)
    patterns = jnp.zeros((1, LANES), F32)
    for row in range(rows_b):
        chosen = jnp.int32(0)
        lines = slice(row * BLOCK, (row + 1) * BLOCK)
        for col in range(cols_b):
            chosen = chosen + col * pat_s[row, col]
            line = row * cols_b + col
            patterns = jnp.where(lane == line, pat_s[row, col].astype(F32), patterns)
            patterns = jnp.where(lane == rows_b * cols_b + line, pat_d[row, col].astype(F32), patterns)
        span = pl.ds(pl.multiple_of(chosen * BLOCK, BLOCK), BLOCK)
        block = marg[lines, span]
        for copy in (small, again):
            copy[lines, :] = block
        product = contract(dip[:, span], block, ((1,), (1,)))
        place = hist_rows + line_of(row, 0)
        message[place : place + 3, :] = product
    message[pl.ds(hist_rows + 3 * rows_b + here_col, 1), :] = patterns
    total = jnp.zeros((hist_rows, LANES), F32)
    for source in range(3):
        line = owner[source : source + 1, :]
        high = lax.broadcasted_iota(jnp.int32, (hist_rows, waters), 0) == (line >> 7)
        low = lax.broadcasted_iota(jnp.int32, (LANES, waters), 0) == (line & 127)
        total = total + contract(
            jnp.where(high, MULTIPLE[source], 0.0).astype(BF16),
            jnp.where(low, 1.0, 0.0).astype(BF16),
            ((1,), (1,)),
        )
    message[0:hist_rows, :] = total
    halo_at = hist_rows + round8(3 * rows_b + ways)
    water_sites(centres, angles, halo, sites, quat, message.at[halo_at:, :])


def water_sites(centres, angles, halo, sites, quat, listed):
    half_angle = 0.5 * angles[...]
    square = half_angle * half_angle
    sine = half_angle * series(square, SIN_TERMS)
    cosine = series(square, COS_TERMS)
    sin_r, sin_p, sin_y = sine[0:1], sine[1:2], sine[2:3]
    cos_r, cos_p, cos_y = cosine[0:1], cosine[1:2], cosine[2:3]
    comp_w = cos_r * cos_p * cos_y + sin_r * sin_p * sin_y
    comp_x = sin_r * cos_p * cos_y - cos_r * sin_p * sin_y
    comp_y = cos_r * sin_p * cos_y + sin_r * cos_p * sin_y
    comp_z = cos_r * cos_p * sin_y - sin_r * sin_p * cos_y
    for place, comp in enumerate((comp_w, comp_x, comp_y, comp_z)):
        quat[place : place + 1, :] = comp
    first = (
        1.0 - 2.0 * (comp_y * comp_y + comp_z * comp_z),
        2.0 * (comp_x * comp_y + comp_w * comp_z),
        2.0 * (comp_x * comp_z - comp_w * comp_y),
    )
    third = (
        2.0 * (comp_x * comp_z + comp_w * comp_y),
        2.0 * (comp_y * comp_z - comp_w * comp_x),
        1.0 - 2.0 * (comp_x * comp_x + comp_y * comp_y),
    )
    sites[...] = jnp.zeros(sites.shape, F32)
    for source in range(3):
        for compo in range(3):
            place = 3 * source + compo
            position = centres[compo : compo + 1, :] + third[compo] * OFFSET[source][2]
            if OFFSET[source][0] != 0.0:
                position = position + first[compo] * OFFSET[source][0]
            sites[place : place + 1, :] = position
    waters, tiles = centres.shape[1], halo.shape[1] // LANES
    for which in range(2):
        for tile in range(tiles):
            index = jnp.broadcast_to(halo[which : which + 1, at(tile)], (8, LANES))
            low, high = index & 127, index >> 7
            for part in range(2):
                found = jnp.zeros((8, LANES), F32)
                for source in range(waters // LANES):
                    value = pick(sites[8 * part : 8 * part + 8, at(source)], low)
                    found = jnp.where(high == source, value, found)
                for comp in range(8 * part, min(8 * part + 8, 9)):
                    place = (which * 9 + comp) * tiles + tile
                    listed[place : place + 1, :] = found[comp - 8 * part : comp - 8 * part + 1]


def merge_kernel(summed, first, second, *refs):
    out = refs[-1]
    if summed > 0:
        out[0:summed, :] = first[0:summed, :] + second[0:summed, :]
    count = first.shape[0] - summed
    if count > 0:
        out[summed : summed + count, :] = first[summed:, :]
        out[summed + count :, :] = second[summed:, :]


def turn_kernel(summed, block_rows, halo_rows, first, second, moments, done, out, halos):
    out[0:summed, :] = first[0:summed, :] + second[0:summed, :]
    count = (first.shape[0] - summed) // (block_rows + halo_rows)
    for number, ref in enumerate((first, second)):
        for block in range(count):
            start = summed + block * (block_rows + halo_rows)
            place = number * count + block
            out[summed + place * block_rows : summed + (place + 1) * block_rows, :] = ref[
                start : start + block_rows, :
            ]
            halos[place * halo_rows : (place + 1) * halo_rows, :] = ref[
                start + block_rows : start + block_rows + halo_rows, :
            ]
    out[summed + 2 * count * block_rows :, :] = moments[...]


def store_words(table, tile, lines):
    fixed = [(line * SCALE + (SHIFT * SCALE + 0.5)).astype(jnp.int32) for line in lines]
    for word in range(5):
        value = fixed[2 * word]
        if word < 4:
            value = value | ((fixed[2 * word + 1] - 32768) << 16)
        table[word, tile] = jnp.broadcast_to(value, (8, LANES))


def gather_words(sources, index, found):
    low = [value & 127 for value in index]
    high = [value >> 7 for value in index]
    for number, table, place in sources:
        here = [value == number for value in high]
        for word in range(5):
            line = table[word, place]
            for part in range(len(index)):
                value = pick(line, low[part])
                old = found[word][part]
                found[word][part] = value if old is None else jnp.where(here[part], value, old)
    return found


def prepare_kernel(sites, dip, message, table, moments, held):
    held[...] = message[...]
    moments[...] = jnp.zeros(moments.shape, F32)
    for col in range(dip.shape[1] // BLOCK):
        moments[3 * col : 3 * col + 3, :] = dip[:, at(col)].astype(F32)
    for tile in range(sites.shape[1] // LANES):
        store_words(table, tile, [sites[word : word + 1, at(tile)] for word in range(9)])


def own_kernel(first, table, neighbours, out):
    slots, waters = neighbours.shape
    sources = [(tile, table, tile) for tile in range(first)]

    def one_tile(tile, carry):
        span = pl.ds(pl.multiple_of(tile * LANES, LANES), LANES)
        for pair in range(slots // 16):
            rows = [slice(16 * pair + 8 * part, 16 * pair + 8 * part + 8) for part in range(2)]
            found = gather_words(sources, [neighbours[row, span] for row in rows], [[None, None] for _ in range(5)])
            for word in range(5):
                for part in range(2):
                    start = word * slots + 16 * pair + 8 * part
                    out[start : start + 8, span] = found[word][part]
        return carry

    lax.fori_loop(0, waters // LANES, one_tile, 0)


def pair_kernel(rows_n, first, sites, own_words, own_table, halos, neighbours, force, table):
    waters, slots = sites.shape[1], neighbours.shape[0]
    depth = halos.shape[0] // rows_n
    own_tiles = waters // LANES
    halo_tiles = table.shape[1] // 2
    here_row = position()[0]
    for which in range(2):
        other = lax.rem(here_row + (rows_n - 1, 1)[which], rows_n)
        start = pl.multiple_of((here_row ^ other) * depth, 8)
        lines = halos[pl.ds(start, depth), :]
        for tile in range(halo_tiles):
            places = [(which * 9 + word) * halo_tiles + tile for word in range(9)]
            store_words(table, which * halo_tiles + tile, [lines[place : place + 1] for place in places])

    sources = [(tile, own_table, tile) for tile in range(first, own_tiles)]
    sources = sources + [(own_tiles + tile, table, tile) for tile in range(2 * halo_tiles)]

    def one_tile(tile, carry):
        span = pl.ds(pl.multiple_of(tile * LANES, LANES), LANES)
        lines = sites[:, span]
        own = []
        for word in range(9):
            line = jnp.broadcast_to(lines[word : word + 1] * SCALE + SHIFT * SCALE, (8, LANES))
            own.append((line, line - 32768.0))
        near = [jnp.zeros((8, LANES), F32) for _ in range(9)]
        far = [jnp.zeros((8, LANES), F32) for _ in range(9)]
        for pair in range(slots // 16):
            starts = [16 * pair + 8 * part for part in range(2)]
            found = [
                [own_words[word * slots + start : word * slots + start + 8, span] for start in starts]
                for word in range(5)
            ]
            index = [neighbours[start : start + 8, span] for start in starts]
            found = gather_words(sources, index, found)
            for part in range(2):
                places = []
                for word in range(9):
                    value = found[word // 2][part]
                    if word == 8:
                        places.append(value.astype(F32))
                    elif word % 2 == 0:
                        places.append((value & 65535).astype(F32))
                    else:
                        places.append((value >> 16).astype(F32))
                for source in range(3):
                    for target in range(3):
                        gap = []
                        for compo in range(3):
                            mine, other = 3 * source + compo, 3 * target + compo
                            gap.append(own[mine][other % 2] - places[other])
                        root = lax.rsqrt(
                            gap[0] * gap[0] + gap[1] * gap[1] + gap[2] * gap[2] + SOFTEN * SCALE * SCALE
                        )
                        weight = root * root * root
                        sums = near if target == 0 else far
                        for compo in range(3):
                            sums[3 * source + compo] = sums[3 * source + compo] + gap[compo] * weight
        for place in range(9):
            factor = CHARGE[place // 3] * UNIT * SCALE * SCALE
            total = factor * (far[place] - 2.0 * near[place])
            force[place : place + 1, span] = jnp.sum(total, axis=0, keepdims=True)
        return carry

    lax.fori_loop(0, own_tiles, one_tile, 0)


def pattern_flags(message, place):
    line = jnp.broadcast_to(message[pl.ds(place, 1), :], (8, LANES))
    return lambda block: pick(line, jnp.full((8, LANES), block, jnp.int32))[0:1].astype(BF16)


def field_kernel(ways, hist_rows, block_rows, summed, message, *refs):
    dens, out, masked, lines = refs[:ways], refs[ways + 1], refs[ways + 2], refs[ways + 3]
    rows, cols = dens[0].shape
    rows_b, cols_b = rows // BLOCK, cols // BLOCK
    depth = (message.shape[0] - summed) // ways
    here_row, here_col = position()
    result = jnp.zeros((16, rows), F32)
    lines[...] = jnp.zeros(lines.shape, F32)
    for step in range(ways):
        device = here_col ^ step
        flag = pattern_flags(message, hist_rows + 3 * rows_b + device)
        for col in range(cols_b):
            other = device * (cols_b // rows_b) + col // rows_b
            place = hist_rows + (here_row ^ other) * block_rows + line_of(col % rows_b, 0)
            start = summed + step * depth + 3 * col
            moment = message[start : start + 3, :]
            pot = UNIT * COUPLE * message[pl.ds(device * cols_b + col, 1), :]
            for comp in range(3):
                product = message[pl.ds(place + comp, 1), :]
                lines[comp : comp + 1, at(col)] = product + pot * moment[comp : comp + 1]
            lines[3:6, at(col)] = moment
            for row in range(rows_b):
                spot = slice(row * BLOCK, (row + 1) * BLOCK)
                target = slice(step * cols + col * BLOCK, step * cols + (col + 1) * BLOCK)
                masked[spot, target] = dens[step][spot, at(col)] * flag(rows_b * cols_b + row * cols_b + col)
        whole = lines[...]
        first = whole.astype(BF16).astype(F32)
        both = jnp.concatenate([first, whole - first], axis=0).astype(BF16)
        result = result + contract(both, masked[:, step * cols : (step + 1) * cols], ((1,), (1,)))
    total = result[0:8] + result[8:16]
    out[...] = jnp.zeros(out.shape, F32)
    for row in range(rows_b):
        pot = UNIT * COUPLE * message[pl.ds(here_row * rows_b + row, 1), :]
        start = line_of(row, 0)
        out[start : start + 3, :] = total[0:3, at(row)] + pot * total[3:6, at(row)]


def advance_kernel(
    rows_n,
    rows_b,
    fields,
    owner,
    sites,
    quat,
    pair,
    centres,
    velocity,
    angmom,
    centres_new,
    velocity_new,
    angmom_new,
    orient_new,
    force,
    table,
):
    waters = owner.shape[1]
    depth = fields.shape[0] // rows_n
    here_row = position()[0]
    table[...] = jnp.zeros(table.shape, F32)
    for step in range(rows_n):
        for row in range(rows_b):
            start = step * depth + line_of(row, 0)
            place = 4 * (step * rows_b + row)
            table[place : place + 3, :] = fields[start : start + 3, :]
    for tile in range(waters // LANES):
        for source in range(3):
            index = jnp.broadcast_to(owner[source : source + 1, at(tile)], (8, LANES))
            low, high = index & 127, index >> 7
            found = jnp.zeros((8, LANES), F32)
            for step in range(rows_n):
                base = (here_row ^ step) * (rows_b // 2)
                for two in range(rows_b // 2):
                    place = 8 * (step * (rows_b // 2) + two)
                    value = pick(table[place : place + 8, :], low)
                    found = jnp.where((high >> 1) == base + two, value, found)
            odd = (high[0:3] & 1) == 1
            found = jnp.where(odd, found[4:7], found[0:3])
            lines = slice(3 * source, 3 * source + 3)
            force[lines, at(tile)] = pair[lines, at(tile)] + CHARGE[source] * found

    def cross(left, right):
        return [
            left[1] * right[2] - left[2] * right[1],
            left[2] * right[0] - left[0] * right[2],
            left[0] * right[1] - left[1] * right[0],
        ]

    def split(array):
        return [array[compo : compo + 1, :] for compo in range(3)]

    total = force[0:3, :] + force[3:6, :] + force[6:9, :]
    torque = None
    centre = split(centres)
    for source in range(3):
        lever = [sites[3 * source + compo : 3 * source + compo + 1, :] - centre[compo] for compo in range(3)]
        push = [force[3 * source + compo : 3 * source + compo + 1, :] for compo in range(3)]
        turn = cross(lever, push)
        torque = turn if torque is None else [old + new for old, new in zip(torque, turn)]
    moving = velocity[...] + STEP_DT * total / WATER_MASS
    velocity_new[...] = moving
    centres_new[...] = centres[...] + STEP_DT * moving
    spin = [angmom[compo : compo + 1, :] + STEP_DT * torque[compo] for compo in range(3)]
    for compo in range(3):
        angmom_new[compo : compo + 1, :] = spin[compo]
    omega = [value * (1.0 / INERTIA) for value in spin]
    scalar = quat[0:1, :]
    vector = [quat[compo + 1 : compo + 2, :] for compo in range(3)]
    delta = [-(omega[0] * vector[0] + omega[1] * vector[1] + omega[2] * vector[2])]
    turned = cross(omega, vector)
    delta = delta + [scalar * omega[compo] + turned[compo] for compo in range(3)]
    moved = [old + 0.5 * STEP_DT * new for old, new in zip([scalar] + vector, delta)]
    length = jnp.sqrt(moved[0] * moved[0] + moved[1] * moved[1] + moved[2] * moved[2] + moved[3] * moved[3])
    for place in range(4):
        orient_new[place : place + 1, :] = moved[place] / length


def product_kernel(steps, hist_rows, block_rows, message, dens, *refs):
    count = len(steps)
    small, before = refs[:count], refs[count:-2]
    out, panel = refs[-2:]
    rows, cols = out.shape
    rows_b, cols_b = rows // BLOCK, cols // BLOCK
    here_row, here_col = position()
    spans = []
    for place, step in enumerate(steps):
        other = here_row ^ step
        base = (here_col ^ (other * rows // cols)) * cols + lax.rem(other * rows, cols)
        spans.append(pl.ds(pl.multiple_of(base, BLOCK), rows))
        flag = pattern_flags(message, hist_rows + step * block_rows + 3 * rows_b + here_col)
        for row in range(rows_b):
            block = small[place][row * BLOCK : (row + 1) * BLOCK, :]
            for col in range(cols_b):
                panel[place, row * BLOCK : (row + 1) * BLOCK, at(col)] = block * flag(row * cols_b + col)

    chunk = 2 * BLOCK
    for part in range(rows // chunk):
        lines = slice(part * chunk, (part + 1) * chunk)
        value = contract(dens[lines, spans[0]], panel[0], ((1,), (0,)))
        for place in range(1, count):
            value = value + contract(dens[lines, spans[place]], panel[place], ((1,), (0,)))
        if before:
            out[lines, :] = (value + before[0][lines, :]).astype(out.dtype)
            continue
        for half in range(2):
            row = 2 * part + half
            lines = slice(row * BLOCK, (row + 1) * BLOCK)
            own = UNIT * COUPLE * message[pl.ds(here_row * rows_b + row, 1), :]
            across = jnp.transpose(jnp.broadcast_to(own, (BLOCK, BLOCK)))
            for col in range(cols_b):
                pot = UNIT * COUPLE * message[pl.ds(here_col * cols_b + col, 1), :]
                sums = (across + pot) * dens[lines, at(col)].astype(F32)
                out[lines, at(col)] = (value[half * BLOCK : (half + 1) * BLOCK, at(col)] + sums).astype(out.dtype)


def tie_kernel(first, second, out):
    pass


VMEM = pl.BlockSpec(memory_space=pltpu.VMEM)
SMEM = pl.BlockSpec(memory_space=pltpu.SMEM)


def fetching(kernel, places, *refs):
    refs, semaphore = list(refs[:-1]), refs[-1]
    held = refs[len(refs) - len(places) :]
    copies = [pltpu.make_async_copy(refs[at_], held[n], semaphore.at[n]) for n, at_ in enumerate(places)]
    for copy in copies:
        copy.start()
    for copy in copies:
        copy.wait()
    for n, at_ in enumerate(places):
        refs[at_] = held[n]
    kernel(*refs[: len(refs) - len(places)])


def call(
    kernel, name, outs, operands, scalars=0, scratch=(), cost=(0, 0), whole=VMEM, fetch=(), unread=(), limit=48 << 20, **more
):
    in_specs = [SMEM] * scalars + [whole] * (len(operands) - scalars)
    scratch = list(scratch)
    for place in unread:
        in_specs[place] = pl.BlockSpec(memory_space=pl.ANY)
    if fetch:
        for place in fetch:
            memory = pltpu.SMEM if place < scalars else pltpu.VMEM
            scratch.append(memory(operands[place].shape, operands[place].dtype))
            in_specs[place] = pl.BlockSpec(memory_space=pltpu.HBM)
        scratch.append(pltpu.SemaphoreType.DMA((len(fetch),)))
        kernel = functools.partial(fetching, kernel, tuple(fetch))
    return pl.pallas_call(
        kernel,
        out_shape=[jax.ShapeDtypeStruct(shape, dtype) for shape, dtype in outs],
        in_specs=in_specs,
        out_specs=[whole] * len(outs),
        scratch_shapes=scratch,
        compiler_params=pltpu.CompilerParams(vmem_limit_bytes=limit),
        cost_estimate=pl.CostEstimate(flops=cost[0], bytes_accessed=cost[1], transcendentals=0),
        name=name,
        **more,
    )(*operands)


def doublings(count):
    step = 1
    while step < count:
        yield step
        step = 2 * step


def shards(
    density,
    margin,
    pattern_d,
    pattern_s,
    dipole,
    owner,
    centres,
    angles,
    velocity,
    angmom,
    halo_list,
    neighbours,
):
    rows, cols = density.shape
    rows_b, cols_b = pattern_d.shape
    rows_n = lax.axis_size("row")
    across = ("col", "sub")
    ways = lax.axis_size("col") * lax.axis_size("sub")
    hist_rows = rows * rows_n // LANES
    waters, listed, slots = centres.shape[1], halo_list.shape[1], neighbours.shape[0]
    block_rows = round8(3 * rows_b + ways)
    halo_rows = round8(18 * (listed // LANES))
    summed = hist_rows + rows_n * block_rows
    field_rows = round8(3 * rows_b)
    moment_rows = round8(3 * cols_b)

    def swap(value, axis, count, step):
        return lax.ppermute(value, axis, [(i, i ^ step) for i in range(count)])

    def tie(value, later):
        (value,) = call(
            tie_kernel,
            "tie",
            [(value.shape, value.dtype)],
            [value, later],
            whole=pl.BlockSpec(memory_space=pl.ANY),
            input_output_aliases={0: 0},
        )
        return value

    def merge(first, second, count, done=None):
        total = 2 * first.shape[0] - count
        operands = [first, second] + ([] if done is None else [done])
        (out,) = call(
            functools.partial(merge_kernel, count),
            "merge",
            [((total, LANES), F32)],
            operands,
            unread=range(2, len(operands)),
        )
        return out

    def send(value, axis, count):
        held = [value] + [None] * (count - 1)
        for step in doublings(count):
            held[step] = swap(value, axis, count, step)
        return held

    def relay(held, axis, count, later):
        for step in range(1, count):
            lowest = step & -step
            if step != lowest:
                if (step - lowest) & (step - lowest - 1) == 0:
                    held[step - lowest] = tie(held[step - lowest], later)
                held[step] = swap(held[step - lowest], axis, count, lowest)
        return held

    dens_all = send(density, across, ways)
    message, small, again, sites, quat = call(
        functools.partial(open_kernel, ways, hist_rows),
        "open",
        [
            ((hist_rows + block_rows + halo_rows, LANES), F32),
            ((rows, BLOCK), BF16),
            ((rows, BLOCK), BF16),
            ((16, waters), F32),
            ((4, waters), F32),
        ],
        [pattern_d, pattern_s, margin, dipole, owner, centres, angles, halo_list],
        scalars=2,
        cost=(10**6, 12 * 10**6),
        fetch=range(8),
        limit=60 << 20,
    )
    table, moments, held = call(
        prepare_kernel,
        "prepare",
        [
            ((5, waters // LANES, 8, LANES), jnp.int32),
            ((moment_rows, LANES), F32),
            (message.shape, F32),
        ],
        [sites, dipole, message],
    )
    first = -(-5 * (waters // LANES) // 8)
    (found,) = call(
        functools.partial(own_kernel, first),
        "own_gathers",
        [((5 * slots, waters), jnp.int32)],
        [table, neighbours],
        cost=(10**6, 6 * 10**6),
    )
    small_all = [small] + [None] * (rows_n - 1)
    small_all[1] = swap(small, "row", rows_n, 1)
    steps = list(doublings(rows_n))
    for step in steps[:-1]:
        message = merge(held, swap(message, "row", rows_n, step), hist_rows, moments)
        held = message
    later = tie(again, message)
    message, halos = call(
        functools.partial(turn_kernel, hist_rows, block_rows, halo_rows),
        "turn",
        [((summed + moment_rows, LANES), F32), ((rows_n * halo_rows, LANES), F32)],
        [message, swap(message, "row", rows_n, steps[-1]), moments, found],
        unread=(3,),
    )
    for step in steps[1:]:
        small_all[step] = swap(later, "row", rows_n, step)
    dens_all = relay(dens_all, across, ways, message)
    for step in doublings(ways):
        message = merge(message, swap(message, across, ways, step), summed)
    (pair,) = call(
        functools.partial(pair_kernel, rows_n, first),
        "pair_forces",
        [((9, waters), F32)],
        [sites, found, table, halos, neighbours],
        scratch=[pltpu.VMEM((5, 2 * listed // LANES, 8, LANES), jnp.int32)],
        cost=(10**6, 15 * 10**6),
    )
    field, masked = call(
        functools.partial(field_kernel, ways, hist_rows, block_rows, summed),
        "field",
        [((field_rows, LANES), F32), ((rows, ways * cols), BF16)],
        [message] + dens_all + [pair],
        unread=(1 + ways,),
        scratch=[pltpu.VMEM((8, cols), F32)],
        cost=(10**6, 5 * 10**6),
    )
    small_all = relay(small_all, "row", rows_n, field)

    def product(these, kind, before):
        return call(
            functools.partial(product_kernel, these, hist_rows, block_rows),
            "product",
            [((rows, cols), kind)],
            [message, masked] + [small_all[step] for step in these] + before,
            scratch=[pltpu.VMEM((len(these), rows, cols), BF16)],
            cost=(10**6, 10 * 10**6),
        )

    early = [0] + steps[1:]
    late = [step for step in range(rows_n) if step not in early]
    (partial,) = product(early, F32, [])
    (qm_out,) = product(late, BF16, [partial])
    for step in steps:
        field = merge(field, swap(field, "row", rows_n, step), 0, {1: partial, steps[-1]: qm_out}.get(step))
    centres_new, velocity_new, angmom_new, orient_new = call(
        functools.partial(advance_kernel, rows_n, rows_b),
        "advance",
        [((3, waters), F32), ((3, waters), F32), ((3, waters), F32), ((4, waters), F32)],
        [field, owner, sites, quat, pair, centres, velocity, angmom],
        scratch=[pltpu.VMEM((16, waters), F32), pltpu.VMEM((4 * hist_rows, LANES), F32)],
        cost=(10**6, 6 * 10**6),
    )
    return (qm_out, centres_new, velocity_new, angmom_new, orient_new)


def solution(mesh):
    square = P(("groups", "row"), ("col", "sub"))
    spread = P(None, ("groups", "row", "col", "sub"))
    return jax.shard_map(
        shards,
        mesh=mesh,
        in_specs=(square,) * 4 + (P(None, ("groups", "col", "sub")),) + (spread,) * 7,
        out_specs=(square,) + (spread,) * 4,
        check_vma=False,
    )
```

```python
import functools

import jax
import jax.numpy as jnp
from jax import lax
from jax.experimental import pallas as pl
from jax.experimental.pallas import tpu as pltpu
from jax.sharding import PartitionSpec as P

BLOCK = 128
LANES = 128

CHARGE = (-0.834, 0.417, 0.417)
UNIT = 0.417
MULTIPLE = (-2.0, 1.0, 1.0)
OFFSET = ((0.0, 0.0, -0.12), (0.76, 0.0, 0.47), (-0.76, 0.0, 0.47))
COUPLE = 0.1
STEP_DT = 0.5
WATER_MASS = 1.0
INERTIA = 0.5
SOFTEN = 1.0

SHIFT = 1.0
SCALE = 65535.0 / 5.0

F32 = jnp.float32
BF16 = jnp.bfloat16

SIN_TERMS = (-1 / 6, 1 / 120, -1 / 5040, 1 / 362880, -1 / 39916800, 1 / 6227020800)
COS_TERMS = (-1 / 2, 1 / 24, -1 / 720, 1 / 40320, -1 / 3628800, 1 / 479001600, -1 / 87178291200)


def at(tile):
    return slice(tile * LANES, (tile + 1) * LANES)


def position():
    return lax.axis_index("row"), lax.axis_index(("col", "sub"))


def pick(table, index):
    return jnp.take_along_axis(table, index, axis=1, mode="promise_in_bounds")


def contract(left, right, dims):
    return lax.dot_general(left, right, (dims, ((), ())), preferred_element_type=F32)


def series(square, terms):
    total = jnp.full_like(square, terms[-1])
    for term in terms[-2::-1]:
        total = total * square + term
    return total * square + 1.0


def line_of(row, comp):
    return 3 * row + comp


def round8(count):
    return -(-count // 8) * 8


def open_kernel(
    ways,
    hist_rows,
    pat_d,
    pat_s,
    marg,
    dip,
    owner,
    centres,
    angles,
    halo,
    message,
    small,
    again,
    sites,
    quat,
):
    rows_b, cols_b = pat_d.shape
    waters = owner.shape[1]
    here_col = position()[1]
    message[...] = jnp.zeros(message.shape, F32)
    lane = lax.broadcasted_iota(jnp.int32, (1, LANES), 1)
    patterns = jnp.zeros((1, LANES), F32)
    for row in range(rows_b):
        chosen = jnp.int32(0)
        lines = slice(row * BLOCK, (row + 1) * BLOCK)
        for col in range(cols_b):
            chosen = chosen + col * pat_s[row, col]
            line = row * cols_b + col
            patterns = jnp.where(lane == line, pat_s[row, col].astype(F32), patterns)
            patterns = jnp.where(lane == rows_b * cols_b + line, pat_d[row, col].astype(F32), patterns)
        span = pl.ds(pl.multiple_of(chosen * BLOCK, BLOCK), BLOCK)
        block = marg[lines, span]
        for copy in (small, again):
            copy[lines, :] = block
        product = contract(dip[:, span], block, ((1,), (1,)))
        place = hist_rows + line_of(row, 0)
        message[place : place + 3, :] = product
    message[pl.ds(hist_rows + 3 * rows_b + here_col, 1), :] = patterns
    total = jnp.zeros((hist_rows, LANES), F32)
    for source in range(3):
        line = owner[source : source + 1, :]
        high = lax.broadcasted_iota(jnp.int32, (hist_rows, waters), 0) == (line >> 7)
        low = lax.broadcasted_iota(jnp.int32, (LANES, waters), 0) == (line & 127)
        total = total + contract(
            jnp.where(high, MULTIPLE[source], 0.0).astype(BF16),
            jnp.where(low, 1.0, 0.0).astype(BF16),
            ((1,), (1,)),
        )
    message[0:hist_rows, :] = total
    halo_at = hist_rows + round8(3 * rows_b + ways)
    water_sites(centres, angles, halo, sites, quat, message.at[halo_at:, :])


def water_sites(centres, angles, halo, sites, quat, listed):
    half_angle = 0.5 * angles[...]
    square = half_angle * half_angle
    sine = half_angle * series(square, SIN_TERMS)
    cosine = series(square, COS_TERMS)
    sin_r, sin_p, sin_y = sine[0:1], sine[1:2], sine[2:3]
    cos_r, cos_p, cos_y = cosine[0:1], cosine[1:2], cosine[2:3]
    comp_w = cos_r * cos_p * cos_y + sin_r * sin_p * sin_y
    comp_x = sin_r * cos_p * cos_y - cos_r * sin_p * sin_y
    comp_y = cos_r * sin_p * cos_y + sin_r * cos_p * sin_y
    comp_z = cos_r * cos_p * sin_y - sin_r * sin_p * cos_y
    for place, comp in enumerate((comp_w, comp_x, comp_y, comp_z)):
        quat[place : place + 1, :] = comp
    first = (
        1.0 - 2.0 * (comp_y * comp_y + comp_z * comp_z),
        2.0 * (comp_x * comp_y + comp_w * comp_z),
        2.0 * (comp_x * comp_z - comp_w * comp_y),
    )
    third = (
        2.0 * (comp_x * comp_z + comp_w * comp_y),
        2.0 * (comp_y * comp_z - comp_w * comp_x),
        1.0 - 2.0 * (comp_x * comp_x + comp_y * comp_y),
    )
    sites[...] = jnp.zeros(sites.shape, F32)
    for source in range(3):
        for compo in range(3):
            place = 3 * source + compo
            position = centres[compo : compo + 1, :] + third[compo] * OFFSET[source][2]
            if OFFSET[source][0] != 0.0:
                position = position + first[compo] * OFFSET[source][0]
            sites[place : place + 1, :] = position
    waters, tiles = centres.shape[1], halo.shape[1] // LANES
    for which in range(2):
        for tile in range(tiles):
            index = jnp.broadcast_to(halo[which : which + 1, at(tile)], (8, LANES))
            low, high = index & 127, index >> 7
            for part in range(2):
                found = jnp.zeros((8, LANES), F32)
                for source in range(waters // LANES):
                    value = pick(sites[8 * part : 8 * part + 8, at(source)], low)
                    found = jnp.where(high == source, value, found)
                for comp in range(8 * part, min(8 * part + 8, 9)):
                    place = (which * 9 + comp) * tiles + tile
                    listed[place : place + 1, :] = found[comp - 8 * part : comp - 8 * part + 1]


def merge_kernel(summed, first, second, *refs):
    out = refs[-1]
    if summed > 0:
        out[0:summed, :] = first[0:summed, :] + second[0:summed, :]
    count = first.shape[0] - summed
    if count > 0:
        out[summed : summed + count, :] = first[summed:, :]
        out[summed + count :, :] = second[summed:, :]


def turn_kernel(summed, block_rows, halo_rows, first, second, moments, done, out, halos):
    out[0:summed, :] = first[0:summed, :] + second[0:summed, :]
    count = (first.shape[0] - summed) // (block_rows + halo_rows)
    for number, ref in enumerate((first, second)):
        for block in range(count):
            start = summed + block * (block_rows + halo_rows)
            place = number * count + block
            out[summed + place * block_rows : summed + (place + 1) * block_rows, :] = ref[
                start : start + block_rows, :
            ]
            halos[place * halo_rows : (place + 1) * halo_rows, :] = ref[
                start + block_rows : start + block_rows + halo_rows, :
            ]
    out[summed + 2 * count * block_rows :, :] = moments[...]


def store_words(table, tile, lines):
    fixed = [(line * SCALE + (SHIFT * SCALE + 0.5)).astype(jnp.int32) for line in lines]
    for word in range(5):
        value = fixed[2 * word]
        if word < 4:
            value = value | ((fixed[2 * word + 1] - 32768) << 16)
        table[word, tile] = jnp.broadcast_to(value, (8, LANES))


def gather_words(sources, index, found):
    low = [value & 127 for value in index]
    high = [value >> 7 for value in index]
    for number, table, place in sources:
        here = [value == number for value in high]
        for word in range(5):
            line = table[word, place]
            for part in range(len(index)):
                value = pick(line, low[part])
                old = found[word][part]
                found[word][part] = value if old is None else jnp.where(here[part], value, old)
    return found


def prepare_kernel(sites, dip, message, table, moments, held):
    held[...] = message[...]
    moments[...] = jnp.zeros(moments.shape, F32)
    for col in range(dip.shape[1] // BLOCK):
        moments[3 * col : 3 * col + 3, :] = dip[:, at(col)].astype(F32)
    for tile in range(sites.shape[1] // LANES):
        store_words(table, tile, [sites[word : word + 1, at(tile)] for word in range(9)])


def own_kernel(first, table, neighbours, out):
    slots, waters = neighbours.shape
    sources = [(tile, table, tile) for tile in range(first)]

    def one_tile(tile, carry):
        span = pl.ds(pl.multiple_of(tile * LANES, LANES), LANES)
        for pair in range(slots // 16):
            rows = [slice(16 * pair + 8 * part, 16 * pair + 8 * part + 8) for part in range(2)]
            found = gather_words(sources, [neighbours[row, span] for row in rows], [[None, None] for _ in range(5)])
            for word in range(5):
                for part in range(2):
                    start = word * slots + 16 * pair + 8 * part
                    out[start : start + 8, span] = found[word][part]
        return carry

    lax.fori_loop(0, waters // LANES, one_tile, 0)


def pair_kernel(rows_n, first, sites, own_words, own_table, halos, neighbours, force, table):
    waters, slots = sites.shape[1], neighbours.shape[0]
    depth = halos.shape[0] // rows_n
    own_tiles = waters // LANES
    halo_tiles = table.shape[1] // 2
    here_row = position()[0]
    for which in range(2):
        other = lax.rem(here_row + (rows_n - 1, 1)[which], rows_n)
        start = pl.multiple_of((here_row ^ other) * depth, 8)
        lines = halos[pl.ds(start, depth), :]
        for tile in range(halo_tiles):
            places = [(which * 9 + word) * halo_tiles + tile for word in range(9)]
            store_words(table, which * halo_tiles + tile, [lines[place : place + 1] for place in places])

    sources = [(tile, own_table, tile) for tile in range(first, own_tiles)]
    sources = sources + [(own_tiles + tile, table, tile) for tile in range(2 * halo_tiles)]

    def one_tile(tile, carry):
        span = pl.ds(pl.multiple_of(tile * LANES, LANES), LANES)
        lines = sites[:, span]
        own = []
        for word in range(9):
            line = jnp.broadcast_to(lines[word : word + 1] * SCALE + SHIFT * SCALE, (8, LANES))
            own.append((line, line - 32768.0))
        near = [jnp.zeros((8, LANES), F32) for _ in range(9)]
        far = [jnp.zeros((8, LANES), F32) for _ in range(9)]
        for pair in range(slots // 16):
            starts = [16 * pair + 8 * part for part in range(2)]
            found = [
                [own_words[word * slots + start : word * slots + start + 8, span] for start in starts]
                for word in range(5)
            ]
            index = [neighbours[start : start + 8, span] for start in starts]
            found = gather_words(sources, index, found)
            for part in range(2):
                places = []
                for word in range(9):
                    value = found[word // 2][part]
                    if word == 8:
                        places.append(value.astype(F32))
                    elif word % 2 == 0:
                        places.append((value & 65535).astype(F32))
                    else:
                        places.append((value >> 16).astype(F32))
                for source in range(3):
                    for target in range(3):
                        gap = []
                        for compo in range(3):
                            mine, other = 3 * source + compo, 3 * target + compo
                            gap.append(own[mine][other % 2] - places[other])
                        root = lax.rsqrt(
                            gap[0] * gap[0] + gap[1] * gap[1] + gap[2] * gap[2] + SOFTEN * SCALE * SCALE
                        )
                        weight = root * root * root
                        sums = near if target == 0 else far
                        for compo in range(3):
                            sums[3 * source + compo] = sums[3 * source + compo] + gap[compo] * weight
        for place in range(9):
            factor = CHARGE[place // 3] * UNIT * SCALE * SCALE
            total = factor * (far[place] - 2.0 * near[place])
            force[place : place + 1, span] = jnp.sum(total, axis=0, keepdims=True)
        return carry

    lax.fori_loop(0, own_tiles, one_tile, 0)


def pattern_flags(message, place):
    line = jnp.broadcast_to(message[pl.ds(place, 1), :], (8, LANES))
    return lambda block: pick(line, jnp.full((8, LANES), block, jnp.int32))[0:1].astype(BF16)


def field_kernel(ways, hist_rows, block_rows, summed, message, *refs):
    dens, out, masked, lines = refs[:ways], refs[ways + 1], refs[ways + 2], refs[ways + 3]
    rows, cols = dens[0].shape
    rows_b, cols_b = rows // BLOCK, cols // BLOCK
    depth = (message.shape[0] - summed) // ways
    here_row, here_col = position()
    result = jnp.zeros((16, rows), F32)
    lines[...] = jnp.zeros(lines.shape, F32)
    for step in range(ways):
        device = here_col ^ step
        flag = pattern_flags(message, hist_rows + 3 * rows_b + device)
        for col in range(cols_b):
            other = device * (cols_b // rows_b) + col // rows_b
            place = hist_rows + (here_row ^ other) * block_rows + line_of(col % rows_b, 0)
            start = summed + step * depth + 3 * col
            moment = message[start : start + 3, :]
            pot = UNIT * COUPLE * message[pl.ds(device * cols_b + col, 1), :]
            for comp in range(3):
                product = message[pl.ds(place + comp, 1), :]
                lines[comp : comp + 1, at(col)] = product + pot * moment[comp : comp + 1]
            lines[3:6, at(col)] = moment
            for row in range(rows_b):
                spot = slice(row * BLOCK, (row + 1) * BLOCK)
                target = slice(step * cols + col * BLOCK, step * cols + (col + 1) * BLOCK)
                masked[spot, target] = dens[step][spot, at(col)] * flag(rows_b * cols_b + row * cols_b + col)
        whole = lines[...]
        first = whole.astype(BF16).astype(F32)
        both = jnp.concatenate([first, whole - first], axis=0).astype(BF16)
        result = result + contract(both, masked[:, step * cols : (step + 1) * cols], ((1,), (1,)))
    total = result[0:8] + result[8:16]
    out[...] = jnp.zeros(out.shape, F32)
    for row in range(rows_b):
        pot = UNIT * COUPLE * message[pl.ds(here_row * rows_b + row, 1), :]
        start = line_of(row, 0)
        out[start : start + 3, :] = total[0:3, at(row)] + pot * total[3:6, at(row)]


def advance_kernel(
    rows_n,
    rows_b,
    fields,
    owner,
    sites,
    quat,
    pair,
    centres,
    velocity,
    angmom,
    centres_new,
    velocity_new,
    angmom_new,
    orient_new,
    force,
    table,
):
    waters = owner.shape[1]
    depth = fields.shape[0] // rows_n
    here_row = position()[0]
    table[...] = jnp.zeros(table.shape, F32)
    for step in range(rows_n):
        for row in range(rows_b):
            start = step * depth + line_of(row, 0)
            place = 4 * (step * rows_b + row)
            table[place : place + 3, :] = fields[start : start + 3, :]
    for tile in range(waters // LANES):
        for source in range(3):
            index = jnp.broadcast_to(owner[source : source + 1, at(tile)], (8, LANES))
            low, high = index & 127, index >> 7
            found = jnp.zeros((8, LANES), F32)
            for step in range(rows_n):
                base = (here_row ^ step) * (rows_b // 2)
                for two in range(rows_b // 2):
                    place = 8 * (step * (rows_b // 2) + two)
                    value = pick(table[place : place + 8, :], low)
                    found = jnp.where((high >> 1) == base + two, value, found)
            odd = (high[0:3] & 1) == 1
            found = jnp.where(odd, found[4:7], found[0:3])
            lines = slice(3 * source, 3 * source + 3)
            force[lines, at(tile)] = pair[lines, at(tile)] + CHARGE[source] * found

    def cross(left, right):
        return [
            left[1] * right[2] - left[2] * right[1],
            left[2] * right[0] - left[0] * right[2],
            left[0] * right[1] - left[1] * right[0],
        ]

    def split(array):
        return [array[compo : compo + 1, :] for compo in range(3)]

    total = force[0:3, :] + force[3:6, :] + force[6:9, :]
    torque = None
    centre = split(centres)
    for source in range(3):
        lever = [sites[3 * source + compo : 3 * source + compo + 1, :] - centre[compo] for compo in range(3)]
        push = [force[3 * source + compo : 3 * source + compo + 1, :] for compo in range(3)]
        turn = cross(lever, push)
        torque = turn if torque is None else [old + new for old, new in zip(torque, turn)]
    moving = velocity[...] + STEP_DT * total / WATER_MASS
    velocity_new[...] = moving
    centres_new[...] = centres[...] + STEP_DT * moving
    spin = [angmom[compo : compo + 1, :] + STEP_DT * torque[compo] for compo in range(3)]
    for compo in range(3):
        angmom_new[compo : compo + 1, :] = spin[compo]
    omega = [value * (1.0 / INERTIA) for value in spin]
    scalar = quat[0:1, :]
    vector = [quat[compo + 1 : compo + 2, :] for compo in range(3)]
    delta = [-(omega[0] * vector[0] + omega[1] * vector[1] + omega[2] * vector[2])]
    turned = cross(omega, vector)
    delta = delta + [scalar * omega[compo] + turned[compo] for compo in range(3)]
    moved = [old + 0.5 * STEP_DT * new for old, new in zip([scalar] + vector, delta)]
    length = jnp.sqrt(moved[0] * moved[0] + moved[1] * moved[1] + moved[2] * moved[2] + moved[3] * moved[3])
    for place in range(4):
        orient_new[place : place + 1, :] = moved[place] / length


def product_kernel(steps, hist_rows, block_rows, message, dens, *refs):
    count = len(steps)
    small, before = refs[:count], refs[count:-2]
    out, panel = refs[-2:]
    rows, cols = out.shape
    rows_b, cols_b = rows // BLOCK, cols // BLOCK
    here_row, here_col = position()
    spans = []
    for place, step in enumerate(steps):
        other = here_row ^ step
        base = (here_col ^ (other * rows // cols)) * cols + lax.rem(other * rows, cols)
        spans.append(pl.ds(pl.multiple_of(base, BLOCK), rows))
        flag = pattern_flags(message, hist_rows + step * block_rows + 3 * rows_b + here_col)
        for row in range(rows_b):
            block = small[place][row * BLOCK : (row + 1) * BLOCK, :]
            for col in range(cols_b):
                panel[place, row * BLOCK : (row + 1) * BLOCK, at(col)] = block * flag(row * cols_b + col)

    chunk = 2 * BLOCK
    for part in range(rows // chunk):
        lines = slice(part * chunk, (part + 1) * chunk)
        value = contract(dens[lines, spans[0]], panel[0], ((1,), (0,)))
        for place in range(1, count):
            value = value + contract(dens[lines, spans[place]], panel[place], ((1,), (0,)))
        if before:
            out[lines, :] = (value + before[0][lines, :]).astype(out.dtype)
            continue
        for half in range(2):
            row = 2 * part + half
            lines = slice(row * BLOCK, (row + 1) * BLOCK)
            own = UNIT * COUPLE * message[pl.ds(here_row * rows_b + row, 1), :]
            across = jnp.transpose(jnp.broadcast_to(own, (BLOCK, BLOCK)))
            for col in range(cols_b):
                pot = UNIT * COUPLE * message[pl.ds(here_col * cols_b + col, 1), :]
                sums = (across + pot) * dens[lines, at(col)].astype(F32)
                out[lines, at(col)] = (value[half * BLOCK : (half + 1) * BLOCK, at(col)] + sums).astype(out.dtype)


def tie_kernel(first, second, out):
    pass


VMEM = pl.BlockSpec(memory_space=pltpu.VMEM)
SMEM = pl.BlockSpec(memory_space=pltpu.SMEM)


def fetching(kernel, places, *refs):
    refs, semaphore = list(refs[:-1]), refs[-1]
    held = refs[len(refs) - len(places) :]
    copies = [pltpu.make_async_copy(refs[at_], held[n], semaphore.at[n]) for n, at_ in enumerate(places)]
    for copy in copies:
        copy.start()
    for copy in copies:
        copy.wait()
    for n, at_ in enumerate(places):
        refs[at_] = held[n]
    kernel(*refs[: len(refs) - len(places)])


def call(
    kernel, name, outs, operands, scalars=0, scratch=(), cost=(0, 0), whole=VMEM, fetch=(), unread=(), limit=48 << 20, **more
):
    in_specs = [SMEM] * scalars + [whole] * (len(operands) - scalars)
    scratch = list(scratch)
    for place in unread:
        in_specs[place] = pl.BlockSpec(memory_space=pl.ANY)
    if fetch:
        for place in fetch:
            memory = pltpu.SMEM if place < scalars else pltpu.VMEM
            scratch.append(memory(operands[place].shape, operands[place].dtype))
            in_specs[place] = pl.BlockSpec(memory_space=pltpu.HBM)
        scratch.append(pltpu.SemaphoreType.DMA((len(fetch),)))
        kernel = functools.partial(fetching, kernel, tuple(fetch))
    return pl.pallas_call(
        kernel,
        out_shape=[jax.ShapeDtypeStruct(shape, dtype) for shape, dtype in outs],
        in_specs=in_specs,
        out_specs=[whole] * len(outs),
        scratch_shapes=scratch,
        compiler_params=pltpu.CompilerParams(vmem_limit_bytes=limit),
        cost_estimate=pl.CostEstimate(flops=cost[0], bytes_accessed=cost[1], transcendentals=0),
        name=name,
        **more,
    )(*operands)


def doublings(count):
    step = 1
    while step < count:
        yield step
        step = 2 * step


def shards(
    density,
    margin,
    pattern_d,
    pattern_s,
    dipole,
    owner,
    centres,
    angles,
    velocity,
    angmom,
    halo_list,
    neighbours,
):
    rows, cols = density.shape
    rows_b, cols_b = pattern_d.shape
    rows_n = lax.axis_size("row")
    across = ("col", "sub")
    ways = lax.axis_size("col") * lax.axis_size("sub")
    hist_rows = rows * rows_n // LANES
    waters, listed, slots = centres.shape[1], halo_list.shape[1], neighbours.shape[0]
    block_rows = round8(3 * rows_b + ways)
    halo_rows = round8(18 * (listed // LANES))
    summed = hist_rows + rows_n * block_rows
    field_rows = round8(3 * rows_b)
    moment_rows = round8(3 * cols_b)

    def swap(value, axis, count, step):
        return lax.ppermute(value, axis, [(i, i ^ step) for i in range(count)])

    def tie(value, later):
        (value,) = call(
            tie_kernel,
            "tie",
            [(value.shape, value.dtype)],
            [value, later],
            whole=pl.BlockSpec(memory_space=pl.ANY),
            input_output_aliases={0: 0},
        )
        return value

    def merge(first, second, count, done=None):
        total = 2 * first.shape[0] - count
        operands = [first, second] + ([] if done is None else [done])
        (out,) = call(
            functools.partial(merge_kernel, count),
            "merge",
            [((total, LANES), F32)],
            operands,
            unread=range(2, len(operands)),
        )
        return out

    def send(value, axis, count):
        held = [value] + [None] * (count - 1)
        for step in doublings(count):
            held[step] = swap(value, axis, count, step)
        return held

    def relay(held, axis, count, later):
        for step in range(1, count):
            lowest = step & -step
            if step != lowest:
                if (step - lowest) & (step - lowest - 1) == 0:
                    held[step - lowest] = tie(held[step - lowest], later)
                held[step] = swap(held[step - lowest], axis, count, lowest)
        return held

    dens_all = send(density, across, ways)
    message, small, again, sites, quat = call(
        functools.partial(open_kernel, ways, hist_rows),
        "open",
        [
            ((hist_rows + block_rows + halo_rows, LANES), F32),
            ((rows, BLOCK), BF16),
            ((rows, BLOCK), BF16),
            ((16, waters), F32),
            ((4, waters), F32),
        ],
        [pattern_d, pattern_s, margin, dipole, owner, centres, angles, halo_list],
        scalars=2,
        cost=(10**6, 12 * 10**6),
        fetch=range(8),
        limit=60 << 20,
    )
    table, moments, held = call(
        prepare_kernel,
        "prepare",
        [
            ((5, waters // LANES, 8, LANES), jnp.int32),
            ((moment_rows, LANES), F32),
            (message.shape, F32),
        ],
        [sites, dipole, message],
    )
    first = -(-5 * (waters // LANES) // 8)
    (found,) = call(
        functools.partial(own_kernel, first),
        "own_gathers",
        [((5 * slots, waters), jnp.int32)],
        [table, neighbours],
        cost=(10**6, 6 * 10**6),
    )
    small_all = [small] + [None] * (rows_n - 1)
    small_all[1] = swap(small, "row", rows_n, 1)
    steps = list(doublings(rows_n))
    for step in steps[:-1]:
        message = merge(held, swap(message, "row", rows_n, step), hist_rows, moments)
        held = message
    later = tie(again, message)
    message, halos = call(
        functools.partial(turn_kernel, hist_rows, block_rows, halo_rows),
        "turn",
        [((summed + moment_rows, LANES), F32), ((rows_n * halo_rows, LANES), F32)],
        [message, swap(message, "row", rows_n, steps[-1]), moments, found],
        unread=(3,),
    )
    for step in steps[1:]:
        small_all[step] = swap(later, "row", rows_n, step)
    dens_all = relay(dens_all, across, ways, message)
    for step in doublings(ways):
        message = merge(message, swap(message, across, ways, step), summed)
    (pair,) = call(
        functools.partial(pair_kernel, rows_n, first),
        "pair_forces",
        [((9, waters), F32)],
        [sites, found, table, halos, neighbours],
        scratch=[pltpu.VMEM((5, 2 * listed // LANES, 8, LANES), jnp.int32)],
        cost=(10**6, 15 * 10**6),
    )
    field, masked = call(
        functools.partial(field_kernel, ways, hist_rows, block_rows, summed),
        "field",
        [((field_rows, LANES), F32), ((rows, ways * cols), BF16)],
        [message] + dens_all + [pair],
        unread=(1 + ways,),
        scratch=[pltpu.VMEM((8, cols), F32)],
        cost=(10**6, 5 * 10**6),
    )
    for step in doublings(rows_n):
        field = merge(field, swap(field, "row", rows_n, step), 0)
        if step == 1:
            small_all = relay(small_all, "row", rows_n, field)
    early = [0] + steps[1:]
    late = [step for step in range(rows_n) if step not in early]
    partial, kinds = [], [(early, F32 if late else BF16)] + ([(late, BF16)] if late else [])
    for these, kind in kinds:
        partial = call(
            functools.partial(product_kernel, these, hist_rows, block_rows),
            "product",
            [((rows, cols), kind)],
            [message, masked] + [small_all[step] for step in these] + list(partial),
            scratch=[pltpu.VMEM((len(these), rows, cols), BF16)],
            cost=(10**6, 10 * 10**6),
        )
    (qm_out,) = partial
    centres_new, velocity_new, angmom_new, orient_new = call(
        functools.partial(advance_kernel, rows_n, rows_b),
        "advance",
        [((3, waters), F32), ((3, waters), F32), ((3, waters), F32), ((4, waters), F32)],
        [field, owner, sites, quat, pair, centres, velocity, angmom],
        scratch=[pltpu.VMEM((16, waters), F32), pltpu.VMEM((4 * hist_rows, LANES), F32)],
        cost=(10**6, 6 * 10**6),
    )
    return (qm_out, centres_new, velocity_new, angmom_new, orient_new)


def solution(mesh):
    square = P(("groups", "row"), ("col", "sub"))
    spread = P(None, ("groups", "row", "col", "sub"))
    return jax.shard_map(
        shards,
        mesh=mesh,
        in_specs=(square,) * 4 + (P(None, ("groups", "col", "sub")),) + (spread,) * 7,
        out_specs=(square,) + (spread,) * 4,
        check_vma=False,
    )
```

```python
import functools

import jax
import jax.numpy as jnp
from jax import lax
from jax.experimental import pallas as pl
from jax.experimental.pallas import tpu as pltpu
from jax.sharding import PartitionSpec as P

BLOCK = 128
LANES = 128

CHARGE = (-0.834, 0.417, 0.417)
UNIT = 0.417
MULTIPLE = (-2.0, 1.0, 1.0)
OFFSET = ((0.0, 0.0, -0.12), (0.76, 0.0, 0.47), (-0.76, 0.0, 0.47))
COUPLE = 0.1
STEP_DT = 0.5
WATER_MASS = 1.0
INERTIA = 0.5
SOFTEN = 1.0

SHIFT = 1.0
SCALE = 65535.0 / 5.0

F32 = jnp.float32
BF16 = jnp.bfloat16

SIN_TERMS = (-1 / 6, 1 / 120, -1 / 5040, 1 / 362880, -1 / 39916800, 1 / 6227020800)
COS_TERMS = (-1 / 2, 1 / 24, -1 / 720, 1 / 40320, -1 / 3628800, 1 / 479001600, -1 / 87178291200)


def at(tile):
    return slice(tile * LANES, (tile + 1) * LANES)


def position():
    return lax.axis_index("row"), lax.axis_index(("col", "sub"))


def pick(table, index):
    return jnp.take_along_axis(table, index, axis=1, mode="promise_in_bounds")


def contract(left, right, dims):
    return lax.dot_general(left, right, (dims, ((), ())), preferred_element_type=F32)


def series(square, terms):
    total = jnp.full_like(square, terms[-1])
    for term in terms[-2::-1]:
        total = total * square + term
    return total * square + 1.0


def line_of(row, comp):
    return 3 * row + comp


def round8(count):
    return -(-count // 8) * 8


def open_kernel(
    ways,
    hist_rows,
    pat_d,
    pat_s,
    marg,
    dip,
    owner,
    centres,
    angles,
    halo,
    message,
    small,
    again,
    sites,
    quat,
):
    rows_b, cols_b = pat_d.shape
    waters = owner.shape[1]
    here_col = position()[1]
    message[...] = jnp.zeros(message.shape, F32)
    lane = lax.broadcasted_iota(jnp.int32, (1, LANES), 1)
    patterns = jnp.zeros((1, LANES), F32)
    for row in range(rows_b):
        chosen = jnp.int32(0)
        lines = slice(row * BLOCK, (row + 1) * BLOCK)
        for col in range(cols_b):
            chosen = chosen + col * pat_s[row, col]
            line = row * cols_b + col
            patterns = jnp.where(lane == line, pat_s[row, col].astype(F32), patterns)
            patterns = jnp.where(lane == rows_b * cols_b + line, pat_d[row, col].astype(F32), patterns)
        span = pl.ds(pl.multiple_of(chosen * BLOCK, BLOCK), BLOCK)
        block = marg[lines, span]
        for copy in (small, again):
            copy[lines, :] = block
        product = contract(dip[:, span], block, ((1,), (1,)))
        place = hist_rows + line_of(row, 0)
        message[place : place + 3, :] = product
    message[pl.ds(hist_rows + 3 * rows_b + here_col, 1), :] = patterns
    total = jnp.zeros((hist_rows, LANES), F32)
    for source in range(3):
        line = owner[source : source + 1, :]
        high = lax.broadcasted_iota(jnp.int32, (hist_rows, waters), 0) == (line >> 7)
        low = lax.broadcasted_iota(jnp.int32, (LANES, waters), 0) == (line & 127)
        total = total + contract(
            jnp.where(high, MULTIPLE[source], 0.0).astype(BF16),
            jnp.where(low, 1.0, 0.0).astype(BF16),
            ((1,), (1,)),
        )
    message[0:hist_rows, :] = total
    halo_at = hist_rows + round8(3 * rows_b + ways)
    water_sites(centres, angles, halo, sites, quat, message.at[halo_at:, :])


def water_sites(centres, angles, halo, sites, quat, listed):
    half_angle = 0.5 * angles[...]
    square = half_angle * half_angle
    sine = half_angle * series(square, SIN_TERMS)
    cosine = series(square, COS_TERMS)
    sin_r, sin_p, sin_y = sine[0:1], sine[1:2], sine[2:3]
    cos_r, cos_p, cos_y = cosine[0:1], cosine[1:2], cosine[2:3]
    comp_w = cos_r * cos_p * cos_y + sin_r * sin_p * sin_y
    comp_x = sin_r * cos_p * cos_y - cos_r * sin_p * sin_y
    comp_y = cos_r * sin_p * cos_y + sin_r * cos_p * sin_y
    comp_z = cos_r * cos_p * sin_y - sin_r * sin_p * cos_y
    for place, comp in enumerate((comp_w, comp_x, comp_y, comp_z)):
        quat[place : place + 1, :] = comp
    first = (
        1.0 - 2.0 * (comp_y * comp_y + comp_z * comp_z),
        2.0 * (comp_x * comp_y + comp_w * comp_z),
        2.0 * (comp_x * comp_z - comp_w * comp_y),
    )
    third = (
        2.0 * (comp_x * comp_z + comp_w * comp_y),
        2.0 * (comp_y * comp_z - comp_w * comp_x),
        1.0 - 2.0 * (comp_x * comp_x + comp_y * comp_y),
    )
    sites[...] = jnp.zeros(sites.shape, F32)
    for source in range(3):
        for compo in range(3):
            place = 3 * source + compo
            position = centres[compo : compo + 1, :] + third[compo] * OFFSET[source][2]
            if OFFSET[source][0] != 0.0:
                position = position + first[compo] * OFFSET[source][0]
            sites[place : place + 1, :] = position
    waters, tiles = centres.shape[1], halo.shape[1] // LANES
    for which in range(2):
        for tile in range(tiles):
            index = jnp.broadcast_to(halo[which : which + 1, at(tile)], (8, LANES))
            low, high = index & 127, index >> 7
            for part in range(2):
                found = jnp.zeros((8, LANES), F32)
                for source in range(waters // LANES):
                    value = pick(sites[8 * part : 8 * part + 8, at(source)], low)
                    found = jnp.where(high == source, value, found)
                for comp in range(8 * part, min(8 * part + 8, 9)):
                    place = (which * 9 + comp) * tiles + tile
                    listed[place : place + 1, :] = found[comp - 8 * part : comp - 8 * part + 1]


def merge_kernel(summed, first, second, *refs):
    out = refs[-1]
    if summed > 0:
        out[0:summed, :] = first[0:summed, :] + second[0:summed, :]
    count = first.shape[0] - summed
    if count > 0:
        out[summed : summed + count, :] = first[summed:, :]
        out[summed + count :, :] = second[summed:, :]


def turn_kernel(summed, block_rows, halo_rows, first, second, moments, done, out, halos):
    out[0:summed, :] = first[0:summed, :] + second[0:summed, :]
    count = (first.shape[0] - summed) // (block_rows + halo_rows)
    for number, ref in enumerate((first, second)):
        for block in range(count):
            start = summed + block * (block_rows + halo_rows)
            place = number * count + block
            out[summed + place * block_rows : summed + (place + 1) * block_rows, :] = ref[
                start : start + block_rows, :
            ]
            halos[place * halo_rows : (place + 1) * halo_rows, :] = ref[
                start + block_rows : start + block_rows + halo_rows, :
            ]
    out[summed + 2 * count * block_rows :, :] = moments[...]


def store_words(table, tile, lines):
    fixed = [(line * SCALE + (SHIFT * SCALE + 0.5)).astype(jnp.int32) for line in lines]
    for word in range(5):
        value = fixed[2 * word]
        if word < 4:
            value = value | ((fixed[2 * word + 1] - 32768) << 16)
        table[word, tile] = jnp.broadcast_to(value, (8, LANES))


def gather_words(sources, index, found):
    low = [value & 127 for value in index]
    high = [value >> 7 for value in index]
    for number, table, place in sources:
        here = [value == number for value in high]
        for word in range(5):
            line = table[word, place]
            for part in range(len(index)):
                value = pick(line, low[part])
                old = found[word][part]
                found[word][part] = value if old is None else jnp.where(here[part], value, old)
    return found


def prepare_kernel(sites, dip, message, table, moments, held):
    held[...] = message[...]
    moments[...] = jnp.zeros(moments.shape, F32)
    for col in range(dip.shape[1] // BLOCK):
        moments[3 * col : 3 * col + 3, :] = dip[:, at(col)].astype(F32)
    for tile in range(sites.shape[1] // LANES):
        store_words(table, tile, [sites[word : word + 1, at(tile)] for word in range(9)])


def own_kernel(first, table, neighbours, out):
    slots, waters = neighbours.shape
    sources = [(tile, table, tile) for tile in range(first)]

    def one_tile(tile, carry):
        span = pl.ds(pl.multiple_of(tile * LANES, LANES), LANES)
        for pair in range(slots // 16):
            rows = [slice(16 * pair + 8 * part, 16 * pair + 8 * part + 8) for part in range(2)]
            found = gather_words(sources, [neighbours[row, span] for row in rows], [[None, None] for _ in range(5)])
            for word in range(5):
                for part in range(2):
                    start = word * slots + 16 * pair + 8 * part
                    out[start : start + 8, span] = found[word][part]
        return carry

    lax.fori_loop(0, waters // LANES, one_tile, 0)


def pair_kernel(rows_n, first, sites, own_words, own_table, halos, neighbours, force, table):
    waters, slots = sites.shape[1], neighbours.shape[0]
    depth = halos.shape[0] // rows_n
    own_tiles = waters // LANES
    halo_tiles = table.shape[1] // 2
    here_row = position()[0]
    for which in range(2):
        other = lax.rem(here_row + (rows_n - 1, 1)[which], rows_n)
        start = pl.multiple_of((here_row ^ other) * depth, 8)
        lines = halos[pl.ds(start, depth), :]
        for tile in range(halo_tiles):
            places = [(which * 9 + word) * halo_tiles + tile for word in range(9)]
            store_words(table, which * halo_tiles + tile, [lines[place : place + 1] for place in places])

    sources = [(tile, own_table, tile) for tile in range(first, own_tiles)]
    sources = sources + [(own_tiles + tile, table, tile) for tile in range(2 * halo_tiles)]

    def one_tile(tile, carry):
        span = pl.ds(pl.multiple_of(tile * LANES, LANES), LANES)
        lines = sites[:, span]
        own = []
        for word in range(9):
            line = jnp.broadcast_to(lines[word : word + 1] * SCALE + SHIFT * SCALE, (8, LANES))
            own.append((line, line - 32768.0))
        near = [jnp.zeros((8, LANES), F32) for _ in range(9)]
        far = [jnp.zeros((8, LANES), F32) for _ in range(9)]
        for pair in range(slots // 16):
            starts = [16 * pair + 8 * part for part in range(2)]
            found = [
                [own_words[word * slots + start : word * slots + start + 8, span] for start in starts]
                for word in range(5)
            ]
            index = [neighbours[start : start + 8, span] for start in starts]
            found = gather_words(sources, index, found)
            for part in range(2):
                places = []
                for word in range(9):
                    value = found[word // 2][part]
                    if word == 8:
                        places.append(value.astype(F32))
                    elif word % 2 == 0:
                        places.append((value & 65535).astype(F32))
                    else:
                        places.append((value >> 16).astype(F32))
                for source in range(3):
                    for target in range(3):
                        gap = []
                        for compo in range(3):
                            mine, other = 3 * source + compo, 3 * target + compo
                            gap.append(own[mine][other % 2] - places[other])
                        root = lax.rsqrt(
                            gap[0] * gap[0] + gap[1] * gap[1] + gap[2] * gap[2] + SOFTEN * SCALE * SCALE
                        )
                        weight = root * root * root
                        sums = near if target == 0 else far
                        for compo in range(3):
                            sums[3 * source + compo] = sums[3 * source + compo] + gap[compo] * weight
        for place in range(9):
            factor = CHARGE[place // 3] * UNIT * SCALE * SCALE
            total = factor * (far[place] - 2.0 * near[place])
            force[place : place + 1, span] = jnp.sum(total, axis=0, keepdims=True)
        return carry

    lax.fori_loop(0, own_tiles, one_tile, 0)


def pattern_flags(message, place):
    line = jnp.broadcast_to(message[pl.ds(place, 1), :], (8, LANES))
    return lambda block: pick(line, jnp.full((8, LANES), block, jnp.int32))[0:1].astype(BF16)


def field_kernel(ways, hist_rows, block_rows, summed, message, *refs):
    dens, out, masked, lines = refs[:ways], refs[ways + 1], refs[ways + 2], refs[ways + 3]
    rows, cols = dens[0].shape
    rows_b, cols_b = rows // BLOCK, cols // BLOCK
    depth = (message.shape[0] - summed) // ways
    here_row, here_col = position()
    result = jnp.zeros((16, rows), F32)
    lines[...] = jnp.zeros(lines.shape, F32)
    for step in range(ways):
        device = here_col ^ step
        flag = pattern_flags(message, hist_rows + 3 * rows_b + device)
        for col in range(cols_b):
            other = device * (cols_b // rows_b) + col // rows_b
            place = hist_rows + (here_row ^ other) * block_rows + line_of(col % rows_b, 0)
            start = summed + step * depth + 3 * col
            moment = message[start : start + 3, :]
            pot = UNIT * COUPLE * message[pl.ds(device * cols_b + col, 1), :]
            for comp in range(3):
                product = message[pl.ds(place + comp, 1), :]
                lines[comp : comp + 1, at(col)] = product + pot * moment[comp : comp + 1]
            lines[3:6, at(col)] = moment
            for row in range(rows_b):
                spot = slice(row * BLOCK, (row + 1) * BLOCK)
                target = slice(step * cols + col * BLOCK, step * cols + (col + 1) * BLOCK)
                masked[spot, target] = dens[step][spot, at(col)] * flag(rows_b * cols_b + row * cols_b + col)
        whole = lines[...]
        first = whole.astype(BF16).astype(F32)
        both = jnp.concatenate([first, whole - first], axis=0).astype(BF16)
        result = result + contract(both, masked[:, step * cols : (step + 1) * cols], ((1,), (1,)))
    total = result[0:8] + result[8:16]
    out[...] = jnp.zeros(out.shape, F32)
    for row in range(rows_b):
        pot = UNIT * COUPLE * message[pl.ds(here_row * rows_b + row, 1), :]
        start = line_of(row, 0)
        out[start : start + 3, :] = total[0:3, at(row)] + pot * total[3:6, at(row)]


def advance_kernel(
    rows_n,
    rows_b,
    fields,
    owner,
    sites,
    quat,
    pair,
    centres,
    velocity,
    angmom,
    centres_new,
    velocity_new,
    angmom_new,
    orient_new,
    force,
    table,
):
    waters = owner.shape[1]
    depth = fields.shape[0] // rows_n
    here_row = position()[0]
    table[...] = jnp.zeros(table.shape, F32)
    for step in range(rows_n):
        for row in range(rows_b):
            start = step * depth + line_of(row, 0)
            place = 4 * (step * rows_b + row)
            table[place : place + 3, :] = fields[start : start + 3, :]
    for tile in range(waters // LANES):
        for source in range(3):
            index = jnp.broadcast_to(owner[source : source + 1, at(tile)], (8, LANES))
            low, high = index & 127, index >> 7
            found = jnp.zeros((8, LANES), F32)
            for step in range(rows_n):
                base = (here_row ^ step) * (rows_b // 2)
                for two in range(rows_b // 2):
                    place = 8 * (step * (rows_b // 2) + two)
                    value = pick(table[place : place + 8, :], low)
                    found = jnp.where((high >> 1) == base + two, value, found)
            odd = (high[0:3] & 1) == 1
            found = jnp.where(odd, found[4:7], found[0:3])
            lines = slice(3 * source, 3 * source + 3)
            force[lines, at(tile)] = pair[lines, at(tile)] + CHARGE[source] * found

    def cross(left, right):
        return [
            left[1] * right[2] - left[2] * right[1],
            left[2] * right[0] - left[0] * right[2],
            left[0] * right[1] - left[1] * right[0],
        ]

    def split(array):
        return [array[compo : compo + 1, :] for compo in range(3)]

    total = force[0:3, :] + force[3:6, :] + force[6:9, :]
    torque = None
    centre = split(centres)
    for source in range(3):
        lever = [sites[3 * source + compo : 3 * source + compo + 1, :] - centre[compo] for compo in range(3)]
        push = [force[3 * source + compo : 3 * source + compo + 1, :] for compo in range(3)]
        turn = cross(lever, push)
        torque = turn if torque is None else [old + new for old, new in zip(torque, turn)]
    moving = velocity[...] + STEP_DT * total / WATER_MASS
    velocity_new[...] = moving
    centres_new[...] = centres[...] + STEP_DT * moving
    spin = [angmom[compo : compo + 1, :] + STEP_DT * torque[compo] for compo in range(3)]
    for compo in range(3):
        angmom_new[compo : compo + 1, :] = spin[compo]
    omega = [value * (1.0 / INERTIA) for value in spin]
    scalar = quat[0:1, :]
    vector = [quat[compo + 1 : compo + 2, :] for compo in range(3)]
    delta = [-(omega[0] * vector[0] + omega[1] * vector[1] + omega[2] * vector[2])]
    turned = cross(omega, vector)
    delta = delta + [scalar * omega[compo] + turned[compo] for compo in range(3)]
    moved = [old + 0.5 * STEP_DT * new for old, new in zip([scalar] + vector, delta)]
    length = jnp.sqrt(moved[0] * moved[0] + moved[1] * moved[1] + moved[2] * moved[2] + moved[3] * moved[3])
    for place in range(4):
        orient_new[place : place + 1, :] = moved[place] / length


def product_kernel(steps, hist_rows, block_rows, message, dens, *refs):
    count = len(steps)
    small, before = refs[:count], refs[count:-2]
    out, panel = refs[-2:]
    rows, cols = out.shape
    rows_b, cols_b = rows // BLOCK, cols // BLOCK
    here_row, here_col = position()
    spans = []
    for place, step in enumerate(steps):
        other = here_row ^ step
        base = (here_col ^ (other * rows // cols)) * cols + lax.rem(other * rows, cols)
        spans.append(pl.ds(pl.multiple_of(base, BLOCK), rows))
        flag = pattern_flags(message, hist_rows + step * block_rows + 3 * rows_b + here_col)
        for row in range(rows_b):
            block = small[place][row * BLOCK : (row + 1) * BLOCK, :]
            for col in range(cols_b):
                panel[place, row * BLOCK : (row + 1) * BLOCK, at(col)] = block * flag(row * cols_b + col)

    chunk = 2 * BLOCK
    for part in range(rows // chunk):
        lines = slice(part * chunk, (part + 1) * chunk)
        value = contract(dens[lines, spans[0]], panel[0], ((1,), (0,)))
        for place in range(1, count):
            value = value + contract(dens[lines, spans[place]], panel[place], ((1,), (0,)))
        if before:
            out[lines, :] = (value + before[0][lines, :]).astype(out.dtype)
            continue
        for half in range(2):
            row = 2 * part + half
            lines = slice(row * BLOCK, (row + 1) * BLOCK)
            own = UNIT * COUPLE * message[pl.ds(here_row * rows_b + row, 1), :]
            across = jnp.transpose(jnp.broadcast_to(own, (BLOCK, BLOCK)))
            for col in range(cols_b):
                pot = UNIT * COUPLE * message[pl.ds(here_col * cols_b + col, 1), :]
                sums = (across + pot) * dens[lines, at(col)].astype(F32)
                out[lines, at(col)] = (value[half * BLOCK : (half + 1) * BLOCK, at(col)] + sums).astype(out.dtype)


def tie_kernel(first, second, out):
    pass


VMEM = pl.BlockSpec(memory_space=pltpu.VMEM)
SMEM = pl.BlockSpec(memory_space=pltpu.SMEM)


def fetching(kernel, places, *refs):
    refs, semaphore = list(refs[:-1]), refs[-1]
    held = refs[len(refs) - len(places) :]
    copies = [pltpu.make_async_copy(refs[at_], held[n], semaphore.at[n]) for n, at_ in enumerate(places)]
    for copy in copies:
        copy.start()
    for copy in copies:
        copy.wait()
    for n, at_ in enumerate(places):
        refs[at_] = held[n]
    kernel(*refs[: len(refs) - len(places)])


def call(
    kernel, name, outs, operands, scalars=0, scratch=(), cost=(0, 0), whole=VMEM, fetch=(), unread=(), limit=48 << 20, **more
):
    in_specs = [SMEM] * scalars + [whole] * (len(operands) - scalars)
    scratch = list(scratch)
    for place in unread:
        in_specs[place] = pl.BlockSpec(memory_space=pl.ANY)
    if fetch:
        for place in fetch:
            memory = pltpu.SMEM if place < scalars else pltpu.VMEM
            scratch.append(memory(operands[place].shape, operands[place].dtype))
            in_specs[place] = pl.BlockSpec(memory_space=pltpu.HBM)
        scratch.append(pltpu.SemaphoreType.DMA((len(fetch),)))
        kernel = functools.partial(fetching, kernel, tuple(fetch))
    return pl.pallas_call(
        kernel,
        out_shape=[jax.ShapeDtypeStruct(shape, dtype) for shape, dtype in outs],
        in_specs=in_specs,
        out_specs=[whole] * len(outs),
        scratch_shapes=scratch,
        compiler_params=pltpu.CompilerParams(vmem_limit_bytes=limit),
        cost_estimate=pl.CostEstimate(flops=cost[0], bytes_accessed=cost[1], transcendentals=0),
        name=name,
        **more,
    )(*operands)


def doublings(count):
    step = 1
    while step < count:
        yield step
        step = 2 * step


def shards(
    density,
    margin,
    pattern_d,
    pattern_s,
    dipole,
    owner,
    centres,
    angles,
    velocity,
    angmom,
    halo_list,
    neighbours,
):
    rows, cols = density.shape
    rows_b, cols_b = pattern_d.shape
    rows_n = lax.axis_size("row")
    across = ("col", "sub")
    ways = lax.axis_size("col") * lax.axis_size("sub")
    hist_rows = rows * rows_n // LANES
    waters, listed, slots = centres.shape[1], halo_list.shape[1], neighbours.shape[0]
    block_rows = round8(3 * rows_b + ways)
    halo_rows = round8(18 * (listed // LANES))
    summed = hist_rows + rows_n * block_rows
    field_rows = round8(3 * rows_b)
    moment_rows = round8(3 * cols_b)

    def swap(value, axis, count, step):
        return lax.ppermute(value, axis, [(i, i ^ step) for i in range(count)])

    def tie(value, later):
        (value,) = call(
            tie_kernel,
            "tie",
            [(value.shape, value.dtype)],
            [value, later],
            whole=pl.BlockSpec(memory_space=pl.ANY),
            input_output_aliases={0: 0},
        )
        return value

    def merge(first, second, count, done=None):
        total = 2 * first.shape[0] - count
        operands = [first, second] + ([] if done is None else [done])
        (out,) = call(
            functools.partial(merge_kernel, count),
            "merge",
            [((total, LANES), F32)],
            operands,
            unread=range(2, len(operands)),
        )
        return out

    def send(value, axis, count):
        held = [value] + [None] * (count - 1)
        for step in doublings(count):
            held[step] = swap(value, axis, count, step)
        return held

    def relay(held, axis, count, later):
        for step in range(1, count):
            lowest = step & -step
            if step != lowest:
                if (step - lowest) & (step - lowest - 1) == 0:
                    held[step - lowest] = tie(held[step - lowest], later)
                held[step] = swap(held[step - lowest], axis, count, lowest)
        return held

    dens_all = send(density, across, ways)
    message, small, again, sites, quat = call(
        functools.partial(open_kernel, ways, hist_rows),
        "open",
        [
            ((hist_rows + block_rows + halo_rows, LANES), F32),
            ((rows, BLOCK), BF16),
            ((rows, BLOCK), BF16),
            ((16, waters), F32),
            ((4, waters), F32),
        ],
        [pattern_d, pattern_s, margin, dipole, owner, centres, angles, halo_list],
        scalars=2,
        cost=(10**6, 12 * 10**6),
        fetch=range(8),
        limit=60 << 20,
    )
    table, moments, held = call(
        prepare_kernel,
        "prepare",
        [
            ((5, waters // LANES, 8, LANES), jnp.int32),
            ((moment_rows, LANES), F32),
            (message.shape, F32),
        ],
        [sites, dipole, message],
    )
    first = -(-5 * (waters // LANES) // 8)
    (found,) = call(
        functools.partial(own_kernel, first),
        "own_gathers",
        [((5 * slots, waters), jnp.int32)],
        [table, neighbours],
        cost=(10**6, 6 * 10**6),
    )
    small_all = [small] + [None] * (rows_n - 1)
    small_all[1] = swap(small, "row", rows_n, 1)
    steps = list(doublings(rows_n))
    for step in steps[:-1]:
        message = merge(held, swap(message, "row", rows_n, step), hist_rows, moments)
        held = message
    later = tie(again, message)
    message, halos = call(
        functools.partial(turn_kernel, hist_rows, block_rows, halo_rows),
        "turn",
        [((summed + moment_rows, LANES), F32), ((rows_n * halo_rows, LANES), F32)],
        [message, swap(message, "row", rows_n, steps[-1]), moments, found],
        unread=(3,),
    )
    for step in steps[1:]:
        small_all[step] = swap(later, "row", rows_n, step)
    dens_all = relay(dens_all, across, ways, message)
    for step in doublings(ways):
        message = merge(message, swap(message, across, ways, step), summed)
    (pair,) = call(
        functools.partial(pair_kernel, rows_n, first),
        "pair_forces",
        [((9, waters), F32)],
        [sites, found, table, halos, neighbours],
        scratch=[pltpu.VMEM((5, 2 * listed // LANES, 8, LANES), jnp.int32)],
        cost=(10**6, 15 * 10**6),
    )
    field, masked = call(
        functools.partial(field_kernel, ways, hist_rows, block_rows, summed),
        "field",
        [((field_rows, LANES), F32), ((rows, ways * cols), BF16)],
        [message] + dens_all + [pair],
        unread=(1 + ways,),
        scratch=[pltpu.VMEM((8, cols), F32)],
        cost=(10**6, 5 * 10**6),
    )
    for step in doublings(rows_n):
        field = merge(field, swap(field, "row", rows_n, step), 0)
        if step == 1:
            small_all = relay(small_all, "row", rows_n, field)
    early = [0] + steps
    late = [step for step in range(rows_n) if step not in early]
    partial, kinds = [], [(early, F32 if late else BF16)] + ([(late, BF16)] if late else [])
    for these, kind in kinds:
        partial = call(
            functools.partial(product_kernel, these, hist_rows, block_rows),
            "product",
            [((rows, cols), kind)],
            [message, masked] + [small_all[step] for step in these] + list(partial),
            scratch=[pltpu.VMEM((len(these), rows, cols), BF16)],
            cost=(10**6, 10 * 10**6),
        )
    (qm_out,) = partial
    centres_new, velocity_new, angmom_new, orient_new = call(
        functools.partial(advance_kernel, rows_n, rows_b),
        "advance",
        [((3, waters), F32), ((3, waters), F32), ((3, waters), F32), ((4, waters), F32)],
        [field, owner, sites, quat, pair, centres, velocity, angmom],
        scratch=[pltpu.VMEM((16, waters), F32), pltpu.VMEM((4 * hist_rows, LANES), F32)],
        cost=(10**6, 6 * 10**6),
    )
    return (qm_out, centres_new, velocity_new, angmom_new, orient_new)


def solution(mesh):
    square = P(("groups", "row"), ("col", "sub"))
    spread = P(None, ("groups", "row", "col", "sub"))
    return jax.shard_map(
        shards,
        mesh=mesh,
        in_specs=(square,) * 4 + (P(None, ("groups", "col", "sub")),) + (spread,) * 7,
        out_specs=(square,) + (spread,) * 4,
        check_vma=False,
    )
```

```python
import functools

import jax
import jax.numpy as jnp
from jax import lax
from jax.experimental import pallas as pl
from jax.experimental.pallas import tpu as pltpu
from jax.sharding import PartitionSpec as P

BLOCK = 128
LANES = 128

CHARGE = (-0.834, 0.417, 0.417)
UNIT = 0.417
MULTIPLE = (-2.0, 1.0, 1.0)
OFFSET = ((0.0, 0.0, -0.12), (0.76, 0.0, 0.47), (-0.76, 0.0, 0.47))
COUPLE = 0.1
STEP_DT = 0.5
WATER_MASS = 1.0
INERTIA = 0.5
SOFTEN = 1.0

SHIFT = 1.0
SCALE = 65535.0 / 5.0

F32 = jnp.float32
BF16 = jnp.bfloat16

SIN_TERMS = (-1 / 6, 1 / 120, -1 / 5040, 1 / 362880, -1 / 39916800, 1 / 6227020800)
COS_TERMS = (-1 / 2, 1 / 24, -1 / 720, 1 / 40320, -1 / 3628800, 1 / 479001600, -1 / 87178291200)


def at(tile):
    return slice(tile * LANES, (tile + 1) * LANES)


def position():
    return lax.axis_index("row"), lax.axis_index(("col", "sub"))


def pick(table, index):
    return jnp.take_along_axis(table, index, axis=1, mode="promise_in_bounds")


def contract(left, right, dims):
    return lax.dot_general(left, right, (dims, ((), ())), preferred_element_type=F32)


def series(square, terms):
    total = jnp.full_like(square, terms[-1])
    for term in terms[-2::-1]:
        total = total * square + term
    return total * square + 1.0


def line_of(row, comp):
    return 3 * row + comp


def round8(count):
    return -(-count // 8) * 8


def open_kernel(
    ways,
    hist_rows,
    pat_d,
    pat_s,
    marg,
    dip,
    owner,
    centres,
    angles,
    halo,
    message,
    small,
    again,
    sites,
    quat,
):
    rows_b, cols_b = pat_d.shape
    waters = owner.shape[1]
    here_col = position()[1]
    message[...] = jnp.zeros(message.shape, F32)
    lane = lax.broadcasted_iota(jnp.int32, (1, LANES), 1)
    patterns = jnp.zeros((1, LANES), F32)
    for row in range(rows_b):
        chosen = jnp.int32(0)
        lines = slice(row * BLOCK, (row + 1) * BLOCK)
        for col in range(cols_b):
            chosen = chosen + col * pat_s[row, col]
            line = row * cols_b + col
            patterns = jnp.where(lane == line, pat_s[row, col].astype(F32), patterns)
            patterns = jnp.where(lane == rows_b * cols_b + line, pat_d[row, col].astype(F32), patterns)
        span = pl.ds(pl.multiple_of(chosen * BLOCK, BLOCK), BLOCK)
        block = marg[lines, span]
        for copy in (small, again):
            copy[lines, :] = block
        product = contract(dip[:, span], block, ((1,), (1,)))
        place = hist_rows + line_of(row, 0)
        message[place : place + 3, :] = product
    message[pl.ds(hist_rows + 3 * rows_b + here_col, 1), :] = patterns
    total = jnp.zeros((hist_rows, LANES), F32)
    for source in range(3):
        line = owner[source : source + 1, :]
        high = lax.broadcasted_iota(jnp.int32, (hist_rows, waters), 0) == (line >> 7)
        low = lax.broadcasted_iota(jnp.int32, (LANES, waters), 0) == (line & 127)
        total = total + contract(
            jnp.where(high, MULTIPLE[source], 0.0).astype(BF16),
            jnp.where(low, 1.0, 0.0).astype(BF16),
            ((1,), (1,)),
        )
    message[0:hist_rows, :] = total
    halo_at = hist_rows + round8(3 * rows_b + ways)
    water_sites(centres, angles, halo, sites, quat, message.at[halo_at:, :])


def water_sites(centres, angles, halo, sites, quat, listed):
    half_angle = 0.5 * angles[...]
    square = half_angle * half_angle
    sine = half_angle * series(square, SIN_TERMS)
    cosine = series(square, COS_TERMS)
    sin_r, sin_p, sin_y = sine[0:1], sine[1:2], sine[2:3]
    cos_r, cos_p, cos_y = cosine[0:1], cosine[1:2], cosine[2:3]
    comp_w = cos_r * cos_p * cos_y + sin_r * sin_p * sin_y
    comp_x = sin_r * cos_p * cos_y - cos_r * sin_p * sin_y
    comp_y = cos_r * sin_p * cos_y + sin_r * cos_p * sin_y
    comp_z = cos_r * cos_p * sin_y - sin_r * sin_p * cos_y
    for place, comp in enumerate((comp_w, comp_x, comp_y, comp_z)):
        quat[place : place + 1, :] = comp
    first = (
        1.0 - 2.0 * (comp_y * comp_y + comp_z * comp_z),
        2.0 * (comp_x * comp_y + comp_w * comp_z),
        2.0 * (comp_x * comp_z - comp_w * comp_y),
    )
    third = (
        2.0 * (comp_x * comp_z + comp_w * comp_y),
        2.0 * (comp_y * comp_z - comp_w * comp_x),
        1.0 - 2.0 * (comp_x * comp_x + comp_y * comp_y),
    )
    sites[...] = jnp.zeros(sites.shape, F32)
    for source in range(3):
        for compo in range(3):
            place = 3 * source + compo
            position = centres[compo : compo + 1, :] + third[compo] * OFFSET[source][2]
            if OFFSET[source][0] != 0.0:
                position = position + first[compo] * OFFSET[source][0]
            sites[place : place + 1, :] = position
    waters, tiles = centres.shape[1], halo.shape[1] // LANES
    for which in range(2):
        for tile in range(tiles):
            index = jnp.broadcast_to(halo[which : which + 1, at(tile)], (8, LANES))
            low, high = index & 127, index >> 7
            for part in range(2):
                found = jnp.zeros((8, LANES), F32)
                for source in range(waters // LANES):
                    value = pick(sites[8 * part : 8 * part + 8, at(source)], low)
                    found = jnp.where(high == source, value, found)
                for comp in range(8 * part, min(8 * part + 8, 9)):
                    place = (which * 9 + comp) * tiles + tile
                    listed[place : place + 1, :] = found[comp - 8 * part : comp - 8 * part + 1]


def merge_kernel(summed, first, second, *refs):
    out = refs[-1]
    if summed > 0:
        out[0:summed, :] = first[0:summed, :] + second[0:summed, :]
    count = first.shape[0] - summed
    if count > 0:
        out[summed : summed + count, :] = first[summed:, :]
        out[summed + count :, :] = second[summed:, :]


def turn_kernel(summed, block_rows, halo_rows, first, second, moments, done, out, halos):
    out[0:summed, :] = first[0:summed, :] + second[0:summed, :]
    count = (first.shape[0] - summed) // (block_rows + halo_rows)
    for number, ref in enumerate((first, second)):
        for block in range(count):
            start = summed + block * (block_rows + halo_rows)
            place = number * count + block
            out[summed + place * block_rows : summed + (place + 1) * block_rows, :] = ref[
                start : start + block_rows, :
            ]
            halos[place * halo_rows : (place + 1) * halo_rows, :] = ref[
                start + block_rows : start + block_rows + halo_rows, :
            ]
    out[summed + 2 * count * block_rows :, :] = moments[...]


def store_words(table, tile, lines):
    fixed = [(line * SCALE + (SHIFT * SCALE + 0.5)).astype(jnp.int32) for line in lines]
    for word in range(5):
        value = fixed[2 * word]
        if word < 4:
            value = value | ((fixed[2 * word + 1] - 32768) << 16)
        table[word, tile] = jnp.broadcast_to(value, (8, LANES))


def gather_words(sources, index, found):
    low = [value & 127 for value in index]
    high = [value >> 7 for value in index]
    for number, table, place in sources:
        here = [value == number for value in high]
        for word in range(5):
            line = table[word, place]
            for part in range(len(index)):
                value = pick(line, low[part])
                old = found[word][part]
                found[word][part] = value if old is None else jnp.where(here[part], value, old)
    return found


def prepare_kernel(sites, dip, message, table, moments, held):
    held[...] = message[...]
    moments[...] = jnp.zeros(moments.shape, F32)
    for col in range(dip.shape[1] // BLOCK):
        moments[3 * col : 3 * col + 3, :] = dip[:, at(col)].astype(F32)
    for tile in range(sites.shape[1] // LANES):
        store_words(table, tile, [sites[word : word + 1, at(tile)] for word in range(9)])


def own_kernel(first, table, neighbours, out):
    slots, waters = neighbours.shape
    sources = [(tile, table, tile) for tile in range(first)]

    def one_tile(tile, carry):
        span = pl.ds(pl.multiple_of(tile * LANES, LANES), LANES)
        for pair in range(slots // 16):
            rows = [slice(16 * pair + 8 * part, 16 * pair + 8 * part + 8) for part in range(2)]
            found = gather_words(sources, [neighbours[row, span] for row in rows], [[None, None] for _ in range(5)])
            for word in range(5):
                for part in range(2):
                    start = word * slots + 16 * pair + 8 * part
                    out[start : start + 8, span] = found[word][part]
        return carry

    lax.fori_loop(0, waters // LANES, one_tile, 0)


def pair_kernel(rows_n, first, sites, own_words, own_table, halos, neighbours, force, table):
    waters, slots = sites.shape[1], neighbours.shape[0]
    depth = halos.shape[0] // rows_n
    own_tiles = waters // LANES
    halo_tiles = table.shape[1] // 2
    here_row = position()[0]
    for which in range(2):
        other = lax.rem(here_row + (rows_n - 1, 1)[which], rows_n)
        start = pl.multiple_of((here_row ^ other) * depth, 8)
        lines = halos[pl.ds(start, depth), :]
        for tile in range(halo_tiles):
            places = [(which * 9 + word) * halo_tiles + tile for word in range(9)]
            store_words(table, which * halo_tiles + tile, [lines[place : place + 1] for place in places])

    sources = [(tile, own_table, tile) for tile in range(first, own_tiles)]
    sources = sources + [(own_tiles + tile, table, tile) for tile in range(2 * halo_tiles)]

    def one_tile(tile, carry):
        span = pl.ds(pl.multiple_of(tile * LANES, LANES), LANES)
        lines = sites[:, span]
        own = []
        for word in range(9):
            line = jnp.broadcast_to(lines[word : word + 1] * SCALE + SHIFT * SCALE, (8, LANES))
            own.append((line, line - 32768.0))
        near = [jnp.zeros((8, LANES), F32) for _ in range(9)]
        far = [jnp.zeros((8, LANES), F32) for _ in range(9)]
        for pair in range(slots // 16):
            starts = [16 * pair + 8 * part for part in range(2)]
            found = [
                [own_words[word * slots + start : word * slots + start + 8, span] for start in starts]
                for word in range(5)
            ]
            index = [neighbours[start : start + 8, span] for start in starts]
            found = gather_words(sources, index, found)
            for part in range(2):
                places = []
                for word in range(9):
                    value = found[word // 2][part]
                    if word == 8:
                        places.append(value.astype(F32))
                    elif word % 2 == 0:
                        places.append((value & 65535).astype(F32))
                    else:
                        places.append((value >> 16).astype(F32))
                for source in range(3):
                    for target in range(3):
                        gap = []
                        for compo in range(3):
                            mine, other = 3 * source + compo, 3 * target + compo
                            gap.append(own[mine][other % 2] - places[other])
                        root = lax.rsqrt(
                            gap[0] * gap[0] + gap[1] * gap[1] + gap[2] * gap[2] + SOFTEN * SCALE * SCALE
                        )
                        weight = root * root * root
                        sums = near if target == 0 else far
                        for compo in range(3):
                            sums[3 * source + compo] = sums[3 * source + compo] + gap[compo] * weight
        for place in range(9):
            factor = CHARGE[place // 3] * UNIT * SCALE * SCALE
            total = factor * (far[place] - 2.0 * near[place])
            force[place : place + 1, span] = jnp.sum(total, axis=0, keepdims=True)
        return carry

    lax.fori_loop(0, own_tiles, one_tile, 0)


def pattern_flags(message, place):
    line = jnp.broadcast_to(message[pl.ds(place, 1), :], (8, LANES))
    return lambda block: pick(line, jnp.full((8, LANES), block, jnp.int32))[0:1].astype(BF16)


def field_kernel(ways, hist_rows, block_rows, summed, message, *refs):
    dens, out, masked, lines = refs[:ways], refs[ways + 1], refs[ways + 2], refs[ways + 3]
    rows, cols = dens[0].shape
    rows_b, cols_b = rows // BLOCK, cols // BLOCK
    depth = (message.shape[0] - summed) // ways
    here_row, here_col = position()
    result = jnp.zeros((16, rows), F32)
    lines[...] = jnp.zeros(lines.shape, F32)
    for step in range(ways):
        device = here_col ^ step
        flag = pattern_flags(message, hist_rows + 3 * rows_b + device)
        for col in range(cols_b):
            other = device * (cols_b // rows_b) + col // rows_b
            place = hist_rows + (here_row ^ other) * block_rows + line_of(col % rows_b, 0)
            start = summed + step * depth + 3 * col
            moment = message[start : start + 3, :]
            pot = UNIT * COUPLE * message[pl.ds(device * cols_b + col, 1), :]
            for comp in range(3):
                product = message[pl.ds(place + comp, 1), :]
                lines[comp : comp + 1, at(col)] = product + pot * moment[comp : comp + 1]
            lines[3:6, at(col)] = moment
            for row in range(rows_b):
                spot = slice(row * BLOCK, (row + 1) * BLOCK)
                target = slice(step * cols + col * BLOCK, step * cols + (col + 1) * BLOCK)
                masked[spot, target] = dens[step][spot, at(col)] * flag(rows_b * cols_b + row * cols_b + col)
        whole = lines[...]
        first = whole.astype(BF16).astype(F32)
        both = jnp.concatenate([first, whole - first], axis=0).astype(BF16)
        result = result + contract(both, masked[:, step * cols : (step + 1) * cols], ((1,), (1,)))
    total = result[0:8] + result[8:16]
    out[...] = jnp.zeros(out.shape, F32)
    for row in range(rows_b):
        pot = UNIT * COUPLE * message[pl.ds(here_row * rows_b + row, 1), :]
        start = line_of(row, 0)
        out[start : start + 3, :] = total[0:3, at(row)] + pot * total[3:6, at(row)]


def advance_kernel(
    rows_n,
    rows_b,
    fields,
    owner,
    sites,
    quat,
    pair,
    centres,
    velocity,
    angmom,
    centres_new,
    velocity_new,
    angmom_new,
    orient_new,
    force,
    table,
):
    waters = owner.shape[1]
    depth = fields.shape[0] // rows_n
    here_row = position()[0]
    table[...] = jnp.zeros(table.shape, F32)
    for step in range(rows_n):
        for row in range(rows_b):
            start = step * depth + line_of(row, 0)
            place = 4 * (step * rows_b + row)
            table[place : place + 3, :] = fields[start : start + 3, :]
    for tile in range(waters // LANES):
        for source in range(3):
            index = jnp.broadcast_to(owner[source : source + 1, at(tile)], (8, LANES))
            low, high = index & 127, index >> 7
            found = jnp.zeros((8, LANES), F32)
            for step in range(rows_n):
                base = (here_row ^ step) * (rows_b // 2)
                for two in range(rows_b // 2):
                    place = 8 * (step * (rows_b // 2) + two)
                    value = pick(table[place : place + 8, :], low)
                    found = jnp.where((high >> 1) == base + two, value, found)
            odd = (high[0:3] & 1) == 1
            found = jnp.where(odd, found[4:7], found[0:3])
            lines = slice(3 * source, 3 * source + 3)
            force[lines, at(tile)] = pair[lines, at(tile)] + CHARGE[source] * found

    def cross(left, right):
        return [
            left[1] * right[2] - left[2] * right[1],
            left[2] * right[0] - left[0] * right[2],
            left[0] * right[1] - left[1] * right[0],
        ]

    def split(array):
        return [array[compo : compo + 1, :] for compo in range(3)]

    total = force[0:3, :] + force[3:6, :] + force[6:9, :]
    torque = None
    centre = split(centres)
    for source in range(3):
        lever = [sites[3 * source + compo : 3 * source + compo + 1, :] - centre[compo] for compo in range(3)]
        push = [force[3 * source + compo : 3 * source + compo + 1, :] for compo in range(3)]
        turn = cross(lever, push)
        torque = turn if torque is None else [old + new for old, new in zip(torque, turn)]
    moving = velocity[...] + STEP_DT * total / WATER_MASS
    velocity_new[...] = moving
    centres_new[...] = centres[...] + STEP_DT * moving
    spin = [angmom[compo : compo + 1, :] + STEP_DT * torque[compo] for compo in range(3)]
    for compo in range(3):
        angmom_new[compo : compo + 1, :] = spin[compo]
    omega = [value * (1.0 / INERTIA) for value in spin]
    scalar = quat[0:1, :]
    vector = [quat[compo + 1 : compo + 2, :] for compo in range(3)]
    delta = [-(omega[0] * vector[0] + omega[1] * vector[1] + omega[2] * vector[2])]
    turned = cross(omega, vector)
    delta = delta + [scalar * omega[compo] + turned[compo] for compo in range(3)]
    moved = [old + 0.5 * STEP_DT * new for old, new in zip([scalar] + vector, delta)]
    length = jnp.sqrt(moved[0] * moved[0] + moved[1] * moved[1] + moved[2] * moved[2] + moved[3] * moved[3])
    for place in range(4):
        orient_new[place : place + 1, :] = moved[place] / length


def product_kernel(steps, hist_rows, block_rows, message, dens, *refs):
    count = len(steps)
    small, before = refs[:count], refs[count:-2]
    out, panel = refs[-2:]
    rows, cols = out.shape
    rows_b, cols_b = rows // BLOCK, cols // BLOCK
    here_row, here_col = position()
    spans = []
    for place, step in enumerate(steps):
        other = here_row ^ step
        base = (here_col ^ (other * rows // cols)) * cols + lax.rem(other * rows, cols)
        spans.append(pl.ds(pl.multiple_of(base, BLOCK), rows))
        flag = pattern_flags(message, hist_rows + step * block_rows + 3 * rows_b + here_col)
        for row in range(rows_b):
            block = small[place][row * BLOCK : (row + 1) * BLOCK, :]
            for col in range(cols_b):
                panel[place, row * BLOCK : (row + 1) * BLOCK, at(col)] = block * flag(row * cols_b + col)

    chunk = 2 * BLOCK
    for part in range(rows // chunk):
        lines = slice(part * chunk, (part + 1) * chunk)
        value = contract(dens[lines, spans[0]], panel[0], ((1,), (0,)))
        for place in range(1, count):
            value = value + contract(dens[lines, spans[place]], panel[place], ((1,), (0,)))
        if before:
            out[lines, :] = (value + before[0][lines, :]).astype(out.dtype)
            continue
        for half in range(2):
            row = 2 * part + half
            lines = slice(row * BLOCK, (row + 1) * BLOCK)
            own = UNIT * COUPLE * message[pl.ds(here_row * rows_b + row, 1), :]
            across = jnp.transpose(jnp.broadcast_to(own, (BLOCK, BLOCK)))
            for col in range(cols_b):
                pot = UNIT * COUPLE * message[pl.ds(here_col * cols_b + col, 1), :]
                sums = (across + pot) * dens[lines, at(col)].astype(F32)
                out[lines, at(col)] = (value[half * BLOCK : (half + 1) * BLOCK, at(col)] + sums).astype(out.dtype)


def tie_kernel(first, second, out):
    pass


VMEM = pl.BlockSpec(memory_space=pltpu.VMEM)
SMEM = pl.BlockSpec(memory_space=pltpu.SMEM)


def fetching(kernel, places, *refs):
    refs, semaphore = list(refs[:-1]), refs[-1]
    held = refs[len(refs) - len(places) :]
    copies = [pltpu.make_async_copy(refs[at_], held[n], semaphore.at[n]) for n, at_ in enumerate(places)]
    for copy in copies:
        copy.start()
    for copy in copies:
        copy.wait()
    for n, at_ in enumerate(places):
        refs[at_] = held[n]
    kernel(*refs[: len(refs) - len(places)])


def call(
    kernel, name, outs, operands, scalars=0, scratch=(), cost=(0, 0), whole=VMEM, fetch=(), unread=(), limit=48 << 20, **more
):
    in_specs = [SMEM] * scalars + [whole] * (len(operands) - scalars)
    scratch = list(scratch)
    for place in unread:
        in_specs[place] = pl.BlockSpec(memory_space=pl.ANY)
    if fetch:
        for place in fetch:
            memory = pltpu.SMEM if place < scalars else pltpu.VMEM
            scratch.append(memory(operands[place].shape, operands[place].dtype))
            in_specs[place] = pl.BlockSpec(memory_space=pltpu.HBM)
        scratch.append(pltpu.SemaphoreType.DMA((len(fetch),)))
        kernel = functools.partial(fetching, kernel, tuple(fetch))
    return pl.pallas_call(
        kernel,
        out_shape=[jax.ShapeDtypeStruct(shape, dtype) for shape, dtype in outs],
        in_specs=in_specs,
        out_specs=[whole] * len(outs),
        scratch_shapes=scratch,
        compiler_params=pltpu.CompilerParams(vmem_limit_bytes=limit),
        cost_estimate=pl.CostEstimate(flops=cost[0], bytes_accessed=cost[1], transcendentals=0),
        name=name,
        **more,
    )(*operands)


def doublings(count):
    step = 1
    while step < count:
        yield step
        step = 2 * step


def shards(
    density,
    margin,
    pattern_d,
    pattern_s,
    dipole,
    owner,
    centres,
    angles,
    velocity,
    angmom,
    halo_list,
    neighbours,
):
    rows, cols = density.shape
    rows_b, cols_b = pattern_d.shape
    rows_n = lax.axis_size("row")
    across = ("col", "sub")
    ways = lax.axis_size("col") * lax.axis_size("sub")
    hist_rows = rows * rows_n // LANES
    waters, listed, slots = centres.shape[1], halo_list.shape[1], neighbours.shape[0]
    block_rows = round8(3 * rows_b + ways)
    halo_rows = round8(18 * (listed // LANES))
    summed = hist_rows + rows_n * block_rows
    field_rows = round8(3 * rows_b)
    moment_rows = round8(3 * cols_b)

    def swap(value, axis, count, step):
        return lax.ppermute(value, axis, [(i, i ^ step) for i in range(count)])

    def tie(value, later):
        (value,) = call(
            tie_kernel,
            "tie",
            [(value.shape, value.dtype)],
            [value, later],
            whole=pl.BlockSpec(memory_space=pl.ANY),
            input_output_aliases={0: 0},
        )
        return value

    def merge(first, second, count, done=None):
        total = 2 * first.shape[0] - count
        operands = [first, second] + ([] if done is None else [done])
        (out,) = call(
            functools.partial(merge_kernel, count),
            "merge",
            [((total, LANES), F32)],
            operands,
            unread=range(2, len(operands)),
        )
        return out

    def send(value, axis, count):
        held = [value] + [None] * (count - 1)
        for step in doublings(count):
            held[step] = swap(value, axis, count, step)
        return held

    def relay(held, axis, count, later):
        for step in range(1, count):
            lowest = step & -step
            if step != lowest:
                if (step - lowest) & (step - lowest - 1) == 0:
                    held[step - lowest] = tie(held[step - lowest], later)
                held[step] = swap(held[step - lowest], axis, count, lowest)
        return held

    dens_all = send(density, across, ways)
    message, small, again, sites, quat = call(
        functools.partial(open_kernel, ways, hist_rows),
        "open",
        [
            ((hist_rows + block_rows + halo_rows, LANES), F32),
            ((rows, BLOCK), BF16),
            ((rows, BLOCK), BF16),
            ((16, waters), F32),
            ((4, waters), F32),
        ],
        [pattern_d, pattern_s, margin, dipole, owner, centres, angles, halo_list],
        scalars=2,
        cost=(10**6, 12 * 10**6),
        fetch=range(8),
        limit=60 << 20,
    )
    table, moments, held = call(
        prepare_kernel,
        "prepare",
        [
            ((5, waters // LANES, 8, LANES), jnp.int32),
            ((moment_rows, LANES), F32),
            (message.shape, F32),
        ],
        [sites, dipole, message],
    )
    first = -(-5 * (waters // LANES) // 8)
    (found,) = call(
        functools.partial(own_kernel, first),
        "own_gathers",
        [((5 * slots, waters), jnp.int32)],
        [table, neighbours],
        cost=(10**6, 6 * 10**6),
    )
    small_all = [small] + [None] * (rows_n - 1)
    small_all[1] = swap(small, "row", rows_n, 1)
    steps = list(doublings(rows_n))
    for step in steps[:-1]:
        message = merge(held, swap(message, "row", rows_n, step), hist_rows, moments)
        held = message
    later = tie(again, message)
    message, halos = call(
        functools.partial(turn_kernel, hist_rows, block_rows, halo_rows),
        "turn",
        [((summed + moment_rows, LANES), F32), ((rows_n * halo_rows, LANES), F32)],
        [message, swap(message, "row", rows_n, steps[-1]), moments, found],
        unread=(3,),
    )
    for step in steps[1:]:
        small_all[step] = swap(later, "row", rows_n, step)
    for step in doublings(ways):
        message = merge(message, swap(message, across, ways, step), summed)
        if step == 1:
            dens_all = relay(dens_all, across, ways, message)
    (pair,) = call(
        functools.partial(pair_kernel, rows_n, first),
        "pair_forces",
        [((9, waters), F32)],
        [sites, found, table, halos, neighbours],
        scratch=[pltpu.VMEM((5, 2 * listed // LANES, 8, LANES), jnp.int32)],
        cost=(10**6, 15 * 10**6),
    )
    field, masked = call(
        functools.partial(field_kernel, ways, hist_rows, block_rows, summed),
        "field",
        [((field_rows, LANES), F32), ((rows, ways * cols), BF16)],
        [message] + dens_all + [pair],
        unread=(1 + ways,),
        scratch=[pltpu.VMEM((8, cols), F32)],
        cost=(10**6, 5 * 10**6),
    )
    for step in doublings(rows_n):
        field = merge(field, swap(field, "row", rows_n, step), 0)
        if step == 1:
            small_all = relay(small_all, "row", rows_n, field)
    early = [0] + steps
    late = [step for step in range(rows_n) if step not in early]
    partial, kinds = [], [(early, F32 if late else BF16)] + ([(late, BF16)] if late else [])
    for these, kind in kinds:
        partial = call(
            functools.partial(product_kernel, these, hist_rows, block_rows),
            "product",
            [((rows, cols), kind)],
            [message, masked] + [small_all[step] for step in these] + list(partial),
            scratch=[pltpu.VMEM((len(these), rows, cols), BF16)],
            cost=(10**6, 10 * 10**6),
        )
    (qm_out,) = partial
    centres_new, velocity_new, angmom_new, orient_new = call(
        functools.partial(advance_kernel, rows_n, rows_b),
        "advance",
        [((3, waters), F32), ((3, waters), F32), ((3, waters), F32), ((4, waters), F32)],
        [field, owner, sites, quat, pair, centres, velocity, angmom],
        scratch=[pltpu.VMEM((16, waters), F32), pltpu.VMEM((4 * hist_rows, LANES), F32)],
        cost=(10**6, 6 * 10**6),
    )
    return (qm_out, centres_new, velocity_new, angmom_new, orient_new)


def solution(mesh):
    square = P(("groups", "row"), ("col", "sub"))
    spread = P(None, ("groups", "row", "col", "sub"))
    return jax.shard_map(
        shards,
        mesh=mesh,
        in_specs=(square,) * 4 + (P(None, ("groups", "col", "sub")),) + (spread,) * 7,
        out_specs=(square,) + (spread,) * 4,
        check_vma=False,
    )
```
